32 devices in a mesh: tm: 8 (over z, y), mod: 4 (over x, core).
Axes of the slice: x: 2, y: 2, z: 4, core: 2. Of those that a mesh axis runs over, the one named last changes fastest.
Arguments:
- filterbank: bfloat16 [1024, 128], P('tm'), may hold values from -6 to 6
- conv_weight: bfloat16 [384, 1280], replicated, may hold values from -0.3125 to 0.3125
- mlp_gain: float32 [1280], replicated, may hold values from 0.25 to 1.75
- up_weight: bfloat16 [1280, 5120], P('tm', 'mod'), may hold values from -0.15625 to 0.15625
- down_weight: bfloat16 [5120, 1280], P('mod', 'tm'), may hold values from -0.078125 to 0.078125
- post_gain: float32 [1280], replicated, may hold values from 0.25 to 1.75
- audio_weight: bfloat16 [1280, 1792], P(None, 'mod'), may hold values from -0.15625 to 0.15625
- patches: bfloat16 [2048, 1280], P('tm'), may hold values from -6 to 6
- vision_gain: float32 [1280], replicated, may hold values from 0.25 to 1.75
- vision_weight: bfloat16 [5120, 1792], P('tm', 'mod'), may hold values from -0.078125 to 0.078125
- retention: int32 [8, 64], P('tm'), may hold values from 0 to 63, each once within a row
- kept_count: int32 [8], P('tm'), may hold values from 1 to 64, 256 in all
Outputs:
- sequence: bfloat16 [8, 96, 1792], P('tm', None, 'mod')
The draws below stay inside these ranges and needn't reach their ends.
Inputs may be any that keep to these rules, and one draw needn't show every extreme that they name: `retention`: each row lists every merged token of its frame once. `kept_count`: the counts sum to 256.
All inputs are finite; a program needn't handle non-finite values. No bound on the sum of `kept_count` on one device may be relied on, other than what follows from the above.
Results may differ from the reference program's by a relative error of at most 0.01.
Values may be sent and summed in bfloat16 or wider, within the bound.
A program may use at most 64 MiB of HBM per device.

```python
import math
import jax
import jax.numpy as jnp
import numpy as np
from jax import lax

D_ENC = 1280
MEL = 128
D_HID = 5120
D_OUT = 1792
MRG_FRAME = 64
AUD_DEV = 128
AUD_TOK = 64
AUD_ALL = 1024
D_MRG = 5120
PATCH_ALL = 2048
KEEP_TOTAL = 256
SEQ_DEV = 96
N_TM = 8


def level_of(stream_key, dims, pieces, low, high):
    loudness, own = 1.0, jax.random.fold_in(stream_key, 6)
    for axis_at, shards_of in pieces:
        heights = jnp.exp(jax.random.uniform(jax.random.fold_in(own, axis_at), (shards_of,), jnp.float32, low / len(pieces), high / len(pieces)))
        loudness = loudness * jnp.repeat(heights, dims[axis_at] // shards_of).reshape([-1 if axis == axis_at else 1 for axis in range(len(dims))])
    return loudness


def length_profile(amount, total, most, skew):
    loads = [(1 << 20) // math.isqrt(rank ** skew) + 1 for rank in range(2, amount + 1)]
    spare, counts = total - most - (amount - 1), [1] * (amount - 1)
    while spare > 0:
        free = [i for i in range(amount - 1) if counts[i] < most]
        whole, left = sum([loads[i] for i in free]), spare
        for i in free:
            extra = min(most - counts[i], max(1, left * loads[i] // whole), spare)
            counts[i] = counts[i] + extra
            spare = spare - extra
    return np.array([most] + counts)


def ragged(rng, number_of, total, reach, lean):
    if number_of == 2:
        one = jax.random.randint(rng, (), max(1, total - reach), min(reach, total - 1) + 1)
        return jnp.stack([one, total - one])
    lengths = jnp.asarray(length_profile(number_of, total, reach, lean), jnp.int32)
    twos = (number_of - 1) // 2
    giver, sink = lengths[1:1 + 2 * twos:2], lengths[2:2 + 2 * twos:2]
    slack = jnp.minimum(giver - 1, reach - sink)
    passed = jax.random.randint(jax.random.fold_in(rng, 1), (twos,), 0, 1 << 20) % (slack + 1)
    lengths = lengths.at[1:1 + 2 * twos:2].set(giver - passed).at[2:2 + 2 * twos:2].set(sink + passed)
    return lengths[jax.random.permutation(jax.random.fold_in(rng, 2), number_of)]


def gaussian(rng, extent, scale, most, shards=(), held_as=jnp.bfloat16):
    drawn = jax.random.normal(rng, extent, jnp.float32) * scale
    if len(shards) > 0:
        drawn = level_of(rng, extent, shards, -0.22, 0.18) * drawn
    return jnp.clip(drawn, min=-most, max=most).astype(held_as)


def setup_inputs(seed: int = 0) -> dict:
    seeds = jax.random.split(jax.random.key(seed), 13)
    filterbank = gaussian(seeds[0], (AUD_ALL, MEL), 1.0, 6.0, ((0, 8),))
    conv_weight = gaussian(seeds[1], (3 * MEL, D_ENC), (3 * MEL) ** -0.5, 0.3125)
    mlp_gain = jnp.clip(1.0 + 0.15 * jax.random.normal(seeds[2], (D_ENC,), jnp.float32), 0.25, 1.75)
    up_weight = gaussian(seeds[3], (D_ENC, D_HID), D_ENC ** -0.5, 0.15625, ((0, 8), (1, 4)))
    down_weight = gaussian(seeds[4], (D_HID, D_ENC), D_HID ** -0.5, 0.078125, ((0, 4), (1, 8)))
    post_gain = jnp.clip(1.0 + 0.15 * jax.random.normal(seeds[5], (D_ENC,), jnp.float32), 0.25, 1.75)
    audio_weight = gaussian(seeds[6], (D_ENC, D_OUT), D_ENC ** -0.5, 0.15625, ((1, 4),))
    patches = gaussian(seeds[7], (PATCH_ALL, D_ENC), 1.0, 6.0, ((0, 8),))
    vision_gain = jnp.clip(1.0 + 0.15 * jax.random.normal(seeds[8], (D_ENC,), jnp.float32), 0.25, 1.75)
    vision_weight = gaussian(seeds[9], (D_MRG, D_OUT), D_MRG ** -0.5, 0.078125, ((0, 8), (1, 4)))
    retention = jax.vmap(lambda own: jax.random.permutation(own, MRG_FRAME))(jax.random.split(seeds[10], N_TM)).reshape((N_TM, MRG_FRAME)).astype(jnp.int32)
    kept_count = ragged(seeds[11], N_TM, KEEP_TOTAL, MRG_FRAME, 2).astype(jnp.int32)
    return {"filterbank": filterbank, "conv_weight": conv_weight, "mlp_gain": mlp_gain, "up_weight": up_weight, "down_weight": down_weight, "post_gain": post_gain, "audio_weight": audio_weight, "patches": patches, "vision_gain": vision_gain, "vision_weight": vision_weight, "retention": retention, "kept_count": kept_count}


def layer_norm(values, scale_gain):
    average = lax.optimization_barrier(jnp.mean(values, axis=-1, keepdims=True))
    centred = values - average
    variance = lax.optimization_barrier(jnp.mean(centred * centred, axis=-1, keepdims=True))
    return centred * lax.rsqrt(variance + 1e-05) * scale_gain

def rms_norm(values, scale_gain):
    square_mean = lax.optimization_barrier(jnp.mean(values * values, axis=-1, keepdims=True))
    return values * lax.rsqrt(square_mean + 1e-06) * scale_gain

def encode_span(stem_rows, mlp_gain, up_weight, down_weight, post_gain, audio_weight):
    residual = stem_rows.astype(jnp.float32)
    hidden = layer_norm(residual, mlp_gain).astype(jnp.bfloat16)
    activated = jax.nn.gelu(jnp.dot(hidden, up_weight, preferred_element_type=jnp.float32), approximate=False).astype(jnp.bfloat16)
    mixed = residual + jnp.dot(activated, down_weight, preferred_element_type=jnp.float32)
    pooled = mixed.reshape(-1, 2, mixed.shape[-1]).mean(axis=1)
    normed = layer_norm(pooled, post_gain).astype(jnp.bfloat16)
    return jnp.dot(normed, audio_weight, preferred_element_type=jnp.float32).astype(jnp.bfloat16)

def reference(filterbank, conv_weight, mlp_gain, up_weight, down_weight, post_gain, audio_weight, patches, vision_gain, vision_weight, retention, kept_count):
    padded = jnp.pad(filterbank, ((1, 1), (0, 0)))
    unfolded = jnp.concatenate([padded[:-2], padded[1:-1], padded[2:]], axis=1)
    stem = jax.nn.gelu(jnp.dot(unfolded, conv_weight, preferred_element_type=jnp.float32), approximate=False).astype(jnp.bfloat16)
    spans = stem.reshape(N_TM, AUD_DEV, D_ENC)
    audio_tokens = lax.map(lambda rows: encode_span(rows, mlp_gain, up_weight, down_weight, post_gain, audio_weight), spans)
    audio_tokens = audio_tokens.reshape(N_TM * AUD_TOK, D_OUT)
    patch_normed = rms_norm(patches.astype(jnp.float32), vision_gain).astype(jnp.bfloat16)
    merged = patch_normed.reshape(N_TM * MRG_FRAME, D_MRG)
    visual_tokens = jnp.dot(merged, vision_weight, preferred_element_type=jnp.float32).astype(jnp.bfloat16)
    placed = (kept_count + AUD_TOK).astype(jnp.int32)
    starts = (jnp.cumsum(placed) - placed).astype(jnp.int32)
    total_len = SEQ_DEV * N_TM
    slot_range = jnp.arange(MRG_FRAME, dtype=jnp.int32)
    visual_pos = jnp.where(slot_range[None, :] < kept_count[:, None], starts[:, None] + slot_range[None, :], total_len).astype(jnp.int32)
    span_base = (jnp.arange(N_TM, dtype=jnp.int32) * MRG_FRAME)[:, None]
    visual_rows = jnp.take(visual_tokens, (span_base + retention).reshape(-1).astype(jnp.int32), axis=0)
    audio_pos = ((starts + kept_count)[:, None] + jnp.arange(AUD_TOK, dtype=jnp.int32)[None, :]).astype(jnp.int32)
    flat = jnp.zeros((total_len, D_OUT), jnp.bfloat16)
    flat = flat.at[visual_pos.reshape(-1)].set(visual_rows, mode='drop')
    flat = flat.at[audio_pos.reshape(-1)].set(audio_tokens, mode='drop')
    return flat.reshape(SEQ_DEV, N_TM, D_OUT).transpose(1, 0, 2)
```

```python
import jax
import jax.numpy as jnp
from jax import lax
from jax.experimental import pallas as pl
from jax.experimental.pallas import tpu as pltpu
from jax.sharding import PartitionSpec as P

MRG_FRAME = 64
AUD_TOK = 64
SEQ_DEV = 96


def carried_in(value, axis, join, neutral):
    count, mine = (lax.axis_size(axis), lax.axis_index(axis))
    pieces = lax.all_gather(value, axis)
    running = jnp.full_like(value, 0) + jnp.asarray(neutral, value.dtype)

    def hop(position, running):
        longer = join(running, pieces[position])
        return jnp.where(position < mine, longer, running)

    return lax.fori_loop(0, count - 1, hop, running)


def padded(shard, sides, width):
    for axis, dim in sides:
        peers, length = (lax.axis_size(axis), shard.shape[dim])
        up = [(i, (i + 1) % peers) for i in range(peers - 1)]
        down = [(j, i) for i, j in up]
        last = lax.slice_in_dim(shard, length - width, length, axis=dim)
        first = lax.slice_in_dim(shard, 0, width, axis=dim)
        before = lax.ppermute(last, axis, up)
        after = lax.ppermute(first, axis, down)
        shard = jnp.concatenate([before, shard, after], axis=dim)
    return shard


def layer_norm(values, scale_gain):
    average = jnp.mean(values, axis=-1, keepdims=True)
    centred = values - average
    variance = jnp.mean(centred * centred, axis=-1, keepdims=True)
    return centred * lax.rsqrt(variance + 1e-05) * scale_gain


def rms_norm(values, scale_gain):
    square_mean = jnp.mean(values * values, axis=-1, keepdims=True)
    return values * lax.rsqrt(square_mean + 1e-06) * scale_gain


def pool_pairs(values):
    return values.reshape(-1, 2, values.shape[-1]).mean(axis=1)


def add_counts(earlier, later):
    return earlier + later


def on_device(
    filterbank,
    conv_weight,
    mlp_gain,
    up_weight,
    down_weight,
    post_gain,
    audio_weight,
    patches,
    vision_gain,
    vision_weight,
    retention,
    kept_count,
):
    placed = kept_count + AUD_TOK
    starts = carried_in(placed, "tm", add_counts, jnp.zeros((1,), jnp.int32))
    framed = padded(filterbank, (("tm", 0),), 1)
    unfolded = jnp.concatenate([framed[:-2], framed[1:-1], framed[2:]], axis=1)
    stem = jax.nn.gelu(
        jnp.dot(unfolded, conv_weight, preferred_element_type=jnp.float32), approximate=False
    ).astype(jnp.bfloat16)
    residual = stem.astype(jnp.float32)
    hidden = layer_norm(residual, mlp_gain).astype(jnp.bfloat16)
    up_share = lax.all_gather(up_weight, "tm", axis=0, tiled=True)
    pre_act = jnp.dot(hidden, up_share, preferred_element_type=jnp.float32)
    activated = jax.nn.gelu(pre_act, approximate=False).astype(jnp.bfloat16)
    down_share = lax.all_gather(down_weight, "tm", axis=1, tiled=True)
    partial_value = jnp.dot(activated, down_share, preferred_element_type=jnp.float32)
    pooled_share = lax.psum_scatter(
        pool_pairs(partial_value).astype(jnp.bfloat16), "mod", scatter_dimension=0, tiled=True
    ).astype(jnp.float32)
    share_rows = pooled_share.shape[0]
    own_rows = lax.dynamic_slice_in_dim(
        pool_pairs(residual), lax.axis_index("mod") * share_rows, share_rows, 0
    )
    share_normed = layer_norm(own_rows + pooled_share, post_gain).astype(jnp.bfloat16)
    normed = lax.all_gather(share_normed, "mod", axis=0, tiled=True)
    audio_tokens = jnp.dot(normed, audio_weight, preferred_element_type=jnp.float32).astype(
        jnp.bfloat16
    )
    patch_normed = rms_norm(patches.astype(jnp.float32), vision_gain).astype(jnp.bfloat16)
    merged = patch_normed.reshape(-1, 4 * patch_normed.shape[1])
    vision_share = lax.all_gather(vision_weight, "tm", axis=0, tiled=True)
    visual_tokens = jnp.dot(merged, vision_share, preferred_element_type=jnp.float32).astype(
        jnp.bfloat16
    )
    peer_count = lax.axis_size("tm")
    per_peer = (AUD_TOK + MRG_FRAME + peer_count - 1) // peer_count
    kept_here = kept_count[0]
    first_slot = starts[0]
    all_tokens = jnp.concatenate([visual_tokens, audio_tokens], axis=0)
    peer_ids = jnp.arange(peer_count, dtype=jnp.int32)[:, None]
    round_ids = jnp.arange(per_peer, dtype=jnp.int32)[None, :]
    local_index = round_ids * peer_count + (peer_ids - first_slot) % peer_count
    valid_rows = local_index < kept_here + AUD_TOK
    kept_index = jnp.take(retention[0], jnp.minimum(local_index, MRG_FRAME - 1), axis=0)
    source_index = jnp.where(
        local_index < kept_here, kept_index, MRG_FRAME + local_index - kept_here
    )
    source_index = jnp.where(valid_rows, source_index, 0).astype(jnp.int32)
    send_rows = jnp.take(all_tokens, source_index.reshape(-1), axis=0).reshape(
        peer_count, per_peer, all_tokens.shape[1]
    )
    send_slots = jnp.where(valid_rows, (first_slot + local_index) // peer_count, SEQ_DEV).astype(
        jnp.int32
    )
    recv_rows, recv_slots = (
        lax.all_to_all(send_rows, "tm", split_axis=0, concat_axis=0, tiled=True),
        lax.all_to_all(send_slots, "tm", split_axis=0, concat_axis=0, tiled=True),
    )
    sequence = jnp.zeros((SEQ_DEV, all_tokens.shape[1]), jnp.bfloat16)
    sequence = sequence.at[recv_slots.reshape(-1)].set(
        recv_rows.reshape(-1, all_tokens.shape[1]), mode="drop"
    )
    return sequence[None]


F32, BF16, I32 = jnp.float32, jnp.bfloat16, jnp.int32
MESH = pl.DeviceIdType.MESH
TM, MOD = 8, 4


def iota(shape, dim):
    return lax.broadcasted_iota(I32, shape, dim)


def onehot(mask, value=1.0):
    return jnp.where(mask, value, 0.0).astype(BF16)


def mm(a, b):
    return lax.dot_general(a, b, (((1,), (0,)), ((), ())), preferred_element_type=F32)


def mm_nt(a, b):
    return lax.dot_general(a, b, (((1,), (1,)), ((), ())), preferred_element_type=F32)


def mm_tn(a, b):
    return lax.dot_general(a, b, (((0,), (0,)), ((), ())), preferred_element_type=F32)


def gelu(x):
    return 0.5 * x * (1.0 + lax.erf(x * 0.7071067811865476))


FB, META, WGT, MRG, VIS, TOT, FWD, NRM, COR, XAX = 0, 7, 14, 21, 28, 35, 42, 45, 48, 49
N_SEM = 50


def fused_kernel(
    fb, conv, gain1, up, dn, gain2, aud_w, pat, gain_v, vis_w, ret, kept, out,
    fbp, meta_s, meta, w_s, w_r, m_s, x_r, v_s, v_r, stem, hid, pa, own,
    a_s, a_r, b_s, b_r, c_s, c_r, nrm, send_sem, recv_sem,
):
    me = lax.axis_index("tm")
    mo = lax.axis_index("mod")
    xx, cc = mo // 2, mo % 2
    tm_peers = [lax.rem(me + d, TM) for d in range(1, TM)]
    mod_peers = [lax.rem(mo + d, MOD) for d in range(1, MOD)]
    core_peer = xx * 2 + (1 - cc)
    x_peer = (1 - xx) * 2 + cc

    barrier = pltpu.get_barrier_semaphore()
    for peer in tm_peers:
        pl.semaphore_signal(barrier, inc=1, device_id={"tm": peer}, device_id_type=MESH)
    for peer in mod_peers:
        pl.semaphore_signal(barrier, inc=1, device_id={"mod": peer}, device_id_type=MESH)

    def copy(src, dst, slot, to):
        c = pltpu.make_async_remote_copy(
            src_ref=src, dst_ref=dst, send_sem=send_sem.at[slot], recv_sem=recv_sem.at[slot],
            device_id=to, device_id_type=MESH,
        )
        c.start()
        return c

    def to_tm(src_of, dst, base):
        return [copy(src_of(p), dst, base + d, {"tm": p}) for d, p in enumerate(tm_peers)]

    def arrive(copies):
        for c in copies:
            c.wait_recv()

    fbp[0:16] = jnp.zeros((16, 128), BF16)
    fbp[1040:1056] = jnp.zeros((16, 128), BF16)
    my_rows = pl.ds(pl.multiple_of(16 + me * 128, 16), 128)
    fbp[my_rows, :] = fb[...]
    hit = ret[...] == iota((64, 64), 0)
    inv = jnp.sum(jnp.where(hit, iota((64, 64), 1).astype(F32), 0.0), axis=1, keepdims=True)
    kept_f = kept[...].astype(F32)
    inv = jnp.where(inv < kept_f, inv, -4096.0)
    meta_s[0:64] = jnp.broadcast_to(inv, (64, 128))
    meta_s[64:72] = jnp.broadcast_to(kept_f, (8, 128))
    meta[me] = meta_s[...]

    pl.semaphore_wait(barrier, TM + MOD - 2)
    fb_copies = to_tm(lambda p: fb, fbp.at[my_rows], FB)
    meta_copies = to_tm(lambda p: meta_s, meta.at[me], META)

    row, col = iota((512, 128), 0), iota((512, 128), 1)
    for t in range(TM):
        w_s[t, 0:160] = up[:, 128 * t : 128 * t + 128]
        w_s[t, 160:320] = dn[:, 128 * t : 128 * t + 128]
    for g in range(2):
        lanes = slice(1024 + 128 * g, 1152 + 128 * g)
        rest = jnp.concatenate(
            [up[0:80, lanes], up[80:160, lanes], dn[0:80, lanes], dn[80:160, lanes]], axis=1
        )
        for a in range(4):
            pick = onehot((row // 128 == col // 32) & (row % 128 == 32 * a + col % 32))
            w_s[4 * g + a, 320:400] = mm(rest, pick).astype(BF16)
    w_copies = to_tm(lambda p: w_s.at[p], w_r.at[me], WGT)
    w_r[me] = w_s[me]

    pv = pat[pl.ds(pl.multiple_of(mo * 64, 64), 64), :].astype(F32)
    ms = jnp.sum(pv * pv, axis=1, keepdims=True) * (1.0 / 1280.0)
    pn = (pv * lax.rsqrt(ms + 1e-06) * gain_v[...]).astype(BF16)
    r64, c64 = iota((64, 64), 0), iota((64, 64), 1)
    pn = mm(onehot(c64 == 4 * (r64 % 16) + r64 // 16), pn).astype(BF16)
    for t in range(TM):
        q, h = t // 2, t % 2
        m_s[t] = pn[16 * q : 16 * q + 16, 640 * h : 640 * h + 640]
    m_copies = to_tm(lambda p: m_s.at[p], x_r.at[mo, me], MRG)
    x_r[mo, me] = m_s[me]

    arrive(fb_copies)

    def stem_step(s, carry):
        base = pl.multiple_of(s * 128, 128)
        rows = fbp[pl.ds(base, 160), :].astype(F32)
        taps = jnp.concatenate([rows[15:143], rows[16:144], rows[17:145]], axis=1).astype(BF16)
        st = gelu(mm(taps, conv[...])).astype(BF16)
        stem[pl.ds(base, 128), :] = st
        v = st.astype(F32)
        v = v - jnp.sum(v, axis=1, keepdims=True) * (1.0 / 1280.0)
        var = jnp.sum(v * v, axis=1, keepdims=True) * (1.0 / 1280.0)
        hid[pl.ds(base, 128), :] = (v * lax.rsqrt(var + 1e-05) * gain1[...]).astype(BF16)
        return carry

    lax.fori_loop(0, 4, stem_step, 0)
    arrive(m_copies)
    x_copies = [
        copy(x_r.at[mo], x_r.at[mo], FWD + d, {"mod": p}) for d, p in enumerate(mod_peers)
    ]
    lax.fori_loop(4, 8, stem_step, 0)

    arrive(meta_copies)
    ends, before, running = [], [], jnp.zeros((1, 128), F32)
    for s in range(TM):
        before.append(running)
        running = running + meta[s, 64:65, :]
        ends.append(running.astype(I32))

    arrive(w_copies)
    rem = jnp.concatenate([w_r[t, 320:400] for t in range(TM)], axis=0)
    ri, ci = iota((128, 512), 0), iota((128, 512), 1)
    rem = mm(rem, onehot((ci % 128 < 32) & (ri == 32 * (ci // 128) + ci % 128))).astype(BF16)

    def assemble(first, lane):
        main = jnp.concatenate([w_r[t, first : first + 160] for t in range(TM)], axis=0)
        parts = []
        for t in range(TM):
            parts.append(rem[80 * t : 80 * t + 80, lane : lane + 128])
            parts.append(rem[80 * t : 80 * t + 80, lane + 128 : lane + 256])
        return jnp.concatenate([main, jnp.concatenate(parts, axis=0)], axis=1)

    up_all = assemble(0, 0)
    dn_all = assemble(160, 256)

    def pool_rows(holder, r_s2, r_q, frames, span_ends):
        blocks = []
        for h in range(2):
            j = 8 * r_q + ((holder - span_ends[h]) & 7)
            blocks.append(onehot((r_s2 == h) & (frames // 2 == j), 0.5))
        return jnp.concatenate(blocks, axis=1)

    r128, c128 = iota((128, 128), 0), iota((128, 128), 1)
    for p in range(MOD):
        act = gelu(mm(hid[256 * p : 256 * p + 256], up_all)).astype(BF16)
        pool = pool_rows(r128 // 16, (r128 // 8) % 2, r128 % 8, c128, ends[2 * p : 2 * p + 2])
        pa[p % 2, p // 2] = mm(pool, act).astype(BF16)

    a_s[...] = mm_nt(pa[1 - cc].reshape(256, 256), dn_all).astype(BF16).reshape(2, 128, 1280)
    a_copy = copy(a_s, a_r, COR, {"mod": core_peer})
    own[...] = mm_nt(pa[cc].reshape(256, 256), dn_all).reshape(2, 128, 1280)
    a_copy.wait_recv()
    b_s[...] = (own[1 - xx] + a_r[1 - xx].astype(F32)).astype(BF16)
    b_copy = copy(b_s, b_r, XAX, {"mod": x_peer})

    arrive(x_copies)
    pos = jnp.concatenate(
        [meta[t, 16 * m : 16 * m + 16, :] + before[t] for m in range(MOD) for t in range(TM)], axis=0
    )
    pos = jnp.concatenate([pos, pos], axis=1).astype(I32)
    lane = iota((512, 256), 1)
    pick = onehot(pos == 8 * (lane % 32) + lane // 32)
    chosen = mm_tn(pick, x_r[...].reshape(512, 640)).astype(BF16)
    v_s[...] = mm_nt(chosen, vis_w[...]).astype(BF16).reshape(TM, 32, 448)

    b_copy.wait_recv()
    total = own[xx] + a_r[xx].astype(F32) + b_r[...].astype(F32)
    c_s[...] = total.astype(BF16).reshape(TM, 16, 1280)
    c_copies = to_tm(lambda p: c_s.at[p], c_r.at[me], TOT)
    v_copies = to_tm(lambda p: v_s.at[p], v_r.at[me], VIS)
    c_r[me] = c_s[me]
    v_r[me] = v_s[me]

    r16, c16 = iota((16, 128), 0), iota((16, 128), 1)
    mine = []
    for h in range(2):
        e = jnp.zeros((1, 128), I32)
        for p in range(MOD):
            e = jnp.where(mo == p, ends[2 * p + h], e)
        mine.append(e)
    pool = pool_rows(me, r16 // 8, r16 % 8, c16, mine)
    pooled = mm(pool, stem[pl.ds(pl.multiple_of(mo * 256, 256), 256), :])

    lane = iota((1, 128), 1)
    g = 8 * lane + me
    v_slot = lane
    a_slot = jnp.zeros((1, 128), I32)
    for s in range(TM):
        v_slot = v_slot + jnp.where(ends[s] <= g, 8, 0)
        j = 8 * (lane % 8) + ((me - ends[s]) & 7)
        a_slot = jnp.where((lane - 32) // 8 == s, ((ends[s] + j) >> 3) + 8 * s, a_slot)
    slot = jnp.where(lane < 32, v_slot, jnp.where(lane < 96, a_slot, -1))
    place = onehot(slot == iota((96, 128), 0))

    arrive(c_copies)
    for t in range(TM):
        pooled = pooled + c_r[t].astype(F32)
    v = pooled - jnp.sum(pooled, axis=1, keepdims=True) * (1.0 / 1280.0)
    var = jnp.sum(v * v, axis=1, keepdims=True) * (1.0 / 1280.0)
    nrm[mo] = (v * lax.rsqrt(var + 1e-05) * gain2[...]).astype(BF16)
    n_copies = [copy(nrm.at[mo], nrm.at[mo], NRM + d, {"mod": p}) for d, p in enumerate(mod_peers)]

    arrive(v_copies)
    visual = v_r[0].astype(F32)
    for t in range(1, TM):
        visual = visual + v_r[t].astype(F32)
    arrive(n_copies)
    audio = mm_nt(nrm[...].reshape(64, 1280), aud_w[...])
    tokens = jnp.concatenate(
        [visual.astype(BF16), audio.astype(BF16), jnp.zeros((32, 448), BF16)], axis=0
    )
    out[...] = mm(place, tokens).astype(BF16)

    for group in (fb_copies, meta_copies, w_copies, m_copies, x_copies, v_copies, c_copies, n_copies):
        for c in group:
            c.wait_send()
    a_copy.wait_send()
    b_copy.wait_send()


def on_device_fused(
    filterbank, conv_weight, mlp_gain, up_weight, down_weight, post_gain, audio_weight,
    patches, vision_gain, vision_weight, retention, kept_count,
):
    vm = pl.BlockSpec(memory_space=pltpu.VMEM)
    scratch = [
        pltpu.VMEM((1056, 128), BF16),
        pltpu.VMEM((72, 128), F32),
        pltpu.VMEM((TM, 72, 128), F32),
        pltpu.VMEM((TM, 400, 128), BF16),
        pltpu.VMEM((TM, 400, 128), BF16),
        pltpu.VMEM((TM, 16, 640), BF16),
        pltpu.VMEM((MOD, TM, 16, 640), BF16),
        pltpu.VMEM((TM, 32, 448), BF16),
        pltpu.VMEM((TM, 32, 448), BF16),
        pltpu.VMEM((1024, 1280), BF16),
        pltpu.VMEM((1024, 1280), BF16),
        pltpu.VMEM((2, 2, 128, 256), BF16),
        pltpu.VMEM((2, 128, 1280), F32),
        pltpu.VMEM((2, 128, 1280), BF16),
        pltpu.VMEM((2, 128, 1280), BF16),
        pltpu.VMEM((128, 1280), BF16),
        pltpu.VMEM((128, 1280), BF16),
        pltpu.VMEM((TM, 16, 1280), BF16),
        pltpu.VMEM((TM, 16, 1280), BF16),
        pltpu.VMEM((MOD, 16, 1280), BF16),
        pltpu.SemaphoreType.DMA((N_SEM,)),
        pltpu.SemaphoreType.DMA((N_SEM,)),
    ]
    sequence = pl.pallas_call(
        fused_kernel,
        out_shape=jax.ShapeDtypeStruct((SEQ_DEV, vision_weight.shape[1]), BF16),
        in_specs=[vm] * 12,
        out_specs=vm,
        scratch_shapes=scratch,
        compiler_params=pltpu.CompilerParams(
            collective_id=0, has_side_effects=True, vmem_limit_bytes=56 * 1024 * 1024
        ),
    )(
        filterbank, conv_weight, mlp_gain[None], up_weight, down_weight.T, post_gain[None],
        audio_weight.T, patches, vision_gain[None], vision_weight.T, retention, kept_count[None],
    )
    return sequence[None]


def solution(mesh):
    fused = mesh.shape["tm"] == TM and mesh.shape["mod"] == MOD
    return jax.shard_map(
        on_device_fused if fused else on_device,
        mesh=mesh,
        in_specs=(
            P("tm", None),
            P(),
            P(),
            P("tm", "mod"),
            P("mod", "tm"),
            P(),
            P(None, "mod"),
            P("tm", None),
            P(),
            P("tm", "mod"),
            P("tm", None),
            P("tm"),
        ),
        out_specs=P("tm", None, "mod"),
        check_vma=False,
    )
```

```python
import jax
import jax.numpy as jnp
from jax import lax
from jax.experimental import pallas as pl
from jax.experimental.pallas import tpu as pltpu
from jax.sharding import PartitionSpec as P

MRG_FRAME = 64
AUD_TOK = 64
SEQ_DEV = 96


def carried_in(value, axis, join, neutral):
    count, mine = (lax.axis_size(axis), lax.axis_index(axis))
    pieces = lax.all_gather(value, axis)
    running = jnp.full_like(value, 0) + jnp.asarray(neutral, value.dtype)

    def hop(position, running):
        longer = join(running, pieces[position])
        return jnp.where(position < mine, longer, running)

    return lax.fori_loop(0, count - 1, hop, running)


def padded(shard, sides, width):
    for axis, dim in sides:
        peers, length = (lax.axis_size(axis), shard.shape[dim])
        up = [(i, (i + 1) % peers) for i in range(peers - 1)]
        down = [(j, i) for i, j in up]
        last = lax.slice_in_dim(shard, length - width, length, axis=dim)
        first = lax.slice_in_dim(shard, 0, width, axis=dim)
        before = lax.ppermute(last, axis, up)
        after = lax.ppermute(first, axis, down)
        shard = jnp.concatenate([before, shard, after], axis=dim)
    return shard


def layer_norm(values, scale_gain):
    average = jnp.mean(values, axis=-1, keepdims=True)
    centred = values - average
    variance = jnp.mean(centred * centred, axis=-1, keepdims=True)
    return centred * lax.rsqrt(variance + 1e-05) * scale_gain


def rms_norm(values, scale_gain):
    square_mean = jnp.mean(values * values, axis=-1, keepdims=True)
    return values * lax.rsqrt(square_mean + 1e-06) * scale_gain


def pool_pairs(values):
    return values.reshape(-1, 2, values.shape[-1]).mean(axis=1)


def add_counts(earlier, later):
    return earlier + later


def on_device(
    filterbank,
    conv_weight,
    mlp_gain,
    up_weight,
    down_weight,
    post_gain,
    audio_weight,
    patches,
    vision_gain,
    vision_weight,
    retention,
    kept_count,
):
    placed = kept_count + AUD_TOK
    starts = carried_in(placed, "tm", add_counts, jnp.zeros((1,), jnp.int32))
    framed = padded(filterbank, (("tm", 0),), 1)
    unfolded = jnp.concatenate([framed[:-2], framed[1:-1], framed[2:]], axis=1)
    stem = jax.nn.gelu(
        jnp.dot(unfolded, conv_weight, preferred_element_type=jnp.float32), approximate=False
    ).astype(jnp.bfloat16)
    residual = stem.astype(jnp.float32)
    hidden = layer_norm(residual, mlp_gain).astype(jnp.bfloat16)
    up_share = lax.all_gather(up_weight, "tm", axis=0, tiled=True)
    pre_act = jnp.dot(hidden, up_share, preferred_element_type=jnp.float32)
    activated = jax.nn.gelu(pre_act, approximate=False).astype(jnp.bfloat16)
    down_share = lax.all_gather(down_weight, "tm", axis=1, tiled=True)
    partial_value = jnp.dot(activated, down_share, preferred_element_type=jnp.float32)
    pooled_share = lax.psum_scatter(
        pool_pairs(partial_value).astype(jnp.bfloat16), "mod", scatter_dimension=0, tiled=True
    ).astype(jnp.float32)
    share_rows = pooled_share.shape[0]
    own_rows = lax.dynamic_slice_in_dim(
        pool_pairs(residual), lax.axis_index("mod") * share_rows, share_rows, 0
    )
    share_normed = layer_norm(own_rows + pooled_share, post_gain).astype(jnp.bfloat16)
    normed = lax.all_gather(share_normed, "mod", axis=0, tiled=True)
    audio_tokens = jnp.dot(normed, audio_weight, preferred_element_type=jnp.float32).astype(
        jnp.bfloat16
    )
    patch_normed = rms_norm(patches.astype(jnp.float32), vision_gain).astype(jnp.bfloat16)
    merged = patch_normed.reshape(-1, 4 * patch_normed.shape[1])
    vision_share = lax.all_gather(vision_weight, "tm", axis=0, tiled=True)
    visual_tokens = jnp.dot(merged, vision_share, preferred_element_type=jnp.float32).astype(
        jnp.bfloat16
    )
    peer_count = lax.axis_size("tm")
    per_peer = (AUD_TOK + MRG_FRAME + peer_count - 1) // peer_count
    kept_here = kept_count[0]
    first_slot = starts[0]
    all_tokens = jnp.concatenate([visual_tokens, audio_tokens], axis=0)
    peer_ids = jnp.arange(peer_count, dtype=jnp.int32)[:, None]
    round_ids = jnp.arange(per_peer, dtype=jnp.int32)[None, :]
    local_index = round_ids * peer_count + (peer_ids - first_slot) % peer_count
    valid_rows = local_index < kept_here + AUD_TOK
    kept_index = jnp.take(retention[0], jnp.minimum(local_index, MRG_FRAME - 1), axis=0)
    source_index = jnp.where(
        local_index < kept_here, kept_index, MRG_FRAME + local_index - kept_here
    )
    source_index = jnp.where(valid_rows, source_index, 0).astype(jnp.int32)
    send_rows = jnp.take(all_tokens, source_index.reshape(-1), axis=0).reshape(
        peer_count, per_peer, all_tokens.shape[1]
    )
    send_slots = jnp.where(valid_rows, (first_slot + local_index) // peer_count, SEQ_DEV).astype(
        jnp.int32
    )
    recv_rows, recv_slots = (
        lax.all_to_all(send_rows, "tm", split_axis=0, concat_axis=0, tiled=True),
        lax.all_to_all(send_slots, "tm", split_axis=0, concat_axis=0, tiled=True),
    )
    sequence = jnp.zeros((SEQ_DEV, all_tokens.shape[1]), jnp.bfloat16)
    sequence = sequence.at[recv_slots.reshape(-1)].set(
        recv_rows.reshape(-1, all_tokens.shape[1]), mode="drop"
    )
    return sequence[None]


F32, BF16, I32 = jnp.float32, jnp.bfloat16, jnp.int32
MESH = pl.DeviceIdType.MESH
TM, MOD = 8, 4


def iota(shape, dim):
    return lax.broadcasted_iota(I32, shape, dim)


def onehot(mask, value=1.0):
    return jnp.where(mask, value, 0.0).astype(BF16)


def mm(a, b):
    return lax.dot_general(a, b, (((1,), (0,)), ((), ())), preferred_element_type=F32)


def mm_nt(a, b):
    return lax.dot_general(a, b, (((1,), (1,)), ((), ())), preferred_element_type=F32)


def mm_tn(a, b):
    return lax.dot_general(a, b, (((0,), (0,)), ((), ())), preferred_element_type=F32)


def gelu(x):
    return 0.5 * x * (1.0 + lax.erf(x * 0.7071067811865476))


FB, META, UPW, DNW, MRG, VIS, TOT, FWD, NRM, HID, COR, XAX = 0, 7, 14, 21, 28, 35, 42, 56, 59, 62, 66, 68
N_SEM = 70
HALF = 640


def fused_kernel(
    fb, conv, gain1, up, dn, gain2, aud_w, pat, gain_v, vis_w, ret, kept, out,
    fbp, meta, w_s, w_r, m_s, x_r, v_s, v_r, stem, hid, pa, own,
    a_s, a_r, b_s, b_r, c_s, c_r, nrm, send_sem, recv_sem,
):
    me = lax.axis_index("tm")
    mo = lax.axis_index("mod")
    xx, cc = mo // 2, mo % 2
    tm_peers = [lax.rem(me + d, TM) for d in range(1, TM)]
    mod_peers = [lax.rem(mo + d, MOD) for d in range(1, MOD)]
    core_peer = xx * 2 + (1 - cc)
    x_peer = (1 - xx) * 2 + cc

    barrier = pltpu.get_barrier_semaphore()
    for peer in tm_peers:
        pl.semaphore_signal(barrier, inc=1, device_id={"tm": peer}, device_id_type=MESH)
    for peer in mod_peers:
        pl.semaphore_signal(barrier, inc=1, device_id={"mod": peer}, device_id_type=MESH)

    sent = []

    def copy(src, dst, slot, to):
        c = pltpu.make_async_remote_copy(
            src_ref=src, dst_ref=dst, send_sem=send_sem.at[slot], recv_sem=recv_sem.at[slot],
            device_id=to, device_id_type=MESH,
        )
        c.start()
        sent.append(c)
        return c

    def to_tm(src_of, dst, base):
        return [copy(src_of(p), dst, base + d, {"tm": p}) for d, p in enumerate(tm_peers)]

    def arrive(copies):
        for c in copies:
            c.wait_recv()

    fbp[0:16] = jnp.zeros((16, 128), BF16)
    fbp[1040:1056] = jnp.zeros((16, 128), BF16)
    my_rows = pl.ds(pl.multiple_of(16 + me * 128, 16), 128)
    fbp[my_rows, :] = fb[...]
    hit = onehot(ret[...] == iota((128, 64), 0) % 64)
    inv = mm_nt(iota((8, 64), 1).astype(F32).astype(BF16), hit)
    kept_f = jnp.full((8, 128), kept[0], I32).astype(F32)
    inv = jnp.where(inv < kept_f, inv, -4096.0)
    meta[me] = jnp.where(iota((8, 128), 0) == 0, inv, kept_f)

    pl.semaphore_wait(barrier, TM + MOD - 2)
    fb_copies = to_tm(lambda p: fb, fbp.at[my_rows], FB)
    meta_copies = to_tm(lambda p: meta.at[me], meta.at[me], META)

    pv = pat[pl.ds(pl.multiple_of(mo * 64, 64), 64), :].astype(F32)
    ms = jnp.sum(pv * pv, axis=1, keepdims=True) * (1.0 / 1280.0)
    pn = (pv * lax.rsqrt(ms + 1e-06) * gain_v[...][None, :]).astype(BF16)
    r64, c64 = iota((64, 64), 0), iota((64, 64), 1)
    pn = mm(onehot(c64 == 4 * (r64 % 16) + r64 // 16), pn).astype(BF16)
    for t in range(TM):
        q, h = t // 2, t % 2
        m_s[t] = pn[16 * q : 16 * q + 16, HALF * h : HALF * h + HALF]
    m_copies = to_tm(lambda p: m_s.at[p], x_r.at[me, mo], MRG)
    x_r[me, mo] = m_s[me]

    row, col = iota((512, 128), 0), iota((512, 128), 1)
    for t in range(TM):
        w_s[t, 0:160] = up[:, 128 * t : 128 * t + 128]
        w_s[t, 240:400] = dn[:, 128 * t : 128 * t + 128]
    for g in range(2):
        lanes = slice(1024 + 128 * g, 1152 + 128 * g)
        rest = jnp.concatenate(
            [up[0:80, lanes], up[80:160, lanes], dn[0:80, lanes], dn[80:160, lanes]], axis=1
        )
        for a in range(4):
            pick = onehot((row // 128 == col // 32) & (row % 128 == 32 * a + col % 32))
            w_s[4 * g + a, 160:240] = mm(rest, pick).astype(BF16)
    up_rows, dn_rows = pl.ds(0, 240), pl.ds(240, 160)
    u_copies = to_tm(lambda p: w_s.at[p, up_rows], w_r.at[me, up_rows], UPW)
    d_copies = to_tm(lambda p: w_s.at[p, dn_rows], w_r.at[me, dn_rows], DNW)
    w_r[me] = w_s[me]

    arrive(fb_copies)

    def stem_step(first):
        base = pl.multiple_of(first * 128, 128)
        rows = fbp[pl.ds(base, 160), :].astype(F32)
        taps = jnp.concatenate([rows[15:143], rows[16:144], rows[17:145]], axis=1).astype(BF16)
        st = gelu(mm(taps, conv[...])).astype(BF16)
        stem[pl.ds(base, 128), :] = st
        v = st.astype(F32)
        v = v - jnp.sum(v, axis=1, keepdims=True) * (1.0 / 1280.0)
        var = jnp.sum(v * v, axis=1, keepdims=True) * (1.0 / 1280.0)
        hid[pl.ds(base, 128), :] = (v * lax.rsqrt(var + 1e-05) * gain1[...][None, :]).astype(BF16)

    h_copies = []
    for k in range(4):
        x_at = 1 - xx if k < 2 else xx
        span = 2 * (2 * x_at + cc) + k % 2
        stem_step(span)
        rows = pl.ds(pl.multiple_of(span * 128, 128), 128)
        h_copies.append(copy(hid.at[rows], hid.at[rows], HID + k, {"mod": core_peer}))
        if k == 1:
            arrive(m_copies)
            x_copies = [
                copy(x_r.at[:, mo], x_r.at[:, mo], FWD + d, {"mod": p})
                for d, p in enumerate(mod_peers)
            ]

    arrive(meta_copies)
    ends, before, running = [], [], jnp.zeros((1, 128), F32)
    for s in range(TM):
        before.append(running)
        running = running + meta[s, 1:2, :]
        ends.append(running.astype(I32))

    def ends_of(pair):
        picked = []
        for h in range(2):
            e = ends[h]
            for p in range(1, MOD):
                e = jnp.where(pair == p, ends[2 * p + h], e)
            picked.append(e)
        return picked

    def pool_rows(holder, r_s2, r_q, frames, span_ends):
        blocks = []
        for h in range(2):
            j = 8 * r_q + ((holder - span_ends[h]) & 7)
            blocks.append(onehot((r_s2 == h) & (frames // 2 == j), 0.5))
        return jnp.concatenate(blocks, axis=1)

    arrive(u_copies)
    rem = jnp.concatenate([w_r[t, 160:240] for t in range(TM)], axis=0)
    ri, ci = iota((128, 512), 0), iota((128, 512), 1)
    rem = mm(rem, onehot((ci % 128 < 32) & (ri == 32 * (ci // 128) + ci % 128))).astype(BF16)

    def assemble(first, lane):
        main = jnp.concatenate([w_r[t, first : first + 160] for t in range(TM)], axis=0)
        parts = []
        for t in range(TM):
            parts.append(rem[80 * t : 80 * t + 80, lane : lane + 128])
            parts.append(rem[80 * t : 80 * t + 80, lane + 128 : lane + 256])
        return jnp.concatenate([main, jnp.concatenate(parts, axis=0)], axis=1)

    up_all = assemble(0, 0)
    r128, c128 = iota((128, 128), 0), iota((128, 128), 1)
    order = [(1 - cc, 1 - xx), (1 - cc, xx), (cc, 1 - xx), (cc, xx)]
    for k in (2, 0, 3, 1):
        if k < 2:
            arrive(h_copies[2 * k : 2 * k + 2])
        pair = 2 * order[k][1] + order[k][0]
        rows = pl.ds(pl.multiple_of(pair * 256, 256), 256)
        act = gelu(mm(hid[rows, :], up_all)).astype(BF16)
        pool = pool_rows(r128 // 16, (r128 // 8) % 2, r128 % 8, c128, ends_of(pair))
        pa[k] = mm(pool, act).astype(BF16)

    arrive(x_copies)
    lane = iota((1, 128), 1)
    pos = jnp.concatenate(
        [
            jnp.where(lane < 64, meta[t, 0:1, :] + before[t], meta[t + 1, 0:1, :] + before[t + 1])
            for t in range(0, TM, 2)
        ],
        axis=1,
    ).astype(I32)
    r256 = iota((256, 512), 0)
    pick = onehot(pos == 8 * (r256 % 32) + r256 // 32)
    chosen = mm(pick, x_r[...].reshape(512, HALF)).astype(BF16)
    v_s[...] = mm_nt(chosen, vis_w[...]).astype(BF16).reshape(TM, 32, 448)
    v_copies = to_tm(lambda p: v_s.at[p], v_r.at[me], VIS)
    v_r[me] = v_s[me]

    arrive(d_copies)
    dn_all = assemble(240, 256)
    a_copies = []
    for k in range(2):
        a_s[k] = mm_nt(pa[k], dn_all).astype(BF16)
        a_copies.append(copy(a_s.at[k], a_r.at[k], COR + k, {"mod": core_peer}))
    own[0] = mm_nt(pa[2], dn_all)
    a_copies[0].wait_recv()
    b_copies = []
    for h in range(2):
        cols = slice(HALF * h, HALF * h + HALF)
        b_s[h] = (own[0, :, cols] + a_r[0, :, cols].astype(F32)).astype(BF16)
        b_copies.append(copy(b_s.at[h], b_r.at[h], XAX + h, {"mod": x_peer}))
    own[1] = mm_nt(pa[3], dn_all)
    a_copies[1].wait_recv()

    r16, c16 = iota((16, 128), 0), iota((16, 128), 1)
    pool = pool_rows(me, r16 // 8, r16 % 8, c16, ends_of(mo))
    pooled = mm(pool, stem[pl.ds(pl.multiple_of(mo * 256, 256), 256), :])
    g = 8 * lane + me
    v_slot = lane
    a_slot = jnp.zeros((1, 128), I32)
    for s in range(TM):
        v_slot = v_slot + jnp.where(ends[s] <= g, 8, 0)
        j = 8 * (lane % 8) + ((me - ends[s]) & 7)
        a_slot = jnp.where((lane - 32) // 8 == s, ((ends[s] + j) >> 3) + 8 * s, a_slot)
    slot = jnp.where(lane < 32, v_slot, jnp.where(lane < 96, a_slot, -1))
    place = onehot(slot == iota((96, 128), 0))

    c_copies = []
    for h in range(2):
        cols = slice(HALF * h, HALF * h + HALF)
        b_copies[h].wait_recv()
        total = own[1, :, cols] + a_r[1, :, cols].astype(F32) + b_r[h].astype(F32)
        c_s[h] = total.astype(BF16).reshape(TM, 16, HALF)
        c_copies.append(to_tm(lambda p: c_s.at[h, p], c_r.at[h, me], TOT + 7 * h))
        c_r[h, me] = c_s[h, me]

    arrive(v_copies)
    visual = v_r[0].astype(F32)
    for t in range(1, TM):
        visual = visual + v_r[t].astype(F32)

    halves = []
    for h in range(2):
        arrive(c_copies[h])
        part = pooled[:, HALF * h : HALF * h + HALF]
        for t in range(TM):
            part = part + c_r[h, t].astype(F32)
        halves.append(part)
    pooled = jnp.concatenate(halves, axis=1)
    v = pooled - jnp.sum(pooled, axis=1, keepdims=True) * (1.0 / 1280.0)
    var = jnp.sum(v * v, axis=1, keepdims=True) * (1.0 / 1280.0)
    nrm[mo] = (v * lax.rsqrt(var + 1e-05) * gain2[...][None, :]).astype(BF16)
    n_copies = [copy(nrm.at[mo], nrm.at[mo], NRM + d, {"mod": p}) for d, p in enumerate(mod_peers)]
    arrive(n_copies)
    audio = mm_nt(nrm[...].reshape(64, 1280), aud_w[...])
    tokens = jnp.concatenate(
        [visual.astype(BF16), audio.astype(BF16), jnp.zeros((32, 448), BF16)], axis=0
    )
    out[...] = mm(place, tokens).astype(BF16)

    for c in sent:
        c.wait_send()


def on_device_fused(
    filterbank, conv_weight, mlp_gain, up_weight, down_weight, post_gain, audio_weight,
    patches, vision_gain, vision_weight, retention, kept_count,
):
    vm = pl.BlockSpec(memory_space=pltpu.VMEM)
    scratch = [
        pltpu.VMEM((1056, 128), BF16),
        pltpu.VMEM((TM, 8, 128), F32),
        pltpu.VMEM((TM, 400, 128), BF16),
        pltpu.VMEM((TM, 400, 128), BF16),
        pltpu.VMEM((TM, 16, HALF), BF16),
        pltpu.VMEM((TM, MOD, 16, HALF), BF16),
        pltpu.VMEM((TM, 32, 448), BF16),
        pltpu.VMEM((TM, 32, 448), BF16),
        pltpu.VMEM((1024, 1280), BF16),
        pltpu.VMEM((1024, 1280), BF16),
        pltpu.VMEM((MOD, 128, 256), BF16),
        pltpu.VMEM((2, 128, 1280), F32),
        pltpu.VMEM((2, 128, 1280), BF16),
        pltpu.VMEM((2, 128, 1280), BF16),
        pltpu.VMEM((2, 128, HALF), BF16),
        pltpu.VMEM((2, 128, HALF), BF16),
        pltpu.VMEM((2, TM, 16, HALF), BF16),
        pltpu.VMEM((2, TM, 16, HALF), BF16),
        pltpu.VMEM((MOD, 16, 1280), BF16),
        pltpu.SemaphoreType.DMA((N_SEM,)),
        pltpu.SemaphoreType.DMA((N_SEM,)),
    ]
    sequence = pl.pallas_call(
        fused_kernel,
        out_shape=jax.ShapeDtypeStruct((SEQ_DEV, vision_weight.shape[1]), BF16),
        in_specs=[vm] * 11 + [pl.BlockSpec(memory_space=pltpu.SMEM)],
        out_specs=vm,
        scratch_shapes=scratch,
        compiler_params=pltpu.CompilerParams(
            collective_id=0, has_side_effects=True, vmem_limit_bytes=56 * 1024 * 1024
        ),
    )(
        filterbank, conv_weight, mlp_gain, up_weight, down_weight.T, post_gain,
        audio_weight.T, patches, vision_gain, vision_weight.T, retention, kept_count,
    )
    return sequence[None]


def solution(mesh):
    fused = mesh.shape["tm"] == TM and mesh.shape["mod"] == MOD
    return jax.shard_map(
        on_device_fused if fused else on_device,
        mesh=mesh,
        in_specs=(
            P("tm", None),
            P(),
            P(),
            P("tm", "mod"),
            P("mod", "tm"),
            P(),
            P(None, "mod"),
            P("tm", None),
            P(),
            P("tm", "mod"),
            P("tm", None),
            P("tm"),
        ),
        out_specs=P("tm", None, "mod"),
        check_vma=False,
    )
```

```python
import jax
import jax.numpy as jnp
from jax import lax
from jax.experimental import pallas as pl
from jax.experimental.pallas import tpu as pltpu
from jax.sharding import PartitionSpec as P

MRG_FRAME = 64
AUD_TOK = 64
SEQ_DEV = 96


def carried_in(value, axis, join, neutral):
    count, mine = (lax.axis_size(axis), lax.axis_index(axis))
    pieces = lax.all_gather(value, axis)
    running = jnp.full_like(value, 0) + jnp.asarray(neutral, value.dtype)

    def hop(position, running):
        longer = join(running, pieces[position])
        return jnp.where(position < mine, longer, running)

    return lax.fori_loop(0, count - 1, hop, running)


def padded(shard, sides, width):
    for axis, dim in sides:
        peers, length = (lax.axis_size(axis), shard.shape[dim])
        up = [(i, (i + 1) % peers) for i in range(peers - 1)]
        down = [(j, i) for i, j in up]
        last = lax.slice_in_dim(shard, length - width, length, axis=dim)
        first = lax.slice_in_dim(shard, 0, width, axis=dim)
        before = lax.ppermute(last, axis, up)
        after = lax.ppermute(first, axis, down)
        shard = jnp.concatenate([before, shard, after], axis=dim)
    return shard


def layer_norm(values, scale_gain):
    average = jnp.mean(values, axis=-1, keepdims=True)
    centred = values - average
    variance = jnp.mean(centred * centred, axis=-1, keepdims=True)
    return centred * lax.rsqrt(variance + 1e-05) * scale_gain


def rms_norm(values, scale_gain):
    square_mean = jnp.mean(values * values, axis=-1, keepdims=True)
    return values * lax.rsqrt(square_mean + 1e-06) * scale_gain


def pool_pairs(values):
    return values.reshape(-1, 2, values.shape[-1]).mean(axis=1)


def add_counts(earlier, later):
    return earlier + later


def on_device(
    filterbank,
    conv_weight,
    mlp_gain,
    up_weight,
    down_weight,
    post_gain,
    audio_weight,
    patches,
    vision_gain,
    vision_weight,
    retention,
    kept_count,
):
    placed = kept_count + AUD_TOK
    starts = carried_in(placed, "tm", add_counts, jnp.zeros((1,), jnp.int32))
    framed = padded(filterbank, (("tm", 0),), 1)
    unfolded = jnp.concatenate([framed[:-2], framed[1:-1], framed[2:]], axis=1)
    stem = jax.nn.gelu(
        jnp.dot(unfolded, conv_weight, preferred_element_type=jnp.float32), approximate=False
    ).astype(jnp.bfloat16)
    residual = stem.astype(jnp.float32)
    hidden = layer_norm(residual, mlp_gain).astype(jnp.bfloat16)
    up_share = lax.all_gather(up_weight, "tm", axis=0, tiled=True)
    pre_act = jnp.dot(hidden, up_share, preferred_element_type=jnp.float32)
    activated = jax.nn.gelu(pre_act, approximate=False).astype(jnp.bfloat16)
    down_share = lax.all_gather(down_weight, "tm", axis=1, tiled=True)
    partial_value = jnp.dot(activated, down_share, preferred_element_type=jnp.float32)
    pooled_share = lax.psum_scatter(
        pool_pairs(partial_value).astype(jnp.bfloat16), "mod", scatter_dimension=0, tiled=True
    ).astype(jnp.float32)
    share_rows = pooled_share.shape[0]
    own_rows = lax.dynamic_slice_in_dim(
        pool_pairs(residual), lax.axis_index("mod") * share_rows, share_rows, 0
    )
    share_normed = layer_norm(own_rows + pooled_share, post_gain).astype(jnp.bfloat16)
    normed = lax.all_gather(share_normed, "mod", axis=0, tiled=True)
    audio_tokens = jnp.dot(normed, audio_weight, preferred_element_type=jnp.float32).astype(
        jnp.bfloat16
    )
    patch_normed = rms_norm(patches.astype(jnp.float32), vision_gain).astype(jnp.bfloat16)
    merged = patch_normed.reshape(-1, 4 * patch_normed.shape[1])
    vision_share = lax.all_gather(vision_weight, "tm", axis=0, tiled=True)
    visual_tokens = jnp.dot(merged, vision_share, preferred_element_type=jnp.float32).astype(
        jnp.bfloat16
    )
    peer_count = lax.axis_size("tm")
    per_peer = (AUD_TOK + MRG_FRAME + peer_count - 1) // peer_count
    kept_here = kept_count[0]
    first_slot = starts[0]
    all_tokens = jnp.concatenate([visual_tokens, audio_tokens], axis=0)
    peer_ids = jnp.arange(peer_count, dtype=jnp.int32)[:, None]
    round_ids = jnp.arange(per_peer, dtype=jnp.int32)[None, :]
    local_index = round_ids * peer_count + (peer_ids - first_slot) % peer_count
    valid_rows = local_index < kept_here + AUD_TOK
    kept_index = jnp.take(retention[0], jnp.minimum(local_index, MRG_FRAME - 1), axis=0)
    source_index = jnp.where(
        local_index < kept_here, kept_index, MRG_FRAME + local_index - kept_here
    )
    source_index = jnp.where(valid_rows, source_index, 0).astype(jnp.int32)
    send_rows = jnp.take(all_tokens, source_index.reshape(-1), axis=0).reshape(
        peer_count, per_peer, all_tokens.shape[1]
    )
    send_slots = jnp.where(valid_rows, (first_slot + local_index) // peer_count, SEQ_DEV).astype(
        jnp.int32
    )
    recv_rows, recv_slots = (
        lax.all_to_all(send_rows, "tm", split_axis=0, concat_axis=0, tiled=True),
        lax.all_to_all(send_slots, "tm", split_axis=0, concat_axis=0, tiled=True),
    )
    sequence = jnp.zeros((SEQ_DEV, all_tokens.shape[1]), jnp.bfloat16)
    sequence = sequence.at[recv_slots.reshape(-1)].set(
        recv_rows.reshape(-1, all_tokens.shape[1]), mode="drop"
    )
    return sequence[None]


F32, BF16, I32 = jnp.float32, jnp.bfloat16, jnp.int32
MESH = pl.DeviceIdType.MESH
TM, MOD = 8, 4


def iota(shape, dim):
    return lax.broadcasted_iota(I32, shape, dim)


def onehot(mask, value=1.0):
    return jnp.where(mask, value, 0.0).astype(BF16)


def mm(a, b):
    return lax.dot_general(a, b, (((1,), (0,)), ((), ())), preferred_element_type=F32)


def mm_nt(a, b):
    return lax.dot_general(a, b, (((1,), (1,)), ((), ())), preferred_element_type=F32)


def mm_tn(a, b):
    return lax.dot_general(a, b, (((0,), (0,)), ((), ())), preferred_element_type=F32)


def gelu(x):
    return 0.5 * x * (1.0 + lax.erf(x * 0.7071067811865476))


FB, META, UPW, DNW, MRG, VIS, TOT, UPX, DNX, FWD, NRM, HID, COR = 0, 7, 14, 21, 28, 35, 42, 56, 64, 72, 75, 78, 80
N_SEM = 82
HALF = 640
FLIPS = (4, 6, 5, 7, 2, 3, 1)


def flipped(index, bits):
    for bit in (1, 2, 4):
        if bits % (2 * bit) >= bit:
            index = index + bit - 2 * bit * ((index // bit) % 2)
    return index


def fused_kernel(
    fb, conv_h, gain1, up, dn, gain2, aud_h, pat_h, gain_v, vis_h, ret, kept, out,
    conv, aud_w, pat, vis_w, fbp, meta, w_s, w_r, m_s, x_r, v_s, v_r, stem, hid, pa,
    a_s, a_r, c_s, c_r, nrm, load_sem, send_sem, recv_sem,
):
    me = lax.axis_index("tm")
    mo = lax.axis_index("mod")
    xx, cc = mo // 2, mo % 2
    tm_peers = [flipped(me, bits) for bits in FLIPS]
    mod_peers = [flipped(mo, bits) for bits in (2, 3, 1)]
    x_peer, core_peer = mod_peers[0], mod_peers[2]

    barrier = pltpu.get_barrier_semaphore()
    for peer in tm_peers:
        pl.semaphore_signal(barrier, inc=1, device_id={"tm": peer}, device_id_type=MESH)
    for peer in mod_peers:
        pl.semaphore_signal(barrier, inc=1, device_id={"mod": peer}, device_id_type=MESH)

    quarter = pl.ds(pl.multiple_of(mo * 64, 64), 64)
    loads = [
        pltpu.make_async_copy(src, dst, load_sem.at[i])
        for i, (src, dst) in enumerate(
            [(pat_h.at[quarter], pat), (conv_h, conv), (vis_h, vis_w), (aud_h, aud_w)]
        )
    ]
    for c in loads:
        c.start()

    sent = []

    def copy(src, dst, slot, to):
        c = pltpu.make_async_remote_copy(
            src_ref=src, dst_ref=dst, send_sem=send_sem.at[slot], recv_sem=recv_sem.at[slot],
            device_id=to, device_id_type=MESH,
        )
        c.start()
        sent.append(c)
        return c

    def to_tm(src_of, dst, base):
        return [copy(src_of(p), dst, base + d, {"tm": p}) for d, p in enumerate(tm_peers)]

    def arrive(copies):
        for c in copies:
            c.wait_recv()

    fbp[0:16] = jnp.zeros((16, 128), BF16)
    fbp[1040:1056] = jnp.zeros((16, 128), BF16)
    my_rows = pl.ds(pl.multiple_of(16 + me * 128, 16), 128)
    fbp[my_rows, :] = fb[...]
    hit = onehot(ret[...] == iota((128, 64), 0) % 64)
    inv = mm_nt(iota((8, 64), 1).astype(F32).astype(BF16), hit)
    kept_f = jnp.full((8, 128), kept[0], I32).astype(F32)
    inv = jnp.where(inv < kept_f, inv, -4096.0)
    meta[me] = jnp.where(iota((8, 128), 0) == 0, inv, kept_f)

    def needed(span):
        return (span + 1 >= 2 * mo) & (span <= 2 * mo + 2)

    fb_copies = [
        pltpu.make_async_remote_copy(
            src_ref=fb, dst_ref=fbp.at[my_rows], send_sem=send_sem.at[FB + d],
            recv_sem=recv_sem.at[FB + d], device_id={"tm": p}, device_id_type=MESH,
        )
        for d, p in enumerate(tm_peers)
    ]
    pl.semaphore_wait(barrier, TM + MOD - 2)

    @pl.when(needed(me))
    def _():
        for c in fb_copies:
            c.start()

    row, col = iota((512, 128), 0), iota((512, 128), 1)
    for t in range(TM):
        w_s[t, 0:160] = up[:, 128 * t : 128 * t + 128]
        w_s[t, 240:400] = dn[:, 128 * t : 128 * t + 128]
    for g in range(2):
        lanes = slice(1024 + 128 * g, 1152 + 128 * g)
        rest = jnp.concatenate(
            [up[0:80, lanes], up[80:160, lanes], dn[0:80, lanes], dn[80:160, lanes]], axis=1
        )
        for a in range(4):
            pick = onehot((row // 128 == col // 32) & (row % 128 == 32 * a + col % 32))
            w_s[4 * g + a, 160:240] = mm(rest, pick).astype(BF16)
    w_r[0, me] = w_s[me]
    up_rows, dn_rows = pl.ds(0, 240), pl.ds(240, 160)
    u_copies = to_tm(lambda p: w_s.at[p, up_rows], w_r.at[0, me, up_rows], UPW)

    def to_x(source, rows, slot):
        return copy(w_r.at[0, source, rows], w_r.at[1, source, rows], slot, {"mod": x_peer})

    ux_copies = [to_x(me, up_rows, UPX + 7)]
    dx_copies = [to_x(me, dn_rows, DNX + 7)]
    meta_copies = to_tm(lambda p: meta.at[me], meta.at[me], META)

    loads[0].wait()
    pv = pat[...].astype(F32)
    ms = jnp.sum(pv * pv, axis=1, keepdims=True) * (1.0 / 1280.0)
    pn = (pv * lax.rsqrt(ms + 1e-06) * gain_v[...][None, :]).astype(BF16)
    r64, c64 = iota((64, 64), 0), iota((64, 64), 1)
    pn = mm(onehot(c64 == 4 * (r64 % 16) + r64 // 16), pn).astype(BF16)
    for t in range(TM):
        q, h = t // 2, t % 2
        m_s[t] = pn[16 * q : 16 * q + 16, HALF * h : HALF * h + HALF]
    m_copies = to_tm(lambda p: m_s.at[p], x_r.at[me, mo], MRG)
    x_r[me, mo] = m_s[me]
    d_copies = to_tm(lambda p: w_s.at[p, dn_rows], w_r.at[0, me, dn_rows], DNW)

    loads[1].wait()
    for c, p in zip(fb_copies, tm_peers):
        pl.when(needed(p))(c.wait_recv)
    h_copies = []
    for k in range(2):
        base = pl.multiple_of((2 * mo + k) * 128, 128)
        rows = fbp[pl.ds(base, 160), :].astype(F32)
        taps = jnp.concatenate([rows[15:143], rows[16:144], rows[17:145]], axis=1).astype(BF16)
        st = gelu(mm(taps, conv[...])).astype(BF16)
        stem[128 * k : 128 * k + 128] = st
        v = st.astype(F32)
        v = v - jnp.sum(v, axis=1, keepdims=True) * (1.0 / 1280.0)
        var = jnp.sum(v * v, axis=1, keepdims=True) * (1.0 / 1280.0)
        part = pl.ds(128 * k, 128)
        hid[cc, part] = (v * lax.rsqrt(var + 1e-05) * gain1[...][None, :]).astype(BF16)
        h_copies.append(copy(hid.at[cc, part], hid.at[cc, part], HID + k, {"mod": core_peer}))

    for d in range(7):
        u_copies[d].wait_recv()
        ux_copies.append(to_x(tm_peers[d], up_rows, UPX + d))
    arrive(m_copies)
    x_copies = [
        copy(x_r.at[:, mo], x_r.at[:, mo], FWD, {"mod": x_peer}),
        copy(x_r.at[:, mo], x_r.at[:, mo], FWD + 1, {"mod": core_peer}),
    ]

    arrive(meta_copies)
    ends, before, running = [], [], jnp.zeros((1, 128), F32)
    for s in range(TM):
        before.append(running)
        running = running + meta[s, 1:2, :]
        ends.append(running.astype(I32))

    def ends_of(pair):
        picked = []
        for h in range(2):
            e = ends[h]
            for p in range(1, MOD):
                e = jnp.where(pair == p, ends[2 * p + h], e)
            picked.append(e)
        return picked

    def pool_rows(holder, r_s2, r_q, frames, span_ends):
        blocks = []
        for h in range(2):
            j = 8 * r_q + ((holder - span_ends[h]) & 7)
            blocks.append(onehot((r_s2 == h) & (frames // 2 == j), 0.5))
        return jnp.concatenate(blocks, axis=1)

    arrive(ux_copies)
    rem = jnp.concatenate(
        [jnp.concatenate([w_r[i, t, 160:240] for t in range(TM)], axis=0) for i in range(2)], axis=1
    )
    ri, ci = iota((256, 512), 0), iota((256, 512), 1)
    unit = ci % 128
    pick = onehot((unit < 64) & (ri == 128 * (unit // 32) + 32 * (ci // 128) + unit % 32))
    rem = mm(rem, pick).astype(BF16)

    def assemble(first, lane):
        parts = []
        for t in range(TM):
            parts.append(rem[80 * t : 80 * t + 80, lane : lane + 128])
            parts.append(rem[80 * t : 80 * t + 80, lane + 128 : lane + 256])
        mains = [
            jnp.concatenate([w_r[i, t, first : first + 160] for t in range(TM)], axis=0)
            for i in range(2)
        ]
        return jnp.concatenate(mains + [jnp.concatenate(parts, axis=0)], axis=1)

    up_all = assemble(0, 0)
    r128, c128 = iota((128, 128), 0), iota((128, 128), 1)

    def feed(k, core):
        act = gelu(mm(hid[core], up_all)).astype(BF16)
        pool = pool_rows(r128 // 16, (r128 // 8) % 2, r128 % 8, c128, ends_of(2 * xx + core))
        pa[k] = mm(pool, act).astype(BF16)

    def forward_down(steps):
        for d in steps:
            d_copies[d].wait_recv()
            dx_copies.append(to_x(tm_peers[d], dn_rows, DNX + d))

    feed(0, cc)
    x_copies[0].wait_recv()
    x_copies.append(copy(x_r.at[:, x_peer], x_r.at[:, x_peer], FWD + 2, {"mod": core_peer}))
    forward_down(range(0, 4))
    arrive(h_copies)
    feed(1, 1 - cc)
    forward_down(range(4, 7))

    arrive(x_copies[1:])
    loads[2].wait()
    lane = iota((1, 128), 1)
    pos = jnp.concatenate(
        [
            jnp.where(lane < 64, meta[t, 0:1, :] + before[t], meta[t + 1, 0:1, :] + before[t + 1])
            for t in range(0, TM, 2)
        ],
        axis=1,
    ).astype(I32)
    r256 = iota((256, 512), 0)
    pick = onehot(pos == 8 * (r256 % 32) + r256 // 32)
    chosen = mm(pick, x_r[...].reshape(512, HALF)).astype(BF16)
    v_s[...] = mm_nt(chosen, vis_w[...]).astype(BF16).reshape(TM, 32, 448)
    v_copies = to_tm(lambda p: v_s.at[p], v_r.at[me], VIS)
    v_r[me] = v_s[me]

    arrive(dx_copies)
    dn_all = assemble(240, 256)
    a_copies = []
    for h in range(2):
        a_s[h] = mm_nt(pa[1], dn_all[HALF * h : HALF * h + HALF]).astype(BF16)
        a_copies.append(copy(a_s.at[h], a_r.at[h], COR + h, {"mod": core_peer}))
    c_copies = []
    for h in range(2):
        own = mm_nt(pa[0], dn_all[HALF * h : HALF * h + HALF])
        a_copies[h].wait_recv()
        c_s[h] = (own + a_r[h].astype(F32)).astype(BF16).reshape(TM, 16, HALF)
        c_copies.append(to_tm(lambda p: c_s.at[h, p], c_r.at[h, me], TOT + 7 * h))
        c_r[h, me] = c_s[h, me]

    r16, c16 = iota((16, 128), 0), iota((16, 128), 1)
    pooled = mm(pool_rows(me, r16 // 8, r16 % 8, c16, ends_of(mo)), stem[...])
    g = 8 * lane + me
    v_slot = lane
    a_slot = jnp.zeros((1, 128), I32)
    for s in range(TM):
        v_slot = v_slot + jnp.where(ends[s] <= g, 8, 0)
        j = 8 * (lane % 8) + ((me - ends[s]) & 7)
        a_slot = jnp.where((lane - 32) // 8 == s, ((ends[s] + j) >> 3) + 8 * s, a_slot)
    slot = jnp.where(lane < 32, v_slot, jnp.where(lane < 96, a_slot, -1))
    place = onehot(slot == iota((96, 128), 0))

    arrive(v_copies)
    visual = v_r[0].astype(F32)
    for t in range(1, TM):
        visual = visual + v_r[t].astype(F32)

    halves = []
    for h in range(2):
        arrive(c_copies[h])
        part = pooled[:, HALF * h : HALF * h + HALF]
        for t in range(TM):
            part = part + c_r[h, t].astype(F32)
        halves.append(part)
    pooled = jnp.concatenate(halves, axis=1)
    v = pooled - jnp.sum(pooled, axis=1, keepdims=True) * (1.0 / 1280.0)
    var = jnp.sum(v * v, axis=1, keepdims=True) * (1.0 / 1280.0)
    nrm[mo] = (v * lax.rsqrt(var + 1e-05) * gain2[...][None, :]).astype(BF16)
    n_copies = [copy(nrm.at[mo], nrm.at[mo], NRM + d, {"mod": p}) for d, p in enumerate(mod_peers)]
    loads[3].wait()
    arrive(n_copies)
    audio = mm_nt(nrm[...].reshape(64, 1280), aud_w[...])
    tokens = jnp.concatenate(
        [visual.astype(BF16), audio.astype(BF16), jnp.zeros((32, 448), BF16)], axis=0
    )
    out[...] = mm(place, tokens).astype(BF16)

    for c in sent:
        c.wait_send()

    @pl.when(needed(me))
    def _():
        for c in fb_copies:
            c.wait_send()


def on_device_fused(
    filterbank, conv_weight, mlp_gain, up_weight, down_weight, post_gain, audio_weight,
    patches, vision_gain, vision_weight, retention, kept_count,
):
    vm = pl.BlockSpec(memory_space=pltpu.VMEM)
    far = pl.BlockSpec(memory_space=pl.ANY)
    n_out = vision_weight.shape[1]
    scratch = [
        pltpu.VMEM(conv_weight.shape, BF16),
        pltpu.VMEM((n_out, 1280), BF16),
        pltpu.VMEM((64, 1280), BF16),
        pltpu.VMEM((n_out, HALF), BF16),
        pltpu.VMEM((1056, 128), BF16),
        pltpu.VMEM((TM, 8, 128), F32),
        pltpu.VMEM((TM, 400, 128), BF16),
        pltpu.VMEM((2, TM, 400, 128), BF16),
        pltpu.VMEM((TM, 16, HALF), BF16),
        pltpu.VMEM((TM, MOD, 16, HALF), BF16),
        pltpu.VMEM((TM, 32, n_out), BF16),
        pltpu.VMEM((TM, 32, n_out), BF16),
        pltpu.VMEM((256, 1280), BF16),
        pltpu.VMEM((2, 256, 1280), BF16),
        pltpu.VMEM((2, 128, 384), BF16),
        pltpu.VMEM((2, 128, HALF), BF16),
        pltpu.VMEM((2, 128, HALF), BF16),
        pltpu.VMEM((2, TM, 16, HALF), BF16),
        pltpu.VMEM((2, TM, 16, HALF), BF16),
        pltpu.VMEM((MOD, 16, 1280), BF16),
        pltpu.SemaphoreType.DMA((4,)),
        pltpu.SemaphoreType.DMA((N_SEM,)),
        pltpu.SemaphoreType.DMA((N_SEM,)),
    ]
    sequence = pl.pallas_call(
        fused_kernel,
        out_shape=jax.ShapeDtypeStruct((SEQ_DEV, vision_weight.shape[1]), BF16),
        in_specs=[vm, far, vm, vm, vm, vm, far, far, vm, far, vm, pl.BlockSpec(memory_space=pltpu.SMEM)],
        out_specs=vm,
        scratch_shapes=scratch,
        compiler_params=pltpu.CompilerParams(
            collective_id=0, has_side_effects=True, vmem_limit_bytes=56 * 1024 * 1024
        ),
    )(
        filterbank, conv_weight, mlp_gain, up_weight, down_weight.T, post_gain,
        audio_weight.T, patches, vision_gain, vision_weight.T, retention, kept_count,
    )
    return sequence[None]


def solution(mesh):
    fused = mesh.shape["tm"] == TM and mesh.shape["mod"] == MOD
    return jax.shard_map(
        on_device_fused if fused else on_device,
        mesh=mesh,
        in_specs=(
            P("tm", None),
            P(),
            P(),
            P("tm", "mod"),
            P("mod", "tm"),
            P(),
            P(None, "mod"),
            P("tm", None),
            P(),
            P("tm", "mod"),
            P("tm", None),
            P("tm"),
        ),
        out_specs=P("tm", None, "mod"),
        check_vma=False,
    )
```

```python
import jax
import jax.numpy as jnp
from jax import lax
from jax.experimental import pallas as pl
from jax.experimental.pallas import tpu as pltpu
from jax.sharding import PartitionSpec as P

MRG_FRAME = 64
AUD_TOK = 64
SEQ_DEV = 96


def carried_in(value, axis, join, neutral):
    count, mine = (lax.axis_size(axis), lax.axis_index(axis))
    pieces = lax.all_gather(value, axis)
    running = jnp.full_like(value, 0) + jnp.asarray(neutral, value.dtype)

    def hop(position, running):
        longer = join(running, pieces[position])
        return jnp.where(position < mine, longer, running)

    return lax.fori_loop(0, count - 1, hop, running)


def padded(shard, sides, width):
    for axis, dim in sides:
        peers, length = (lax.axis_size(axis), shard.shape[dim])
        up = [(i, (i + 1) % peers) for i in range(peers - 1)]
        down = [(j, i) for i, j in up]
        last = lax.slice_in_dim(shard, length - width, length, axis=dim)
        first = lax.slice_in_dim(shard, 0, width, axis=dim)
        before = lax.ppermute(last, axis, up)
        after = lax.ppermute(first, axis, down)
        shard = jnp.concatenate([before, shard, after], axis=dim)
    return shard


def layer_norm(values, scale_gain):
    average = jnp.mean(values, axis=-1, keepdims=True)
    centred = values - average
    variance = jnp.mean(centred * centred, axis=-1, keepdims=True)
    return centred * lax.rsqrt(variance + 1e-05) * scale_gain


def rms_norm(values, scale_gain):
    square_mean = jnp.mean(values * values, axis=-1, keepdims=True)
    return values * lax.rsqrt(square_mean + 1e-06) * scale_gain


def pool_pairs(values):
    return values.reshape(-1, 2, values.shape[-1]).mean(axis=1)


def add_counts(earlier, later):
    return earlier + later


def on_device(
    filterbank,
    conv_weight,
    mlp_gain,
    up_weight,
    down_weight,
    post_gain,
    audio_weight,
    patches,
    vision_gain,
    vision_weight,
    retention,
    kept_count,
):
    placed = kept_count + AUD_TOK
    starts = carried_in(placed, "tm", add_counts, jnp.zeros((1,), jnp.int32))
    framed = padded(filterbank, (("tm", 0),), 1)
    unfolded = jnp.concatenate([framed[:-2], framed[1:-1], framed[2:]], axis=1)
    stem = jax.nn.gelu(
        jnp.dot(unfolded, conv_weight, preferred_element_type=jnp.float32), approximate=False
    ).astype(jnp.bfloat16)
    residual = stem.astype(jnp.float32)
    hidden = layer_norm(residual, mlp_gain).astype(jnp.bfloat16)
    up_share = lax.all_gather(up_weight, "tm", axis=0, tiled=True)
    pre_act = jnp.dot(hidden, up_share, preferred_element_type=jnp.float32)
    activated = jax.nn.gelu(pre_act, approximate=False).astype(jnp.bfloat16)
    down_share = lax.all_gather(down_weight, "tm", axis=1, tiled=True)
    partial_value = jnp.dot(activated, down_share, preferred_element_type=jnp.float32)
    pooled_share = lax.psum_scatter(
        pool_pairs(partial_value).astype(jnp.bfloat16), "mod", scatter_dimension=0, tiled=True
    ).astype(jnp.float32)
    share_rows = pooled_share.shape[0]
    own_rows = lax.dynamic_slice_in_dim(
        pool_pairs(residual), lax.axis_index("mod") * share_rows, share_rows, 0
    )
    share_normed = layer_norm(own_rows + pooled_share, post_gain).astype(jnp.bfloat16)
    normed = lax.all_gather(share_normed, "mod", axis=0, tiled=True)
    audio_tokens = jnp.dot(normed, audio_weight, preferred_element_type=jnp.float32).astype(
        jnp.bfloat16
    )
    patch_normed = rms_norm(patches.astype(jnp.float32), vision_gain).astype(jnp.bfloat16)
    merged = patch_normed.reshape(-1, 4 * patch_normed.shape[1])
    vision_share = lax.all_gather(vision_weight, "tm", axis=0, tiled=True)
    visual_tokens = jnp.dot(merged, vision_share, preferred_element_type=jnp.float32).astype(
        jnp.bfloat16
    )
    peer_count = lax.axis_size("tm")
    per_peer = (AUD_TOK + MRG_FRAME + peer_count - 1) // peer_count
    kept_here = kept_count[0]
    first_slot = starts[0]
    all_tokens = jnp.concatenate([visual_tokens, audio_tokens], axis=0)
    peer_ids = jnp.arange(peer_count, dtype=jnp.int32)[:, None]
    round_ids = jnp.arange(per_peer, dtype=jnp.int32)[None, :]
    local_index = round_ids * peer_count + (peer_ids - first_slot) % peer_count
    valid_rows = local_index < kept_here + AUD_TOK
    kept_index = jnp.take(retention[0], jnp.minimum(local_index, MRG_FRAME - 1), axis=0)
    source_index = jnp.where(
        local_index < kept_here, kept_index, MRG_FRAME + local_index - kept_here
    )
    source_index = jnp.where(valid_rows, source_index, 0).astype(jnp.int32)
    send_rows = jnp.take(all_tokens, source_index.reshape(-1), axis=0).reshape(
        peer_count, per_peer, all_tokens.shape[1]
    )
    send_slots = jnp.where(valid_rows, (first_slot + local_index) // peer_count, SEQ_DEV).astype(
        jnp.int32
    )
    recv_rows, recv_slots = (
        lax.all_to_all(send_rows, "tm", split_axis=0, concat_axis=0, tiled=True),
        lax.all_to_all(send_slots, "tm", split_axis=0, concat_axis=0, tiled=True),
    )
    sequence = jnp.zeros((SEQ_DEV, all_tokens.shape[1]), jnp.bfloat16)
    sequence = sequence.at[recv_slots.reshape(-1)].set(
        recv_rows.reshape(-1, all_tokens.shape[1]), mode="drop"
    )
    return sequence[None]


F32, BF16, I32 = jnp.float32, jnp.bfloat16, jnp.int32
MESH = pl.DeviceIdType.MESH
TM, MOD = 8, 4


def iota(shape, dim):
    return lax.broadcasted_iota(I32, shape, dim)


def onehot(mask, value=1.0):
    return jnp.where(mask, value, 0.0).astype(BF16)


def mm(a, b):
    return lax.dot_general(a, b, (((1,), (0,)), ((), ())), preferred_element_type=F32)


def mm_nt(a, b):
    return lax.dot_general(a, b, (((1,), (1,)), ((), ())), preferred_element_type=F32)


def mm_tn(a, b):
    return lax.dot_general(a, b, (((0,), (0,)), ((), ())), preferred_element_type=F32)


def gelu(x):
    return 0.5 * x * (1.0 + lax.erf(x * 0.7071067811865476))


FB, META, UPW, DNW, MRG, VIS, TOT, FWD, NRM, HID, COR, XAX = 0, 7, 14, 21, 28, 35, 42, 56, 59, 62, 66, 68
N_SEM = 70
HALF = 640
FLIPS = (4, 6, 5, 7, 2, 3, 1)


def flipped(index, bits):
    for bit in (1, 2, 4):
        if bits % (2 * bit) >= bit:
            index = index + bit - 2 * bit * ((index // bit) % 2)
    return index


def fused_kernel(
    fb, conv_h, gain1, up, dn, gain2, aud_h, pat_h, gain_v, vis_h, ret, kept, out,
    conv, aud_w, pat, vis_w, fbp, meta, w_s, w_r, m_s, x_r, v_s, v_r, stem, hid, pa, own,
    a_s, a_r, b_s, b_r, c_s, c_r, nrm, load_sem, send_sem, recv_sem,
):
    me = lax.axis_index("tm")
    mo = lax.axis_index("mod")
    xx, cc = mo // 2, mo % 2
    tm_peers = [flipped(me, bits) for bits in FLIPS]
    mod_peers = [flipped(mo, bits) for bits in (2, 3, 1)]
    x_peer, core_peer = mod_peers[0], mod_peers[2]

    barrier = pltpu.get_barrier_semaphore()
    for peer in tm_peers:
        pl.semaphore_signal(barrier, inc=1, device_id={"tm": peer}, device_id_type=MESH)
    for peer in mod_peers:
        pl.semaphore_signal(barrier, inc=1, device_id={"mod": peer}, device_id_type=MESH)

    quarter = pl.ds(pl.multiple_of(mo * 64, 64), 64)
    loads = [
        pltpu.make_async_copy(src, dst, load_sem.at[i])
        for i, (src, dst) in enumerate(
            [(pat_h.at[quarter], pat), (conv_h, conv), (vis_h, vis_w), (aud_h, aud_w)]
        )
    ]
    for c in loads:
        c.start()

    sent = []

    def copy(src, dst, slot, to):
        c = pltpu.make_async_remote_copy(
            src_ref=src, dst_ref=dst, send_sem=send_sem.at[slot], recv_sem=recv_sem.at[slot],
            device_id=to, device_id_type=MESH,
        )
        c.start()
        sent.append(c)
        return c

    def to_tm(src_of, dst, base):
        return [copy(src_of(p), dst, base + d, {"tm": p}) for d, p in enumerate(tm_peers)]

    def arrive(copies):
        for c in copies:
            c.wait_recv()

    fbp[0:16] = jnp.zeros((16, 128), BF16)
    fbp[1040:1056] = jnp.zeros((16, 128), BF16)
    my_rows = pl.ds(pl.multiple_of(16 + me * 128, 16), 128)
    fbp[my_rows, :] = fb[...]
    hit = onehot(ret[...] == iota((128, 64), 0) % 64)
    inv = mm_nt(iota((8, 64), 1).astype(F32).astype(BF16), hit)
    kept_f = jnp.full((8, 128), kept[0], I32).astype(F32)
    inv = jnp.where(inv < kept_f, inv, -4096.0)
    meta[me] = jnp.where(iota((8, 128), 0) == 0, inv, kept_f)

    row, col = iota((512, 128), 0), iota((512, 128), 1)
    for t in range(TM):
        w_s[t, 0:160] = up[:, 128 * t : 128 * t + 128]
        w_s[t, 240:400] = dn[:, 128 * t : 128 * t + 128]
    picks = [onehot((row // 128 == col // 32) & (row % 128 == 32 * a + col % 32)) for a in range(4)]
    for g in range(2):
        lanes = slice(1024 + 128 * g, 1152 + 128 * g)
        rest = jnp.concatenate(
            [up[0:80, lanes], up[80:160, lanes], dn[0:80, lanes], dn[80:160, lanes]], axis=1
        )
        for a in range(4):
            w_s[4 * g + a, 160:240] = mm(rest, picks[a]).astype(BF16)
    w_r[me] = w_s[me]

    def frames(d, p, source):
        first = 112 * (source % 2)
        edge = pl.ds(pl.multiple_of(first, 16), 16)
        there = pl.ds(pl.multiple_of(16 + source * 128 + first, 16), 16)
        whole = pl.ds(pl.multiple_of(16 + source * 128, 16), 128)
        return [
            pltpu.make_async_remote_copy(
                src_ref=src, dst_ref=dst, send_sem=send_sem.at[FB + d], recv_sem=recv_sem.at[FB + d],
                device_id={"tm": p}, device_id_type=MESH,
            )
            for src, dst in ((fb, fbp.at[whole]), (fb.at[edge], fbp.at[there]))
        ]

    def both_ways(source, act):
        here = (source // 2) % 2 == cc
        pl.when(here)(lambda: act(0))
        pl.when(jnp.logical_not(here))(lambda: act(1))

    fb_out = [frames(d, p, me) for d, p in enumerate(tm_peers)]
    fb_in = [frames(d, p, p) for d, p in enumerate(tm_peers)]
    pl.semaphore_wait(barrier, TM + MOD - 2)
    both_ways(me, lambda i: [c[i].start() for c in fb_out] and None)
    up_rows, dn_rows = pl.ds(0, 240), pl.ds(240, 160)
    u_copies = to_tm(lambda p: w_s.at[p, up_rows], w_r.at[me, up_rows], UPW)
    meta_copies = to_tm(lambda p: meta.at[me], meta.at[me], META)

    loads[0].wait()
    pv = pat[...].astype(F32)
    ms = jnp.sum(pv * pv, axis=1, keepdims=True) * (1.0 / 1280.0)
    pn = (pv * lax.rsqrt(ms + 1e-06) * gain_v[...][None, :]).astype(BF16)
    r64, c64 = iota((64, 64), 0), iota((64, 64), 1)
    pn = mm(onehot(c64 == 4 * (r64 % 16) + r64 // 16), pn).astype(BF16)
    for t in range(TM):
        q, h = t // 2, t % 2
        m_s[t] = pn[16 * q : 16 * q + 16, HALF * h : HALF * h + HALF]
    m_copies = to_tm(lambda p: m_s.at[p], x_r.at[me, mo], MRG)
    x_r[me, mo] = m_s[me]
    d_copies = to_tm(lambda p: w_s.at[p, dn_rows], w_r.at[me, dn_rows], DNW)

    loads[1].wait()
    for d, p in enumerate(tm_peers):
        both_ways(p, lambda i: fb_in[d][i].wait_recv())

    def stem_step(first):
        base = pl.multiple_of(first * 128, 128)
        rows = fbp[pl.ds(base, 160), :].astype(F32)
        taps = jnp.concatenate([rows[15:143], rows[16:144], rows[17:145]], axis=1).astype(BF16)
        st = gelu(mm(taps, conv[...])).astype(BF16)
        stem[pl.ds(base, 128), :] = st
        v = st.astype(F32)
        v = v - jnp.sum(v, axis=1, keepdims=True) * (1.0 / 1280.0)
        var = jnp.sum(v * v, axis=1, keepdims=True) * (1.0 / 1280.0)
        hid[pl.ds(base, 128), :] = (v * lax.rsqrt(var + 1e-05) * gain1[...][None, :]).astype(BF16)

    h_copies = []
    for k in range(4):
        x_at = 1 - xx if k < 2 else xx
        span = 2 * (2 * x_at + cc) + k % 2
        stem_step(span)
        rows = pl.ds(pl.multiple_of(span * 128, 128), 128)
        h_copies.append(copy(hid.at[rows], hid.at[rows], HID + k, {"mod": core_peer}))
        if k == 1:
            arrive(m_copies)
            x_copies = [
                copy(x_r.at[:, mo], x_r.at[:, mo], FWD + d, {"mod": p})
                for d, p in enumerate(mod_peers)
            ]

    arrive(meta_copies)
    ends, before, running = [], [], jnp.zeros((1, 128), F32)
    for s in range(TM):
        before.append(running)
        running = running + meta[s, 1:2, :]
        ends.append(running.astype(I32))

    def ends_of(pair):
        picked = []
        for h in range(2):
            e = ends[h]
            for p in range(1, MOD):
                e = jnp.where(pair == p, ends[2 * p + h], e)
            picked.append(e)
        return picked

    def pool_rows(holder, r_s2, r_q, frames, span_ends):
        blocks = []
        for h in range(2):
            j = 8 * r_q + ((holder - span_ends[h]) & 7)
            blocks.append(onehot((r_s2 == h) & (frames // 2 == j), 0.5))
        return jnp.concatenate(blocks, axis=1)

    arrive(u_copies)
    rem = jnp.concatenate([w_r[t, 160:240] for t in range(TM)], axis=0)
    ri, ci = iota((128, 512), 0), iota((128, 512), 1)
    rem = mm(rem, onehot((ci % 128 < 32) & (ri == 32 * (ci // 128) + ci % 128))).astype(BF16)

    def assemble(first, lane):
        main = jnp.concatenate([w_r[t, first : first + 160] for t in range(TM)], axis=0)
        parts = []
        for t in range(TM):
            parts.append(rem[80 * t : 80 * t + 80, lane : lane + 128])
            parts.append(rem[80 * t : 80 * t + 80, lane + 128 : lane + 256])
        return jnp.concatenate([main, jnp.concatenate(parts, axis=0)], axis=1)

    up_all = assemble(0, 0)
    r128, c128 = iota((128, 128), 0), iota((128, 128), 1)
    order = [(1 - cc, 1 - xx), (1 - cc, xx), (cc, 1 - xx), (cc, xx)]
    for k in (2, 0, 3, 1):
        if k < 2:
            arrive(h_copies[2 * k : 2 * k + 2])
        pair = 2 * order[k][1] + order[k][0]
        rows = pl.ds(pl.multiple_of(pair * 256, 256), 256)
        act = gelu(mm(hid[rows, :], up_all)).astype(BF16)
        pool = pool_rows(r128 // 16, (r128 // 8) % 2, r128 % 8, c128, ends_of(pair))
        pa[k] = mm(pool, act).astype(BF16)

    arrive(x_copies)
    lane = iota((1, 128), 1)
    pos = jnp.concatenate(
        [
            jnp.where(lane < 64, meta[t, 0:1, :] + before[t], meta[t + 1, 0:1, :] + before[t + 1])
            for t in range(0, TM, 2)
        ],
        axis=1,
    ).astype(I32)
    r256 = iota((256, 512), 0)
    pick = onehot(pos == 8 * (r256 % 32) + r256 // 32)
    chosen = mm(pick, x_r[...].reshape(512, HALF)).astype(BF16)
    loads[2].wait()
    v_s[...] = mm_nt(chosen, vis_w[...]).astype(BF16).reshape(TM, 32, 448)
    v_copies = to_tm(lambda p: v_s.at[p], v_r.at[me], VIS)
    v_r[me] = v_s[me]

    arrive(d_copies)
    dn_all = assemble(240, 256)
    a_copies, b_copies, c_copies = [], [], []
    for h in range(2):
        product = mm_nt(pa[...].reshape(512, 256), dn_all[HALF * h : HALF * h + HALF])
        a_s[h] = product[0:256].astype(BF16)
        a_copies.append(copy(a_s.at[h], a_r.at[h], COR + h, {"mod": core_peer}))
        own[h] = product[256:512]
    for h in range(2):
        a_copies[h].wait_recv()
        b_s[h] = (own[h, 0:128] + a_r[h, 0:128].astype(F32)).astype(BF16)
        b_copies.append(copy(b_s.at[h], b_r.at[h], XAX + h, {"mod": x_peer}))

    r16, c16 = iota((16, 128), 0), iota((16, 128), 1)
    pool = pool_rows(me, r16 // 8, r16 % 8, c16, ends_of(mo))
    pooled = mm(pool, stem[pl.ds(pl.multiple_of(mo * 256, 256), 256), :])
    g = 8 * lane + me
    v_slot = lane
    a_slot = jnp.zeros((1, 128), I32)
    for s in range(TM):
        v_slot = v_slot + jnp.where(ends[s] <= g, 8, 0)
        j = 8 * (lane % 8) + ((me - ends[s]) & 7)
        a_slot = jnp.where((lane - 32) // 8 == s, ((ends[s] + j) >> 3) + 8 * s, a_slot)
    slot = jnp.where(lane < 32, v_slot, jnp.where(lane < 96, a_slot, -1))
    place = onehot(slot == iota((96, 128), 0))

    for h in range(2):
        total = own[h, 128:256] + a_r[h, 128:256].astype(F32)
        b_copies[h].wait_recv()
        total = total + b_r[h].astype(F32)
        c_s[h] = total.astype(BF16).reshape(TM, 16, HALF)
        c_copies.append(to_tm(lambda p: c_s.at[h, p], c_r.at[h, me], TOT + 7 * h))
        c_r[h, me] = c_s[h, me]

    arrive(v_copies)
    visual = v_r[0].astype(F32)
    for t in range(1, TM):
        visual = visual + v_r[t].astype(F32)

    halves = []
    for h in range(2):
        arrive(c_copies[h])
        part = pooled[:, HALF * h : HALF * h + HALF]
        for t in range(TM):
            part = part + c_r[h, t].astype(F32)
        halves.append(part)
    pooled = jnp.concatenate(halves, axis=1)
    v = pooled - jnp.sum(pooled, axis=1, keepdims=True) * (1.0 / 1280.0)
    var = jnp.sum(v * v, axis=1, keepdims=True) * (1.0 / 1280.0)
    nrm[mo] = (v * lax.rsqrt(var + 1e-05) * gain2[...][None, :]).astype(BF16)
    n_copies = [copy(nrm.at[mo], nrm.at[mo], NRM + d, {"mod": p}) for d, p in enumerate(mod_peers)]
    loads[3].wait()
    arrive(n_copies)
    audio = mm_nt(nrm[...].reshape(64, 1280), aud_w[...])
    tokens = jnp.concatenate(
        [visual.astype(BF16), audio.astype(BF16), jnp.zeros((32, 448), BF16)], axis=0
    )
    out[...] = mm(place, tokens).astype(BF16)

    for c in sent:
        c.wait_send()
    both_ways(me, lambda i: [c[i].wait_send() for c in fb_out] and None)


def on_device_fused(
    filterbank, conv_weight, mlp_gain, up_weight, down_weight, post_gain, audio_weight,
    patches, vision_gain, vision_weight, retention, kept_count,
):
    vm = pl.BlockSpec(memory_space=pltpu.VMEM)
    far = pl.BlockSpec(memory_space=pl.ANY)
    n_out = vision_weight.shape[1]
    scratch = [
        pltpu.VMEM(conv_weight.shape, BF16),
        pltpu.VMEM((n_out, 1280), BF16),
        pltpu.VMEM((64, 1280), BF16),
        pltpu.VMEM((n_out, HALF), BF16),
        pltpu.VMEM((1056, 128), BF16),
        pltpu.VMEM((TM, 8, 128), F32),
        pltpu.VMEM((TM, 400, 128), BF16),
        pltpu.VMEM((TM, 400, 128), BF16),
        pltpu.VMEM((TM, 16, HALF), BF16),
        pltpu.VMEM((TM, MOD, 16, HALF), BF16),
        pltpu.VMEM((TM, 32, n_out), BF16),
        pltpu.VMEM((TM, 32, n_out), BF16),
        pltpu.VMEM((1024, 1280), BF16),
        pltpu.VMEM((1024, 1280), BF16),
        pltpu.VMEM((MOD, 128, 256), BF16),
        pltpu.VMEM((2, 256, HALF), F32),
        pltpu.VMEM((2, 256, HALF), BF16),
        pltpu.VMEM((2, 256, HALF), BF16),
        pltpu.VMEM((2, 128, HALF), BF16),
        pltpu.VMEM((2, 128, HALF), BF16),
        pltpu.VMEM((2, TM, 16, HALF), BF16),
        pltpu.VMEM((2, TM, 16, HALF), BF16),
        pltpu.VMEM((MOD, 16, 1280), BF16),
        pltpu.SemaphoreType.DMA((4,)),
        pltpu.SemaphoreType.DMA((N_SEM,)),
        pltpu.SemaphoreType.DMA((N_SEM,)),
    ]
    sequence = pl.pallas_call(
        fused_kernel,
        out_shape=jax.ShapeDtypeStruct((SEQ_DEV, vision_weight.shape[1]), BF16),
        in_specs=[vm, far, vm, vm, vm, vm, far, far, vm, far, vm, pl.BlockSpec(memory_space=pltpu.SMEM)],
        out_specs=vm,
        scratch_shapes=scratch,
        compiler_params=pltpu.CompilerParams(
            collective_id=0, has_side_effects=True, vmem_limit_bytes=56 * 1024 * 1024
        ),
    )(
        filterbank, conv_weight, mlp_gain, up_weight, down_weight.T, post_gain,
        audio_weight.T, patches, vision_gain, vision_weight.T, retention, kept_count,
    )
    return sequence[None]


def solution(mesh):
    fused = mesh.shape["tm"] == TM and mesh.shape["mod"] == MOD
    return jax.shard_map(
        on_device_fused if fused else on_device,
        mesh=mesh,
        in_specs=(
            P("tm", None),
            P(),
            P(),
            P("tm", "mod"),
            P("mod", "tm"),
            P(),
            P(None, "mod"),
            P("tm", None),
            P(),
            P("tm", "mod"),
            P("tm", None),
            P("tm"),
        ),
        out_specs=P("tm", None, "mod"),
        check_vma=False,
    )
```

```python
import jax
import jax.numpy as jnp
from jax import lax
from jax.experimental import pallas as pl
from jax.experimental.pallas import tpu as pltpu
from jax.sharding import PartitionSpec as P

MRG_FRAME = 64
AUD_TOK = 64
SEQ_DEV = 96


def carried_in(value, axis, join, neutral):
    count, mine = (lax.axis_size(axis), lax.axis_index(axis))
    pieces = lax.all_gather(value, axis)
    running = jnp.full_like(value, 0) + jnp.asarray(neutral, value.dtype)

    def hop(position, running):
        longer = join(running, pieces[position])
        return jnp.where(position < mine, longer, running)

    return lax.fori_loop(0, count - 1, hop, running)


def padded(shard, sides, width):
    for axis, dim in sides:
        peers, length = (lax.axis_size(axis), shard.shape[dim])
        up = [(i, (i + 1) % peers) for i in range(peers - 1)]
        down = [(j, i) for i, j in up]
        last = lax.slice_in_dim(shard, length - width, length, axis=dim)
        first = lax.slice_in_dim(shard, 0, width, axis=dim)
        before = lax.ppermute(last, axis, up)
        after = lax.ppermute(first, axis, down)
        shard = jnp.concatenate([before, shard, after], axis=dim)
    return shard


def layer_norm(values, scale_gain):
    average = jnp.mean(values, axis=-1, keepdims=True)
    centred = values - average
    variance = jnp.mean(centred * centred, axis=-1, keepdims=True)
    return centred * lax.rsqrt(variance + 1e-05) * scale_gain


def rms_norm(values, scale_gain):
    square_mean = jnp.mean(values * values, axis=-1, keepdims=True)
    return values * lax.rsqrt(square_mean + 1e-06) * scale_gain


def pool_pairs(values):
    return values.reshape(-1, 2, values.shape[-1]).mean(axis=1)


def add_counts(earlier, later):
    return earlier + later


def on_device(
    filterbank,
    conv_weight,
    mlp_gain,
    up_weight,
    down_weight,
    post_gain,
    audio_weight,
    patches,
    vision_gain,
    vision_weight,
    retention,
    kept_count,
):
    placed = kept_count + AUD_TOK
    starts = carried_in(placed, "tm", add_counts, jnp.zeros((1,), jnp.int32))
    framed = padded(filterbank, (("tm", 0),), 1)
    unfolded = jnp.concatenate([framed[:-2], framed[1:-1], framed[2:]], axis=1)
    stem = jax.nn.gelu(
        jnp.dot(unfolded, conv_weight, preferred_element_type=jnp.float32), approximate=False
    ).astype(jnp.bfloat16)
    residual = stem.astype(jnp.float32)
    hidden = layer_norm(residual, mlp_gain).astype(jnp.bfloat16)
    up_share = lax.all_gather(up_weight, "tm", axis=0, tiled=True)
    pre_act = jnp.dot(hidden, up_share, preferred_element_type=jnp.float32)
    activated = jax.nn.gelu(pre_act, approximate=False).astype(jnp.bfloat16)
    down_share = lax.all_gather(down_weight, "tm", axis=1, tiled=True)
    partial_value = jnp.dot(activated, down_share, preferred_element_type=jnp.float32)
    pooled_share = lax.psum_scatter(
        pool_pairs(partial_value).astype(jnp.bfloat16), "mod", scatter_dimension=0, tiled=True
    ).astype(jnp.float32)
    share_rows = pooled_share.shape[0]
    own_rows = lax.dynamic_slice_in_dim(
        pool_pairs(residual), lax.axis_index("mod") * share_rows, share_rows, 0
    )
    share_normed = layer_norm(own_rows + pooled_share, post_gain).astype(jnp.bfloat16)
    normed = lax.all_gather(share_normed, "mod", axis=0, tiled=True)
    audio_tokens = jnp.dot(normed, audio_weight, preferred_element_type=jnp.float32).astype(
        jnp.bfloat16
    )
    patch_normed = rms_norm(patches.astype(jnp.float32), vision_gain).astype(jnp.bfloat16)
    merged = patch_normed.reshape(-1, 4 * patch_normed.shape[1])
    vision_share = lax.all_gather(vision_weight, "tm", axis=0, tiled=True)
    visual_tokens = jnp.dot(merged, vision_share, preferred_element_type=jnp.float32).astype(
        jnp.bfloat16
    )
    peer_count = lax.axis_size("tm")
    per_peer = (AUD_TOK + MRG_FRAME + peer_count - 1) // peer_count
    kept_here = kept_count[0]
    first_slot = starts[0]
    all_tokens = jnp.concatenate([visual_tokens, audio_tokens], axis=0)
    peer_ids = jnp.arange(peer_count, dtype=jnp.int32)[:, None]
    round_ids = jnp.arange(per_peer, dtype=jnp.int32)[None, :]
    local_index = round_ids * peer_count + (peer_ids - first_slot) % peer_count
    valid_rows = local_index < kept_here + AUD_TOK
    kept_index = jnp.take(retention[0], jnp.minimum(local_index, MRG_FRAME - 1), axis=0)
    source_index = jnp.where(
        local_index < kept_here, kept_index, MRG_FRAME + local_index - kept_here
    )
    source_index = jnp.where(valid_rows, source_index, 0).astype(jnp.int32)
    send_rows = jnp.take(all_tokens, source_index.reshape(-1), axis=0).reshape(
        peer_count, per_peer, all_tokens.shape[1]
    )
    send_slots = jnp.where(valid_rows, (first_slot + local_index) // peer_count, SEQ_DEV).astype(
        jnp.int32
    )
    recv_rows, recv_slots = (
        lax.all_to_all(send_rows, "tm", split_axis=0, concat_axis=0, tiled=True),
        lax.all_to_all(send_slots, "tm", split_axis=0, concat_axis=0, tiled=True),
    )
    sequence = jnp.zeros((SEQ_DEV, all_tokens.shape[1]), jnp.bfloat16)
    sequence = sequence.at[recv_slots.reshape(-1)].set(
        recv_rows.reshape(-1, all_tokens.shape[1]), mode="drop"
    )
    return sequence[None]


F32, BF16, I32 = jnp.float32, jnp.bfloat16, jnp.int32
MESH = pl.DeviceIdType.MESH
TM, MOD = 8, 4


def iota(shape, dim):
    return lax.broadcasted_iota(I32, shape, dim)


def onehot(mask, value=1.0):
    return jnp.where(mask, value, 0.0).astype(BF16)


def mm(a, b):
    return lax.dot_general(a, b, (((1,), (0,)), ((), ())), preferred_element_type=F32)


def mm_nt(a, b):
    return lax.dot_general(a, b, (((1,), (1,)), ((), ())), preferred_element_type=F32)


def mm_tn(a, b):
    return lax.dot_general(a, b, (((0,), (0,)), ((), ())), preferred_element_type=F32)


def gelu(x):
    return 0.5 * x * (1.0 + lax.erf(x * 0.7071067811865476))


FB, META, UPW, DNW, MRG, VIS, TOT, FWD, NRM, HID, COR, XAX = 0, 7, 14, 21, 28, 35, 42, 56, 59, 62, 66, 68
N_SEM = 70
HALF = 640
SHIFTS = (4, 3, 5, 2, 6, 1, 7)


def flipped(index, bits):
    for bit in (1, 2, 4):
        if bits % (2 * bit) >= bit:
            index = index + bit - 2 * bit * ((index // bit) % 2)
    return index


def fused_kernel(
    fb, conv_h, gain1, up, dn, gain2, aud_h, pat_h, gain_v, vis_h, ret, kept, out,
    conv, aud_w, pat, vis_w, fbp, meta, w_s, w_r, m_s, x_r, v_s, v_r, stem, hid, pa, own,
    a_s, a_r, b_s, b_r, c_s, c_r, nrm, load_sem, send_sem, recv_sem,
):
    me = lax.axis_index("tm")
    mo = lax.axis_index("mod")
    xx, cc = mo // 2, mo % 2
    tm_peers = [lax.rem(me + d, TM) for d in SHIFTS]
    tm_sources = [lax.rem(me + TM - d, TM) for d in SHIFTS]
    mod_peers = [flipped(mo, bits) for bits in (2, 3, 1)]
    x_peer, core_peer = mod_peers[0], mod_peers[2]

    barrier = pltpu.get_barrier_semaphore()
    for peer in tm_peers:
        pl.semaphore_signal(barrier, inc=1, device_id={"tm": peer}, device_id_type=MESH)
    for peer in mod_peers:
        pl.semaphore_signal(barrier, inc=1, device_id={"mod": peer}, device_id_type=MESH)

    quarter = pl.ds(pl.multiple_of(mo * 64, 64), 64)
    loads = [
        pltpu.make_async_copy(src, dst, load_sem.at[i])
        for i, (src, dst) in enumerate(
            [(pat_h.at[quarter], pat), (conv_h, conv), (vis_h, vis_w), (aud_h, aud_w)]
        )
    ]
    for c in loads:
        c.start()

    sent = []

    def copy(src, dst, slot, to):
        c = pltpu.make_async_remote_copy(
            src_ref=src, dst_ref=dst, send_sem=send_sem.at[slot], recv_sem=recv_sem.at[slot],
            device_id=to, device_id_type=MESH,
        )
        c.start()
        sent.append(c)
        return c

    def to_tm(src_of, dst, base):
        return [copy(src_of(p), dst, base + d, {"tm": p}) for d, p in enumerate(tm_peers)]

    def arrive(copies):
        for c in copies:
            c.wait_recv()

    fbp[0:16] = jnp.zeros((16, 128), BF16)
    fbp[1040:1056] = jnp.zeros((16, 128), BF16)
    my_rows = pl.ds(pl.multiple_of(16 + me * 128, 16), 128)
    fbp[my_rows, :] = fb[...]
    hit = onehot(ret[...] == iota((128, 64), 0) % 64)
    inv = mm_nt(iota((8, 64), 1).astype(F32).astype(BF16), hit)
    kept_f = jnp.full((8, 128), kept[0], I32).astype(F32)
    inv = jnp.where(inv < kept_f, inv, -4096.0)
    meta[me] = jnp.where(iota((8, 128), 0) == 0, inv, kept_f)

    row, col = iota((512, 128), 0), iota((512, 128), 1)
    for t in range(TM):
        w_s[t, 0:160] = up[:, 128 * t : 128 * t + 128]
        w_s[t, 240:400] = dn[:, 128 * t : 128 * t + 128]
    picks = [onehot((row // 128 == col // 32) & (row % 128 == 32 * a + col % 32)) for a in range(4)]
    for g in range(2):
        lanes = slice(1024 + 128 * g, 1152 + 128 * g)
        rest = jnp.concatenate(
            [up[0:80, lanes], up[80:160, lanes], dn[0:80, lanes], dn[80:160, lanes]], axis=1
        )
        for a in range(4):
            w_s[4 * g + a, 160:240] = mm(rest, picks[a]).astype(BF16)
    w_r[me] = w_s[me]

    def frames(d, p, source):
        first = 112 * (source % 2)
        edge = pl.ds(pl.multiple_of(first, 16), 16)
        there = pl.ds(pl.multiple_of(16 + source * 128 + first, 16), 16)
        whole = pl.ds(pl.multiple_of(16 + source * 128, 16), 128)
        return [
            pltpu.make_async_remote_copy(
                src_ref=src, dst_ref=dst, send_sem=send_sem.at[FB + d], recv_sem=recv_sem.at[FB + d],
                device_id={"tm": p}, device_id_type=MESH,
            )
            for src, dst in ((fb, fbp.at[whole]), (fb.at[edge], fbp.at[there]))
        ]

    def both_ways(source, act):
        here = (source // 2) % 2 == cc
        pl.when(here)(lambda: act(0))
        pl.when(jnp.logical_not(here))(lambda: act(1))

    fb_out = [frames(d, p, me) for d, p in enumerate(tm_peers)]
    fb_in = [frames(d, p, p) for d, p in enumerate(tm_sources)]
    pl.semaphore_wait(barrier, TM + MOD - 2)
    both_ways(me, lambda i: [c[i].start() for c in fb_out] and None)
    up_rows, dn_rows = pl.ds(0, 240), pl.ds(240, 160)
    u_copies = to_tm(lambda p: w_s.at[p, up_rows], w_r.at[me, up_rows], UPW)
    meta_copies = to_tm(lambda p: meta.at[me], meta.at[me], META)

    loads[0].wait()
    pv = pat[...].astype(F32)
    ms = jnp.sum(pv * pv, axis=1, keepdims=True) * (1.0 / 1280.0)
    pn = (pv * lax.rsqrt(ms + 1e-06) * gain_v[...][None, :]).astype(BF16)
    r64, c64 = iota((64, 64), 0), iota((64, 64), 1)
    pn = mm(onehot(c64 == 4 * (r64 % 16) + r64 // 16), pn).astype(BF16)
    for t in range(TM):
        q, h = t // 2, t % 2
        m_s[t] = pn[16 * q : 16 * q + 16, HALF * h : HALF * h + HALF]
    m_copies = to_tm(lambda p: m_s.at[p], x_r.at[me, mo], MRG)
    x_r[me, mo] = m_s[me]
    d_copies = to_tm(lambda p: w_s.at[p, dn_rows], w_r.at[me, dn_rows], DNW)

    loads[1].wait()
    for d, p in enumerate(tm_sources):
        both_ways(p, lambda i: fb_in[d][i].wait_recv())

    def stem_step(first):
        base = pl.multiple_of(first * 128, 128)
        rows = fbp[pl.ds(base, 160), :].astype(F32)
        taps = jnp.concatenate([rows[15:143], rows[16:144], rows[17:145]], axis=1).astype(BF16)
        st = gelu(mm(taps, conv[...])).astype(BF16)
        stem[pl.ds(base, 128), :] = st
        v = st.astype(F32)
        v = v - jnp.sum(v, axis=1, keepdims=True) * (1.0 / 1280.0)
        var = jnp.sum(v * v, axis=1, keepdims=True) * (1.0 / 1280.0)
        hid[pl.ds(base, 128), :] = (v * lax.rsqrt(var + 1e-05) * gain1[...][None, :]).astype(BF16)

    h_copies = []
    for k in range(4):
        x_at = 1 - xx if k < 2 else xx
        span = 2 * (2 * x_at + cc) + k % 2
        stem_step(span)
        rows = pl.ds(pl.multiple_of(span * 128, 128), 128)
        h_copies.append(copy(hid.at[rows], hid.at[rows], HID + k, {"mod": core_peer}))
        if k == 1:
            arrive(m_copies)
            x_copies = [
                copy(x_r.at[:, mo], x_r.at[:, mo], FWD + d, {"mod": p})
                for d, p in enumerate((x_peer, core_peer))
            ]
    x_copies[0].wait_recv()
    x_copies.append(copy(x_r.at[:, x_peer], x_r.at[:, x_peer], FWD + 2, {"mod": core_peer}))

    arrive(meta_copies)
    ends, before, running = [], [], jnp.zeros((1, 128), F32)
    for s in range(TM):
        before.append(running)
        running = running + meta[s, 1:2, :]
        ends.append(running.astype(I32))

    def ends_of(pair):
        picked = []
        for h in range(2):
            e = ends[h]
            for p in range(1, MOD):
                e = jnp.where(pair == p, ends[2 * p + h], e)
            picked.append(e)
        return picked

    def pool_rows(holder, r_s2, r_q, frames, span_ends):
        blocks = []
        for h in range(2):
            j = 8 * r_q + ((holder - span_ends[h]) & 7)
            blocks.append(onehot((r_s2 == h) & (frames // 2 == j), 0.5))
        return jnp.concatenate(blocks, axis=1)

    arrive(u_copies)
    rem = jnp.concatenate([w_r[t, 160:240] for t in range(TM)], axis=0)
    ri, ci = iota((128, 512), 0), iota((128, 512), 1)
    rem = mm(rem, onehot((ci % 128 < 32) & (ri == 32 * (ci // 128) + ci % 128))).astype(BF16)

    def assemble(first, lane):
        main = jnp.concatenate([w_r[t, first : first + 160] for t in range(TM)], axis=0)
        parts = []
        for t in range(TM):
            parts.append(rem[80 * t : 80 * t + 80, lane : lane + 128])
            parts.append(rem[80 * t : 80 * t + 80, lane + 128 : lane + 256])
        return jnp.concatenate([main, jnp.concatenate(parts, axis=0)], axis=1)

    up_all = assemble(0, 0)
    r128, c128 = iota((128, 128), 0), iota((128, 128), 1)
    order = [(1 - cc, 1 - xx), (1 - cc, xx), (cc, 1 - xx), (cc, xx)]
    for k in (2, 0, 3, 1):
        if k < 2:
            arrive(h_copies[2 * k : 2 * k + 2])
        pair = 2 * order[k][1] + order[k][0]
        rows = pl.ds(pl.multiple_of(pair * 256, 256), 256)
        act = gelu(mm(hid[rows, :], up_all)).astype(BF16)
        pool = pool_rows(r128 // 16, (r128 // 8) % 2, r128 % 8, c128, ends_of(pair))
        pa[k] = mm(pool, act).astype(BF16)

    arrive(x_copies[1:])
    lane = iota((1, 128), 1)
    pos = jnp.concatenate(
        [
            jnp.where(lane < 64, meta[t, 0:1, :] + before[t], meta[t + 1, 0:1, :] + before[t + 1])
            for t in range(0, TM, 2)
        ],
        axis=1,
    ).astype(I32)
    r256 = iota((256, 512), 0)
    pick = onehot(pos == 8 * (r256 % 32) + r256 // 32)
    chosen = mm(pick, x_r[...].reshape(512, HALF)).astype(BF16)
    loads[2].wait()
    v_s[...] = mm_nt(chosen, vis_w[...]).astype(BF16).reshape(TM, 32, 448)
    v_copies = to_tm(lambda p: v_s.at[p], v_r.at[me], VIS)
    v_r[me] = v_s[me]

    arrive(d_copies)
    dn_all = assemble(240, 256)
    a_copies, b_copies, c_copies = [], [], []
    for h in range(2):
        product = mm_nt(pa[...].reshape(512, 256), dn_all[HALF * h : HALF * h + HALF])
        a_s[h] = product[0:256].astype(BF16)
        a_copies.append(copy(a_s.at[h], a_r.at[h], COR + h, {"mod": core_peer}))
        own[h] = product[256:512]
    for h in range(2):
        a_copies[h].wait_recv()
        b_s[h] = (own[h, 0:128] + a_r[h, 0:128].astype(F32)).astype(BF16)
        b_copies.append(copy(b_s.at[h], b_r.at[h], XAX + h, {"mod": x_peer}))

    r16, c16 = iota((16, 128), 0), iota((16, 128), 1)
    pool = pool_rows(me, r16 // 8, r16 % 8, c16, ends_of(mo))
    pooled = mm(pool, stem[pl.ds(pl.multiple_of(mo * 256, 256), 256), :])
    g = 8 * lane + me
    v_slot = lane
    a_slot = jnp.zeros((1, 128), I32)
    for s in range(TM):
        v_slot = v_slot + jnp.where(ends[s] <= g, 8, 0)
        j = 8 * (lane % 8) + ((me - ends[s]) & 7)
        a_slot = jnp.where((lane - 32) // 8 == s, ((ends[s] + j) >> 3) + 8 * s, a_slot)
    slot = jnp.where(lane < 32, v_slot, jnp.where(lane < 96, a_slot, -1))
    place = onehot(slot == iota((96, 128), 0))

    for h in range(2):
        total = own[h, 128:256] + a_r[h, 128:256].astype(F32)
        b_copies[h].wait_recv()
        total = total + b_r[h].astype(F32)
        c_s[h] = total.astype(BF16).reshape(TM, 16, HALF)
        c_copies.append(to_tm(lambda p: c_s.at[h, p], c_r.at[h, me], TOT + 7 * h))
        c_r[h, me] = c_s[h, me]

    arrive(v_copies)
    visual = v_r[0].astype(F32)
    for t in range(1, TM):
        visual = visual + v_r[t].astype(F32)

    halves = []
    for h in range(2):
        arrive(c_copies[h])
        part = pooled[:, HALF * h : HALF * h + HALF]
        for t in range(TM):
            part = part + c_r[h, t].astype(F32)
        halves.append(part)
    pooled = jnp.concatenate(halves, axis=1)
    v = pooled - jnp.sum(pooled, axis=1, keepdims=True) * (1.0 / 1280.0)
    var = jnp.sum(v * v, axis=1, keepdims=True) * (1.0 / 1280.0)
    nrm[mo] = (v * lax.rsqrt(var + 1e-05) * gain2[...][None, :]).astype(BF16)
    n_copies = [copy(nrm.at[mo], nrm.at[mo], NRM + d, {"mod": p}) for d, p in enumerate(mod_peers)]
    loads[3].wait()
    arrive(n_copies)
    audio = mm_nt(nrm[...].reshape(64, 1280), aud_w[...])
    tokens = jnp.concatenate(
        [visual.astype(BF16), audio.astype(BF16), jnp.zeros((32, 448), BF16)], axis=0
    )
    out[...] = mm(place, tokens).astype(BF16)

    for c in sent:
        c.wait_send()
    both_ways(me, lambda i: [c[i].wait_send() for c in fb_out] and None)


def on_device_fused(
    filterbank, conv_weight, mlp_gain, up_weight, down_weight, post_gain, audio_weight,
    patches, vision_gain, vision_weight, retention, kept_count,
):
    vm = pl.BlockSpec(memory_space=pltpu.VMEM)
    far = pl.BlockSpec(memory_space=pl.ANY)
    n_out = vision_weight.shape[1]
    scratch = [
        pltpu.VMEM(conv_weight.shape, BF16),
        pltpu.VMEM((n_out, 1280), BF16),
        pltpu.VMEM((64, 1280), BF16),
        pltpu.VMEM((n_out, HALF), BF16),
        pltpu.VMEM((1056, 128), BF16),
        pltpu.VMEM((TM, 8, 128), F32),
        pltpu.VMEM((TM, 400, 128), BF16),
        pltpu.VMEM((TM, 400, 128), BF16),
        pltpu.VMEM((TM, 16, HALF), BF16),
        pltpu.VMEM((TM, MOD, 16, HALF), BF16),
        pltpu.VMEM((TM, 32, n_out), BF16),
        pltpu.VMEM((TM, 32, n_out), BF16),
        pltpu.VMEM((1024, 1280), BF16),
        pltpu.VMEM((1024, 1280), BF16),
        pltpu.VMEM((MOD, 128, 256), BF16),
        pltpu.VMEM((2, 256, HALF), F32),
        pltpu.VMEM((2, 256, HALF), BF16),
        pltpu.VMEM((2, 256, HALF), BF16),
        pltpu.VMEM((2, 128, HALF), BF16),
        pltpu.VMEM((2, 128, HALF), BF16),
        pltpu.VMEM((2, TM, 16, HALF), BF16),
        pltpu.VMEM((2, TM, 16, HALF), BF16),
        pltpu.VMEM((MOD, 16, 1280), BF16),
        pltpu.SemaphoreType.DMA((4,)),
        pltpu.SemaphoreType.DMA((N_SEM,)),
        pltpu.SemaphoreType.DMA((N_SEM,)),
    ]
    sequence = pl.pallas_call(
        fused_kernel,
        out_shape=jax.ShapeDtypeStruct((SEQ_DEV, vision_weight.shape[1]), BF16),
        in_specs=[vm, far, vm, vm, vm, vm, far, far, vm, far, vm, pl.BlockSpec(memory_space=pltpu.SMEM)],
        out_specs=vm,
        scratch_shapes=scratch,
        compiler_params=pltpu.CompilerParams(
            collective_id=0, has_side_effects=True, vmem_limit_bytes=56 * 1024 * 1024
        ),
    )(
        filterbank, conv_weight, mlp_gain, up_weight, down_weight.T, post_gain,
        audio_weight.T, patches, vision_gain, vision_weight.T, retention, kept_count,
    )
    return sequence[None]


def solution(mesh):
    fused = mesh.shape["tm"] == TM and mesh.shape["mod"] == MOD
    return jax.shard_map(
        on_device_fused if fused else on_device,
        mesh=mesh,
        in_specs=(
            P("tm", None),
            P(),
            P(),
            P("tm", "mod"),
            P("mod", "tm"),
            P(),
            P(None, "mod"),
            P("tm", None),
            P(),
            P("tm", "mod"),
            P("tm", None),
            P("tm"),
        ),
        out_specs=P("tm", None, "mod"),
        check_vma=False,
    )
```

```python
import jax
import jax.numpy as jnp
from jax import lax
from jax.experimental import pallas as pl
from jax.experimental.pallas import tpu as pltpu
from jax.sharding import PartitionSpec as P

MRG_FRAME = 64
AUD_TOK = 64
SEQ_DEV = 96


def carried_in(value, axis, join, neutral):
    count, mine = (lax.axis_size(axis), lax.axis_index(axis))
    pieces = lax.all_gather(value, axis)
    running = jnp.full_like(value, 0) + jnp.asarray(neutral, value.dtype)

    def hop(position, running):
        longer = join(running, pieces[position])
        return jnp.where(position < mine, longer, running)

    return lax.fori_loop(0, count - 1, hop, running)


def padded(shard, sides, width):
    for axis, dim in sides:
        peers, length = (lax.axis_size(axis), shard.shape[dim])
        up = [(i, (i + 1) % peers) for i in range(peers - 1)]
        down = [(j, i) for i, j in up]
        last = lax.slice_in_dim(shard, length - width, length, axis=dim)
        first = lax.slice_in_dim(shard, 0, width, axis=dim)
        before = lax.ppermute(last, axis, up)
        after = lax.ppermute(first, axis, down)
        shard = jnp.concatenate([before, shard, after], axis=dim)
    return shard


def layer_norm(values, scale_gain):
    average = jnp.mean(values, axis=-1, keepdims=True)
    centred = values - average
    variance = jnp.mean(centred * centred, axis=-1, keepdims=True)
    return centred * lax.rsqrt(variance + 1e-05) * scale_gain


def rms_norm(values, scale_gain):
    square_mean = jnp.mean(values * values, axis=-1, keepdims=True)
    return values * lax.rsqrt(square_mean + 1e-06) * scale_gain


def pool_pairs(values):
    return values.reshape(-1, 2, values.shape[-1]).mean(axis=1)


def add_counts(earlier, later):
    return earlier + later


def on_device(
    filterbank,
    conv_weight,
    mlp_gain,
    up_weight,
    down_weight,
    post_gain,
    audio_weight,
    patches,
    vision_gain,
    vision_weight,
    retention,
    kept_count,
):
    placed = kept_count + AUD_TOK
    starts = carried_in(placed, "tm", add_counts, jnp.zeros((1,), jnp.int32))
    framed = padded(filterbank, (("tm", 0),), 1)
    unfolded = jnp.concatenate([framed[:-2], framed[1:-1], framed[2:]], axis=1)
    stem = jax.nn.gelu(
        jnp.dot(unfolded, conv_weight, preferred_element_type=jnp.float32), approximate=False
    ).astype(jnp.bfloat16)
    residual = stem.astype(jnp.float32)
    hidden = layer_norm(residual, mlp_gain).astype(jnp.bfloat16)
    up_share = lax.all_gather(up_weight, "tm", axis=0, tiled=True)
    pre_act = jnp.dot(hidden, up_share, preferred_element_type=jnp.float32)
    activated = jax.nn.gelu(pre_act, approximate=False).astype(jnp.bfloat16)
    down_share = lax.all_gather(down_weight, "tm", axis=1, tiled=True)
    partial_value = jnp.dot(activated, down_share, preferred_element_type=jnp.float32)
    pooled_share = lax.psum_scatter(
        pool_pairs(partial_value).astype(jnp.bfloat16), "mod", scatter_dimension=0, tiled=True
    ).astype(jnp.float32)
    share_rows = pooled_share.shape[0]
    own_rows = lax.dynamic_slice_in_dim(
        pool_pairs(residual), lax.axis_index("mod") * share_rows, share_rows, 0
    )
    share_normed = layer_norm(own_rows + pooled_share, post_gain).astype(jnp.bfloat16)
    normed = lax.all_gather(share_normed, "mod", axis=0, tiled=True)
    audio_tokens = jnp.dot(normed, audio_weight, preferred_element_type=jnp.float32).astype(
        jnp.bfloat16
    )
    patch_normed = rms_norm(patches.astype(jnp.float32), vision_gain).astype(jnp.bfloat16)
    merged = patch_normed.reshape(-1, 4 * patch_normed.shape[1])
    vision_share = lax.all_gather(vision_weight, "tm", axis=0, tiled=True)
    visual_tokens = jnp.dot(merged, vision_share, preferred_element_type=jnp.float32).astype(
        jnp.bfloat16
    )
    peer_count = lax.axis_size("tm")
    per_peer = (AUD_TOK + MRG_FRAME + peer_count - 1) // peer_count
    kept_here = kept_count[0]
    first_slot = starts[0]
    all_tokens = jnp.concatenate([visual_tokens, audio_tokens], axis=0)
    peer_ids = jnp.arange(peer_count, dtype=jnp.int32)[:, None]
    round_ids = jnp.arange(per_peer, dtype=jnp.int32)[None, :]
    local_index = round_ids * peer_count + (peer_ids - first_slot) % peer_count
    valid_rows = local_index < kept_here + AUD_TOK
    kept_index = jnp.take(retention[0], jnp.minimum(local_index, MRG_FRAME - 1), axis=0)
    source_index = jnp.where(
        local_index < kept_here, kept_index, MRG_FRAME + local_index - kept_here
    )
    source_index = jnp.where(valid_rows, source_index, 0).astype(jnp.int32)
    send_rows = jnp.take(all_tokens, source_index.reshape(-1), axis=0).reshape(
        peer_count, per_peer, all_tokens.shape[1]
    )
    send_slots = jnp.where(valid_rows, (first_slot + local_index) // peer_count, SEQ_DEV).astype(
        jnp.int32
    )
    recv_rows, recv_slots = (
        lax.all_to_all(send_rows, "tm", split_axis=0, concat_axis=0, tiled=True),
        lax.all_to_all(send_slots, "tm", split_axis=0, concat_axis=0, tiled=True),
    )
    sequence = jnp.zeros((SEQ_DEV, all_tokens.shape[1]), jnp.bfloat16)
    sequence = sequence.at[recv_slots.reshape(-1)].set(
        recv_rows.reshape(-1, all_tokens.shape[1]), mode="drop"
    )
    return sequence[None]


F32, BF16, I32 = jnp.float32, jnp.bfloat16, jnp.int32
MESH = pl.DeviceIdType.MESH
TM, MOD = 8, 4


def iota(shape, dim):
    return lax.broadcasted_iota(I32, shape, dim)


def onehot(mask, value=1.0):
    return jnp.where(mask, value, 0.0).astype(BF16)


def mm(a, b):
    return lax.dot_general(a, b, (((1,), (0,)), ((), ())), preferred_element_type=F32)


def mm_nt(a, b):
    return lax.dot_general(a, b, (((1,), (1,)), ((), ())), preferred_element_type=F32)


def mm_tn(a, b):
    return lax.dot_general(a, b, (((0,), (0,)), ((), ())), preferred_element_type=F32)


def gelu(x):
    return 0.5 * x * (1.0 + lax.erf(x * 0.7071067811865476))


FB, META, UPW, DNW, MRG, VIS, TOT, FWD, NRM, HID, COR, XAX = 0, 7, 14, 21, 28, 35, 42, 56, 59, 62, 66, 68
N_SEM = 70
HALF = 640
SHIFTS = (4, 3, 5, 2, 6, 1, 7)


def flipped(index, bits):
    for bit in (1, 2, 4):
        if bits % (2 * bit) >= bit:
            index = index + bit - 2 * bit * ((index // bit) % 2)
    return index


def fused_kernel(
    fb, conv_h, gain1, up, dn, gain2, aud_h, pat_h, gain_v, vis_h, ret, kept, out,
    conv, aud_w, pat, vis_w, fbp, meta, w_s, w_r, m_s, x_r, v_s, v_r, pre, w_all, stem, hid, pa, own,
    a_s, a_r, b_s, b_r, c_s, c_r, nrm, load_sem, send_sem, recv_sem,
):
    me = lax.axis_index("tm")
    mo = lax.axis_index("mod")
    xx, cc = mo // 2, mo % 2
    tm_peers = [lax.rem(me + d, TM) for d in SHIFTS]
    tm_sources = [lax.rem(me + TM - d, TM) for d in SHIFTS]
    mod_peers = [flipped(mo, bits) for bits in (2, 3, 1)]
    x_peer, core_peer = mod_peers[0], mod_peers[2]

    barrier = pltpu.get_barrier_semaphore()
    for peer in tm_peers:
        pl.semaphore_signal(barrier, inc=1, device_id={"tm": peer}, device_id_type=MESH)
    for peer in mod_peers:
        pl.semaphore_signal(barrier, inc=1, device_id={"mod": peer}, device_id_type=MESH)

    quarter = pl.ds(pl.multiple_of(mo * 64, 64), 64)
    loads = [
        pltpu.make_async_copy(src, dst, load_sem.at[i])
        for i, (src, dst) in enumerate(
            [(pat_h.at[quarter], pat), (conv_h, conv), (vis_h, vis_w), (aud_h, aud_w)]
        )
    ]
    for c in loads:
        c.start()

    sent = []

    def describe(src, dst, slot, to):
        return pltpu.make_async_remote_copy(
            src_ref=src, dst_ref=dst, send_sem=send_sem.at[slot], recv_sem=recv_sem.at[slot],
            device_id=to, device_id_type=MESH,
        )

    def copy(src, dst, slot, to):
        c = describe(src, dst, slot, to)
        c.start()
        sent.append(c)
        return c

    def to_tm(src_of, dst, base):
        return [copy(src_of(p), dst, base + d, {"tm": p}) for d, p in enumerate(tm_peers)]

    def arrive(copies):
        for c in copies:
            c.wait_recv()

    fbp[0:16] = jnp.zeros((16, 128), BF16)
    fbp[1040:1056] = jnp.zeros((16, 128), BF16)
    my_rows = pl.ds(pl.multiple_of(16 + me * 128, 16), 128)
    fbp[my_rows, :] = fb[...]
    hit = onehot(ret[...] == iota((128, 64), 0) % 64)
    inv = mm_nt(iota((8, 64), 1).astype(F32).astype(BF16), hit)
    kept_f = jnp.full((8, 128), kept[0], I32).astype(F32)
    inv = jnp.where(inv < kept_f, inv, -4096.0)
    meta[me] = jnp.where(iota((8, 128), 0) == 0, inv, kept_f)

    row, col = iota((512, 128), 0), iota((512, 128), 1)
    for t in range(TM):
        w_s[t, 0:160] = up[:, 128 * t : 128 * t + 128]
        w_s[t, 240:400] = dn[:, 128 * t : 128 * t + 128]
    picks = [onehot((row // 128 == col // 32) & (row % 128 == 32 * a + col % 32)) for a in range(4)]
    for g in range(2):
        lanes = slice(1024 + 128 * g, 1152 + 128 * g)
        rest = jnp.concatenate(
            [up[0:80, lanes], up[80:160, lanes], dn[0:80, lanes], dn[80:160, lanes]], axis=1
        )
        for a in range(4):
            w_s[4 * g + a, 160:240] = mm(rest, picks[a]).astype(BF16)
    w_r[me] = w_s[me]

    def frames(d, p, source):
        first = 112 * (source % 2)
        edge = pl.ds(pl.multiple_of(first, 16), 16)
        there = pl.ds(pl.multiple_of(16 + source * 128 + first, 16), 16)
        whole = pl.ds(pl.multiple_of(16 + source * 128, 16), 128)
        return [
            pltpu.make_async_remote_copy(
                src_ref=src, dst_ref=dst, send_sem=send_sem.at[FB + d], recv_sem=recv_sem.at[FB + d],
                device_id={"tm": p}, device_id_type=MESH,
            )
            for src, dst in ((fb, fbp.at[whole]), (fb.at[edge], fbp.at[there]))
        ]

    def both_ways(source, act):
        here = (source // 2) % 2 == cc
        pl.when(here)(lambda: act(0))
        pl.when(jnp.logical_not(here))(lambda: act(1))

    fb_out = [frames(d, p, me) for d, p in enumerate(tm_peers)]
    fb_in = [frames(d, p, p) for d, p in enumerate(tm_sources)]
    pl.semaphore_wait(barrier, TM + MOD - 2)
    both_ways(me, lambda i: [c[i].start() for c in fb_out] and None)
    up_rows, dn_rows = pl.ds(0, 240), pl.ds(240, 160)
    u_copies = to_tm(lambda p: w_s.at[p, up_rows], w_r.at[me, up_rows], UPW)
    meta_copies = to_tm(lambda p: meta.at[me], meta.at[me], META)

    loads[0].wait()
    pv = pat[...].astype(F32)
    ms = jnp.sum(pv * pv, axis=1, keepdims=True) * (1.0 / 1280.0)
    pn = (pv * lax.rsqrt(ms + 1e-06) * gain_v[...][None, :]).astype(BF16)
    r64, c64 = iota((64, 64), 0), iota((64, 64), 1)
    pn = mm(onehot(c64 == 4 * (r64 % 16) + r64 // 16), pn).astype(BF16)
    for t in range(TM):
        q, h = t // 2, t % 2
        m_s[t] = pn[16 * q : 16 * q + 16, HALF * h : HALF * h + HALF]
    m_copies = to_tm(lambda p: m_s.at[p], x_r.at[me, mo], MRG)
    x_r[me, mo] = m_s[me]
    d_copies = to_tm(lambda p: w_s.at[p, dn_rows], w_r.at[me, dn_rows], DNW)

    loads[1].wait()
    for d, p in enumerate(tm_sources):
        both_ways(p, lambda i: fb_in[d][i].wait_recv())

    def span_of(k):
        x_at = (1 - xx) + (k // 2) * (2 * xx - 1)
        return 2 * (2 * x_at + cc) + k % 2

    def hidden_rows(k):
        rows = pl.ds(pl.multiple_of(span_of(k) * 128, 128), 128)
        return describe(hid.at[rows], hid.at[rows], HID + k, {"mod": core_peer})

    x_copies = [
        describe(x_r.at[:, mo], x_r.at[:, mo], FWD + d, {"mod": p})
        for d, p in enumerate((x_peer, core_peer))
    ]

    def stem_step(k, carry):
        base = pl.multiple_of(span_of(k) * 128, 128)
        rows = fbp[pl.ds(base, 160), :].astype(F32)
        taps = jnp.concatenate([rows[15:143], rows[16:144], rows[17:145]], axis=1).astype(BF16)
        pre[...] = mm(taps, conv[...])

        def piece(i, carry):
            at = pl.multiple_of(i * 32, 32)
            st = gelu(pre[pl.ds(at, 32), :]).astype(BF16)
            there = pl.ds(pl.multiple_of(base + at, 32), 32)
            stem[there, :] = st
            v = st.astype(F32)
            v = v - jnp.sum(v, axis=1, keepdims=True) * (1.0 / 1280.0)
            var = jnp.sum(v * v, axis=1, keepdims=True) * (1.0 / 1280.0)
            hid[there, :] = (v * lax.rsqrt(var + 1e-05) * gain1[...][None, :]).astype(BF16)
            return carry

        lax.fori_loop(0, 4, piece, 0)
        hidden_rows(k).start()

        @pl.when(k == 1)
        def _():
            arrive(m_copies)
            for c in x_copies:
                c.start()

        return carry

    lax.fori_loop(0, 4, stem_step, 0)
    h_copies = [hidden_rows(k) for k in range(4)]
    sent.extend(h_copies + x_copies)
    x_copies[0].wait_recv()
    x_copies.append(copy(x_r.at[:, x_peer], x_r.at[:, x_peer], FWD + 2, {"mod": core_peer}))

    arrive(meta_copies)
    ends, before, running = [], [], jnp.zeros((1, 128), F32)
    for s in range(TM):
        before.append(running)
        running = running + meta[s, 1:2, :]
        ends.append(running.astype(I32))

    def ends_of(pair):
        picked = []
        for h in range(2):
            e = ends[h]
            for p in range(1, MOD):
                e = jnp.where(pair == p, ends[2 * p + h], e)
            picked.append(e)
        return picked

    def pool_rows(holder, r_s2, r_q, frames, span_ends):
        blocks = []
        for h in range(2):
            j = 8 * r_q + ((holder - span_ends[h]) & 7)
            blocks.append(onehot((r_s2 == h) & (frames // 2 == j), 0.5))
        return jnp.concatenate(blocks, axis=1)

    arrive(u_copies)
    rem = jnp.concatenate([w_r[t, 160:240] for t in range(TM)], axis=0)
    ri, ci = iota((128, 512), 0), iota((128, 512), 1)
    rem = mm(rem, onehot((ci % 128 < 32) & (ri == 32 * (ci // 128) + ci % 128))).astype(BF16)

    def assemble(first, lane):
        main = jnp.concatenate([w_r[t, first : first + 160] for t in range(TM)], axis=0)
        parts = []
        for t in range(TM):
            parts.append(rem[80 * t : 80 * t + 80, lane : lane + 128])
            parts.append(rem[80 * t : 80 * t + 80, lane + 128 : lane + 256])
        return jnp.concatenate([main, jnp.concatenate(parts, axis=0)], axis=1)

    w_all[...] = assemble(0, 0)
    r128, c128 = iota((128, 128), 0), iota((128, 128), 1)

    def feed(step, carry):
        k = lax.rem(2 + 2 * step + step // 2, 4)
        core = (1 - cc) + (k // 2) * (2 * cc - 1)
        x_at = (1 - xx) + (k % 2) * (2 * xx - 1)
        pl.when(step == 1)(lambda: arrive(h_copies[0:2]))
        pl.when(step == 3)(lambda: arrive(h_copies[2:4]))
        pair = 2 * x_at + core
        rows = pl.ds(pl.multiple_of(pair * 256, 256), 256)
        act = gelu(mm(hid[rows, :], w_all[...])).astype(BF16)
        pool = pool_rows(r128 // 16, (r128 // 8) % 2, r128 % 8, c128, ends_of(pair))
        pa[k] = mm(pool, act).astype(BF16)
        return carry

    lax.fori_loop(0, 4, feed, 0)

    arrive(x_copies[1:])
    lane = iota((1, 128), 1)
    pos = jnp.concatenate(
        [
            jnp.where(lane < 64, meta[t, 0:1, :] + before[t], meta[t + 1, 0:1, :] + before[t + 1])
            for t in range(0, TM, 2)
        ],
        axis=1,
    ).astype(I32)
    r256 = iota((256, 512), 0)
    pick = onehot(pos == 8 * (r256 % 32) + r256 // 32)
    chosen = mm(pick, x_r[...].reshape(512, HALF)).astype(BF16)
    loads[2].wait()
    v_s[...] = mm_nt(chosen, vis_w[...]).astype(BF16).reshape(TM, 32, 448)
    v_copies = to_tm(lambda p: v_s.at[p], v_r.at[me], VIS)
    v_r[me] = v_s[me]

    arrive(d_copies)
    w_all[...] = assemble(240, 256)

    def core_sum(h):
        return describe(a_s.at[h], a_r.at[h], COR + h, {"mod": core_peer})

    def x_sum(h):
        return describe(b_s.at[h], b_r.at[h], XAX + h, {"mod": x_peer})

    def product_half(h, carry):
        cols = pl.ds(pl.multiple_of(h * HALF, HALF), HALF)
        product = mm_nt(pa[...].reshape(512, 256), w_all[cols, :])
        a_s[h] = product[0:256].astype(BF16)
        core_sum(h).start()
        own[h] = product[256:512]
        return carry

    lax.fori_loop(0, 2, product_half, 0)

    def x_half(h, carry):
        core_sum(h).wait_recv()
        b_s[h] = (own[h, 0:128] + a_r[h, 0:128].astype(F32)).astype(BF16)
        x_sum(h).start()
        return carry

    lax.fori_loop(0, 2, x_half, 0)
    b_copies = [x_sum(h) for h in range(2)]
    sent.extend([core_sum(h) for h in range(2)] + b_copies)
    c_copies = []

    r16, c16 = iota((16, 128), 0), iota((16, 128), 1)
    pool = pool_rows(me, r16 // 8, r16 % 8, c16, ends_of(mo))
    pooled = mm(pool, stem[pl.ds(pl.multiple_of(mo * 256, 256), 256), :])
    g = 8 * lane + me
    v_slot = lane
    a_slot = jnp.zeros((1, 128), I32)
    for s in range(TM):
        v_slot = v_slot + jnp.where(ends[s] <= g, 8, 0)
        j = 8 * (lane % 8) + ((me - ends[s]) & 7)
        a_slot = jnp.where((lane - 32) // 8 == s, ((ends[s] + j) >> 3) + 8 * s, a_slot)
    slot = jnp.where(lane < 32, v_slot, jnp.where(lane < 96, a_slot, -1))
    place = onehot(slot == iota((96, 128), 0))

    for h in range(2):
        total = own[h, 128:256] + a_r[h, 128:256].astype(F32)
        b_copies[h].wait_recv()
        total = total + b_r[h].astype(F32)
        c_s[h] = total.astype(BF16).reshape(TM, 16, HALF)
        c_copies.append(to_tm(lambda p: c_s.at[h, p], c_r.at[h, me], TOT + 7 * h))
        c_r[h, me] = c_s[h, me]

    arrive(v_copies)
    visual = v_r[0].astype(F32)
    for t in range(1, TM):
        visual = visual + v_r[t].astype(F32)

    halves = []
    for h in range(2):
        arrive(c_copies[h])
        part = pooled[:, HALF * h : HALF * h + HALF]
        for t in range(TM):
            part = part + c_r[h, t].astype(F32)
        halves.append(part)
    pooled = jnp.concatenate(halves, axis=1)
    v = pooled - jnp.sum(pooled, axis=1, keepdims=True) * (1.0 / 1280.0)
    var = jnp.sum(v * v, axis=1, keepdims=True) * (1.0 / 1280.0)
    nrm[mo] = (v * lax.rsqrt(var + 1e-05) * gain2[...][None, :]).astype(BF16)
    n_copies = [copy(nrm.at[mo], nrm.at[mo], NRM + d, {"mod": p}) for d, p in enumerate(mod_peers)]
    loads[3].wait()
    arrive(n_copies)
    audio = mm_nt(nrm[...].reshape(64, 1280), aud_w[...])
    tokens = jnp.concatenate(
        [visual.astype(BF16), audio.astype(BF16), jnp.zeros((32, 448), BF16)], axis=0
    )
    out[...] = mm(place, tokens).astype(BF16)

    for c in sent:
        c.wait_send()
    both_ways(me, lambda i: [c[i].wait_send() for c in fb_out] and None)


def on_device_fused(
    filterbank, conv_weight, mlp_gain, up_weight, down_weight, post_gain, audio_weight,
    patches, vision_gain, vision_weight, retention, kept_count,
):
    vm = pl.BlockSpec(memory_space=pltpu.VMEM)
    far = pl.BlockSpec(memory_space=pl.ANY)
    n_out = vision_weight.shape[1]
    scratch = [
        pltpu.VMEM(conv_weight.shape, BF16),
        pltpu.VMEM((n_out, 1280), BF16),
        pltpu.VMEM((64, 1280), BF16),
        pltpu.VMEM((n_out, HALF), BF16),
        pltpu.VMEM((1056, 128), BF16),
        pltpu.VMEM((TM, 8, 128), F32),
        pltpu.VMEM((TM, 400, 128), BF16),
        pltpu.VMEM((TM, 400, 128), BF16),
        pltpu.VMEM((TM, 16, HALF), BF16),
        pltpu.VMEM((TM, MOD, 16, HALF), BF16),
        pltpu.VMEM((TM, 32, n_out), BF16),
        pltpu.VMEM((TM, 32, n_out), BF16),
        pltpu.VMEM((128, 1280), F32),
        pltpu.VMEM((1280, 256), BF16),
        pltpu.VMEM((1024, 1280), BF16),
        pltpu.VMEM((1024, 1280), BF16),
        pltpu.VMEM((MOD, 128, 256), BF16),
        pltpu.VMEM((2, 256, HALF), F32),
        pltpu.VMEM((2, 256, HALF), BF16),
        pltpu.VMEM((2, 256, HALF), BF16),
        pltpu.VMEM((2, 128, HALF), BF16),
        pltpu.VMEM((2, 128, HALF), BF16),
        pltpu.VMEM((2, TM, 16, HALF), BF16),
        pltpu.VMEM((2, TM, 16, HALF), BF16),
        pltpu.VMEM((MOD, 16, 1280), BF16),
        pltpu.SemaphoreType.DMA((4,)),
        pltpu.SemaphoreType.DMA((N_SEM,)),
        pltpu.SemaphoreType.DMA((N_SEM,)),
    ]
    sequence = pl.pallas_call(
        fused_kernel,
        out_shape=jax.ShapeDtypeStruct((SEQ_DEV, vision_weight.shape[1]), BF16),
        in_specs=[vm, far, vm, vm, vm, vm, far, far, vm, far, vm, pl.BlockSpec(memory_space=pltpu.SMEM)],
        out_specs=vm,
        scratch_shapes=scratch,
        compiler_params=pltpu.CompilerParams(
            collective_id=0, has_side_effects=True, vmem_limit_bytes=56 * 1024 * 1024
        ),
    )(
        filterbank, conv_weight, mlp_gain, up_weight, down_weight.T, post_gain,
        audio_weight.T, patches, vision_gain, vision_weight.T, retention, kept_count,
    )
    return sequence[None]


def solution(mesh):
    fused = mesh.shape["tm"] == TM and mesh.shape["mod"] == MOD
    return jax.shard_map(
        on_device_fused if fused else on_device,
        mesh=mesh,
        in_specs=(
            P("tm", None),
            P(),
            P(),
            P("tm", "mod"),
            P("mod", "tm"),
            P(),
            P(None, "mod"),
            P("tm", None),
            P(),
            P("tm", "mod"),
            P("tm", None),
            P("tm"),
        ),
        out_specs=P("tm", None, "mod"),
        check_vma=False,
    )
```

```python
import jax
import jax.numpy as jnp
from jax import lax
from jax.experimental import pallas as pl
from jax.experimental.pallas import tpu as pltpu
from jax.sharding import PartitionSpec as P

MRG_FRAME = 64
AUD_TOK = 64
SEQ_DEV = 96


def carried_in(value, axis, join, neutral):
    count, mine = (lax.axis_size(axis), lax.axis_index(axis))
    pieces = lax.all_gather(value, axis)
    running = jnp.full_like(value, 0) + jnp.asarray(neutral, value.dtype)

    def hop(position, running):
        longer = join(running, pieces[position])
        return jnp.where(position < mine, longer, running)

    return lax.fori_loop(0, count - 1, hop, running)


def padded(shard, sides, width):
    for axis, dim in sides:
        peers, length = (lax.axis_size(axis), shard.shape[dim])
        up = [(i, (i + 1) % peers) for i in range(peers - 1)]
        down = [(j, i) for i, j in up]
        last = lax.slice_in_dim(shard, length - width, length, axis=dim)
        first = lax.slice_in_dim(shard, 0, width, axis=dim)
        before = lax.ppermute(last, axis, up)
        after = lax.ppermute(first, axis, down)
        shard = jnp.concatenate([before, shard, after], axis=dim)
    return shard


def layer_norm(values, scale_gain):
    average = jnp.mean(values, axis=-1, keepdims=True)
    centred = values - average
    variance = jnp.mean(centred * centred, axis=-1, keepdims=True)
    return centred * lax.rsqrt(variance + 1e-05) * scale_gain


def rms_norm(values, scale_gain):
    square_mean = jnp.mean(values * values, axis=-1, keepdims=True)
    return values * lax.rsqrt(square_mean + 1e-06) * scale_gain


def pool_pairs(values):
    return values.reshape(-1, 2, values.shape[-1]).mean(axis=1)


def add_counts(earlier, later):
    return earlier + later


def on_device(
    filterbank,
    conv_weight,
    mlp_gain,
    up_weight,
    down_weight,
    post_gain,
    audio_weight,
    patches,
    vision_gain,
    vision_weight,
    retention,
    kept_count,
):
    placed = kept_count + AUD_TOK
    starts = carried_in(placed, "tm", add_counts, jnp.zeros((1,), jnp.int32))
    framed = padded(filterbank, (("tm", 0),), 1)
    unfolded = jnp.concatenate([framed[:-2], framed[1:-1], framed[2:]], axis=1)
    stem = jax.nn.gelu(
        jnp.dot(unfolded, conv_weight, preferred_element_type=jnp.float32), approximate=False
    ).astype(jnp.bfloat16)
    residual = stem.astype(jnp.float32)
    hidden = layer_norm(residual, mlp_gain).astype(jnp.bfloat16)
    up_share = lax.all_gather(up_weight, "tm", axis=0, tiled=True)
    pre_act = jnp.dot(hidden, up_share, preferred_element_type=jnp.float32)
    activated = jax.nn.gelu(pre_act, approximate=False).astype(jnp.bfloat16)
    down_share = lax.all_gather(down_weight, "tm", axis=1, tiled=True)
    partial_value = jnp.dot(activated, down_share, preferred_element_type=jnp.float32)
    pooled_share = lax.psum_scatter(
        pool_pairs(partial_value).astype(jnp.bfloat16), "mod", scatter_dimension=0, tiled=True
    ).astype(jnp.float32)
    share_rows = pooled_share.shape[0]
    own_rows = lax.dynamic_slice_in_dim(
        pool_pairs(residual), lax.axis_index("mod") * share_rows, share_rows, 0
    )
    share_normed = layer_norm(own_rows + pooled_share, post_gain).astype(jnp.bfloat16)
    normed = lax.all_gather(share_normed, "mod", axis=0, tiled=True)
    audio_tokens = jnp.dot(normed, audio_weight, preferred_element_type=jnp.float32).astype(
        jnp.bfloat16
    )
    patch_normed = rms_norm(patches.astype(jnp.float32), vision_gain).astype(jnp.bfloat16)
    merged = patch_normed.reshape(-1, 4 * patch_normed.shape[1])
    vision_share = lax.all_gather(vision_weight, "tm", axis=0, tiled=True)
    visual_tokens = jnp.dot(merged, vision_share, preferred_element_type=jnp.float32).astype(
        jnp.bfloat16
    )
    peer_count = lax.axis_size("tm")
    per_peer = (AUD_TOK + MRG_FRAME + peer_count - 1) // peer_count
    kept_here = kept_count[0]
    first_slot = starts[0]
    all_tokens = jnp.concatenate([visual_tokens, audio_tokens], axis=0)
    peer_ids = jnp.arange(peer_count, dtype=jnp.int32)[:, None]
    round_ids = jnp.arange(per_peer, dtype=jnp.int32)[None, :]
    local_index = round_ids * peer_count + (peer_ids - first_slot) % peer_count
    valid_rows = local_index < kept_here + AUD_TOK
    kept_index = jnp.take(retention[0], jnp.minimum(local_index, MRG_FRAME - 1), axis=0)
    source_index = jnp.where(
        local_index < kept_here, kept_index, MRG_FRAME + local_index - kept_here
    )
    source_index = jnp.where(valid_rows, source_index, 0).astype(jnp.int32)
    send_rows = jnp.take(all_tokens, source_index.reshape(-1), axis=0).reshape(
        peer_count, per_peer, all_tokens.shape[1]
    )
    send_slots = jnp.where(valid_rows, (first_slot + local_index) // peer_count, SEQ_DEV).astype(
        jnp.int32
    )
    recv_rows, recv_slots = (
        lax.all_to_all(send_rows, "tm", split_axis=0, concat_axis=0, tiled=True),
        lax.all_to_all(send_slots, "tm", split_axis=0, concat_axis=0, tiled=True),
    )
    sequence = jnp.zeros((SEQ_DEV, all_tokens.shape[1]), jnp.bfloat16)
    sequence = sequence.at[recv_slots.reshape(-1)].set(
        recv_rows.reshape(-1, all_tokens.shape[1]), mode="drop"
    )
    return sequence[None]


F32, BF16, I32 = jnp.float32, jnp.bfloat16, jnp.int32
MESH = pl.DeviceIdType.MESH
TM, MOD = 8, 4


def iota(shape, dim):
    return lax.broadcasted_iota(I32, shape, dim)


def onehot(mask, value=1.0):
    return jnp.where(mask, value, 0.0).astype(BF16)


def mm(a, b):
    return lax.dot_general(a, b, (((1,), (0,)), ((), ())), preferred_element_type=F32)


def mm_nt(a, b):
    return lax.dot_general(a, b, (((1,), (1,)), ((), ())), preferred_element_type=F32)


def mm_tn(a, b):
    return lax.dot_general(a, b, (((0,), (0,)), ((), ())), preferred_element_type=F32)


ERF_TOP = (
    -2.72614225801306e-10, 2.77068142495902e-08, -2.10102402082508e-06, -5.69250639462346e-05,
    -7.34990630326855e-04, -2.95459980854025e-03, -1.60960333262415e-02,
)
ERF_BOTTOM = (
    -1.45660718464996e-05, -2.13374055278905e-04, -1.68282697438203e-03, -7.37332916720468e-03,
    -1.42647390514189e-02,
)


def polynomial(x, terms):
    value = jnp.full_like(x, terms[0])
    for term in terms[1:]:
        value = value * x + term
    return value


def erf(x):
    x = jnp.clip(x, -4.0, 4.0)
    square = x * x
    return x * polynomial(square, ERF_TOP) / polynomial(square, ERF_BOTTOM)


def gelu(x):
    return 0.5 * x * (1.0 + erf(x * 0.7071067811865476))


FB, META, UPW, DNW, MRG, VIS, TOT, FWD, NRM, HID, COR, XAX = 0, 7, 14, 21, 28, 35, 42, 56, 59, 62, 66, 68
N_SEM = 70
HALF = 640
SHIFTS = (4, 3, 5, 2, 6, 1, 7)


def flipped(index, bits):
    for bit in (1, 2, 4):
        if bits % (2 * bit) >= bit:
            index = index + bit - 2 * bit * ((index // bit) % 2)
    return index


def fused_kernel(
    fb, conv_h, gain1, up, dn, gain2, aud_h, pat_h, gain_v, vis_h, ret, kept, out,
    conv, aud_w, pat, vis_w, fbp, meta, w_s, w_r, m_s, x_r, v_s, v_r, pre, w_all, stem, hid, pa, own,
    a_s, a_r, b_s, b_r, c_s, c_r, nrm, load_sem, send_sem, recv_sem,
):
    me = lax.axis_index("tm")
    mo = lax.axis_index("mod")
    xx, cc = mo // 2, mo % 2
    tm_peers = [lax.rem(me + d, TM) for d in SHIFTS]
    tm_sources = [lax.rem(me + TM - d, TM) for d in SHIFTS]
    mod_peers = [flipped(mo, bits) for bits in (2, 3, 1)]
    x_peer, core_peer = mod_peers[0], mod_peers[2]

    barrier = pltpu.get_barrier_semaphore()
    for peer in tm_peers:
        pl.semaphore_signal(barrier, inc=1, device_id={"tm": peer}, device_id_type=MESH)
    for peer in mod_peers:
        pl.semaphore_signal(barrier, inc=1, device_id={"mod": peer}, device_id_type=MESH)

    quarter = pl.ds(pl.multiple_of(mo * 64, 64), 64)
    loads = [
        pltpu.make_async_copy(src, dst, load_sem.at[i])
        for i, (src, dst) in enumerate(
            [(pat_h.at[quarter], pat), (conv_h, conv), (vis_h, vis_w), (aud_h, aud_w)]
        )
    ]
    for c in loads:
        c.start()

    sent = []

    def describe(src, dst, slot, to):
        return pltpu.make_async_remote_copy(
            src_ref=src, dst_ref=dst, send_sem=send_sem.at[slot], recv_sem=recv_sem.at[slot],
            device_id=to, device_id_type=MESH,
        )

    def copy(src, dst, slot, to):
        c = describe(src, dst, slot, to)
        c.start()
        sent.append(c)
        return c

    def to_tm(src_of, dst, base):
        return [copy(src_of(p), dst, base + d, {"tm": p}) for d, p in enumerate(tm_peers)]

    def arrive(copies):
        for c in copies:
            c.wait_recv()

    fbp[0:16] = jnp.zeros((16, 128), BF16)
    fbp[1040:1056] = jnp.zeros((16, 128), BF16)
    my_rows = pl.ds(pl.multiple_of(16 + me * 128, 16), 128)
    fbp[my_rows, :] = fb[...]
    hit = onehot(ret[...] == iota((128, 64), 0) % 64)
    inv = mm_nt(iota((8, 64), 1).astype(F32).astype(BF16), hit)
    kept_f = jnp.full((8, 128), kept[0], I32).astype(F32)
    inv = jnp.where(inv < kept_f, inv, -4096.0)
    meta[me] = jnp.where(iota((8, 128), 0) == 0, inv, kept_f)

    row, col = iota((512, 128), 0), iota((512, 128), 1)
    for t in range(TM):
        w_s[t, 0:160] = up[:, 128 * t : 128 * t + 128]
        w_s[t, 240:400] = dn[:, 128 * t : 128 * t + 128]
    picks = [onehot((row // 128 == col // 32) & (row % 128 == 32 * a + col % 32)) for a in range(4)]
    for g in range(2):
        lanes = slice(1024 + 128 * g, 1152 + 128 * g)
        rest = jnp.concatenate(
            [up[0:80, lanes], up[80:160, lanes], dn[0:80, lanes], dn[80:160, lanes]], axis=1
        )
        for a in range(4):
            w_s[4 * g + a, 160:240] = mm(rest, picks[a]).astype(BF16)
    w_r[me] = w_s[me]

    def frames(d, p, source):
        first = 112 * (source % 2)
        edge = pl.ds(pl.multiple_of(first, 16), 16)
        there = pl.ds(pl.multiple_of(16 + source * 128 + first, 16), 16)
        whole = pl.ds(pl.multiple_of(16 + source * 128, 16), 128)
        return [
            pltpu.make_async_remote_copy(
                src_ref=src, dst_ref=dst, send_sem=send_sem.at[FB + d], recv_sem=recv_sem.at[FB + d],
                device_id={"tm": p}, device_id_type=MESH,
            )
            for src, dst in ((fb, fbp.at[whole]), (fb.at[edge], fbp.at[there]))
        ]

    def both_ways(source, act):
        here = (source // 2) % 2 == cc
        pl.when(here)(lambda: act(0))
        pl.when(jnp.logical_not(here))(lambda: act(1))

    fb_out = [frames(d, p, me) for d, p in enumerate(tm_peers)]
    fb_in = [frames(d, p, p) for d, p in enumerate(tm_sources)]
    pl.semaphore_wait(barrier, TM + MOD - 2)
    both_ways(me, lambda i: [c[i].start() for c in fb_out] and None)
    up_rows, dn_rows = pl.ds(0, 240), pl.ds(240, 160)
    u_copies = to_tm(lambda p: w_s.at[p, up_rows], w_r.at[me, up_rows], UPW)
    meta_copies = to_tm(lambda p: meta.at[me], meta.at[me], META)

    loads[0].wait()
    pv = pat[...].astype(F32)
    ms = jnp.sum(pv * pv, axis=1, keepdims=True) * (1.0 / 1280.0)
    pn = (pv * lax.rsqrt(ms + 1e-06) * gain_v[...][None, :]).astype(BF16)
    r64, c64 = iota((64, 64), 0), iota((64, 64), 1)
    pn = mm(onehot(c64 == 4 * (r64 % 16) + r64 // 16), pn).astype(BF16)
    for t in range(TM):
        q, h = t // 2, t % 2
        m_s[t] = pn[16 * q : 16 * q + 16, HALF * h : HALF * h + HALF]
    m_copies = to_tm(lambda p: m_s.at[p], x_r.at[me, mo], MRG)
    x_r[me, mo] = m_s[me]
    d_copies = to_tm(lambda p: w_s.at[p, dn_rows], w_r.at[me, dn_rows], DNW)

    loads[1].wait()
    for d, p in enumerate(tm_sources):
        both_ways(p, lambda i: fb_in[d][i].wait_recv())

    def span_of(k):
        x_at = (1 - xx) + (k // 2) * (2 * xx - 1)
        return 2 * (2 * x_at + cc) + k % 2

    def hidden_rows(k):
        rows = pl.ds(pl.multiple_of(span_of(k) * 128, 128), 128)
        return describe(hid.at[rows], hid.at[rows], HID + k, {"mod": core_peer})

    x_copies = [
        describe(x_r.at[:, mo], x_r.at[:, mo], FWD + d, {"mod": p})
        for d, p in enumerate((x_peer, core_peer))
    ]

    gain_row = gain1[...][None, :]

    def stem_step(k, carry):
        base = pl.multiple_of(span_of(k) * 128, 128)
        rows = fbp[pl.ds(base, 160), :].astype(F32)
        taps = jnp.concatenate([rows[15:143], rows[16:144], rows[17:145]], axis=1).astype(BF16)
        pre[...] = mm(taps, conv[...])

        def piece(i, carry):
            at = pl.multiple_of(i * 32, 32)
            st = gelu(pre[pl.ds(at, 32), :]).astype(BF16)
            there = pl.ds(pl.multiple_of(base + at, 32), 32)
            stem[there, :] = st
            v = st.astype(F32)
            v = v - jnp.sum(v, axis=1, keepdims=True) * (1.0 / 1280.0)
            var = jnp.sum(v * v, axis=1, keepdims=True) * (1.0 / 1280.0)
            hid[there, :] = (v * lax.rsqrt(var + 1e-05) * gain_row).astype(BF16)
            return carry

        lax.fori_loop(0, 4, piece, 0)
        hidden_rows(k).start()

        @pl.when(k == 1)
        def _():
            arrive(m_copies)
            for c in x_copies:
                c.start()

        return carry

    lax.fori_loop(0, 4, stem_step, 0)
    h_copies = [hidden_rows(k) for k in range(4)]
    sent.extend(h_copies + x_copies)
    x_copies[0].wait_recv()
    x_copies.append(copy(x_r.at[:, x_peer], x_r.at[:, x_peer], FWD + 2, {"mod": core_peer}))

    arrive(meta_copies)
    ends, before, running = [], [], jnp.zeros((1, 128), F32)
    for s in range(TM):
        before.append(running)
        running = running + meta[s, 1:2, :]
        ends.append(running.astype(I32))

    def ends_of(pair):
        picked = []
        for h in range(2):
            e = ends[h]
            for p in range(1, MOD):
                e = jnp.where(pair == p, ends[2 * p + h], e)
            picked.append(e)
        return picked

    def pool_rows(holder, r_s2, r_q, frames, span_ends):
        blocks = []
        for h in range(2):
            j = 8 * r_q + ((holder - span_ends[h]) & 7)
            blocks.append(onehot((r_s2 == h) & (frames // 2 == j), 0.5))
        return jnp.concatenate(blocks, axis=1)

    arrive(u_copies)
    rem = jnp.concatenate([w_r[t, 160:240] for t in range(TM)], axis=0)
    ri, ci = iota((128, 512), 0), iota((128, 512), 1)
    rem = mm(rem, onehot((ci % 128 < 32) & (ri == 32 * (ci // 128) + ci % 128))).astype(BF16)

    def assemble(first, lane):
        main = jnp.concatenate([w_r[t, first : first + 160] for t in range(TM)], axis=0)
        parts = []
        for t in range(TM):
            parts.append(rem[80 * t : 80 * t + 80, lane : lane + 128])
            parts.append(rem[80 * t : 80 * t + 80, lane + 128 : lane + 256])
        return jnp.concatenate([main, jnp.concatenate(parts, axis=0)], axis=1)

    w_all[...] = assemble(0, 0)
    r128, c128 = iota((128, 128), 0), iota((128, 128), 1)

    def feed(step, carry):
        k = lax.rem(2 + 2 * step + step // 2, 4)
        core = (1 - cc) + (k // 2) * (2 * cc - 1)
        x_at = (1 - xx) + (k % 2) * (2 * xx - 1)
        pl.when(step == 1)(lambda: arrive(h_copies[0:2]))
        pl.when(step == 3)(lambda: arrive(h_copies[2:4]))
        pair = 2 * x_at + core
        rows = pl.ds(pl.multiple_of(pair * 256, 256), 256)
        act = gelu(mm(hid[rows, :], w_all[...])).astype(BF16)
        pool = pool_rows(r128 // 16, (r128 // 8) % 2, r128 % 8, c128, ends_of(pair))
        pa[k] = mm(pool, act).astype(BF16)
        return carry

    lax.fori_loop(0, 4, feed, 0)

    arrive(x_copies[1:])
    lane = iota((1, 128), 1)
    pos = jnp.concatenate(
        [
            jnp.where(lane < 64, meta[t, 0:1, :] + before[t], meta[t + 1, 0:1, :] + before[t + 1])
            for t in range(0, TM, 2)
        ],
        axis=1,
    ).astype(I32)
    r256 = iota((256, 512), 0)
    pick = onehot(pos == 8 * (r256 % 32) + r256 // 32)
    chosen = mm(pick, x_r[...].reshape(512, HALF)).astype(BF16)
    loads[2].wait()
    v_s[...] = mm_nt(chosen, vis_w[...]).astype(BF16).reshape(TM, 32, 448)
    v_copies = to_tm(lambda p: v_s.at[p], v_r.at[me], VIS)
    v_r[me] = v_s[me]

    arrive(d_copies)
    w_all[...] = assemble(240, 256)

    def core_sum(h):
        return describe(a_s.at[h], a_r.at[h], COR + h, {"mod": core_peer})

    def x_sum(h):
        return describe(b_s.at[h], b_r.at[h], XAX + h, {"mod": x_peer})

    def product_half(h, carry):
        cols = pl.ds(pl.multiple_of(h * HALF, HALF), HALF)
        product = mm_nt(pa[...].reshape(512, 256), w_all[cols, :])
        a_s[h] = product[0:256].astype(BF16)
        core_sum(h).start()
        own[h] = product[256:512]
        return carry

    lax.fori_loop(0, 2, product_half, 0)

    def x_half(h, carry):
        core_sum(h).wait_recv()
        b_s[h] = (own[h, 0:128] + a_r[h, 0:128].astype(F32)).astype(BF16)
        x_sum(h).start()
        return carry

    lax.fori_loop(0, 2, x_half, 0)
    b_copies = [x_sum(h) for h in range(2)]
    sent.extend([core_sum(h) for h in range(2)] + b_copies)
    c_copies = []

    r16, c16 = iota((16, 128), 0), iota((16, 128), 1)
    pool = pool_rows(me, r16 // 8, r16 % 8, c16, ends_of(mo))
    pooled = mm(pool, stem[pl.ds(pl.multiple_of(mo * 256, 256), 256), :])
    g = 8 * lane + me
    v_slot = lane
    a_slot = jnp.zeros((1, 128), I32)
    for s in range(TM):
        v_slot = v_slot + jnp.where(ends[s] <= g, 8, 0)
        j = 8 * (lane % 8) + ((me - ends[s]) & 7)
        a_slot = jnp.where((lane - 32) // 8 == s, ((ends[s] + j) >> 3) + 8 * s, a_slot)
    slot = jnp.where(lane < 32, v_slot, jnp.where(lane < 96, a_slot, -1))
    place = onehot(slot == iota((96, 128), 0))

    for h in range(2):
        total = own[h, 128:256] + a_r[h, 128:256].astype(F32)
        b_copies[h].wait_recv()
        total = total + b_r[h].astype(F32)
        c_s[h] = total.astype(BF16).reshape(TM, 16, HALF)
        c_copies.append(to_tm(lambda p: c_s.at[h, p], c_r.at[h, me], TOT + 7 * h))
        c_r[h, me] = c_s[h, me]

    arrive(v_copies)
    visual = v_r[0].astype(F32)
    for t in range(1, TM):
        visual = visual + v_r[t].astype(F32)

    halves = []
    for h in range(2):
        arrive(c_copies[h])
        part = pooled[:, HALF * h : HALF * h + HALF]
        for t in range(TM):
            part = part + c_r[h, t].astype(F32)
        halves.append(part)
    pooled = jnp.concatenate(halves, axis=1)
    v = pooled - jnp.sum(pooled, axis=1, keepdims=True) * (1.0 / 1280.0)
    var = jnp.sum(v * v, axis=1, keepdims=True) * (1.0 / 1280.0)
    nrm[mo] = (v * lax.rsqrt(var + 1e-05) * gain2[...][None, :]).astype(BF16)
    n_copies = [copy(nrm.at[mo], nrm.at[mo], NRM + d, {"mod": p}) for d, p in enumerate(mod_peers)]
    loads[3].wait()
    arrive(n_copies)
    audio = mm_nt(nrm[...].reshape(64, 1280), aud_w[...])
    tokens = jnp.concatenate(
        [visual.astype(BF16), audio.astype(BF16), jnp.zeros((32, 448), BF16)], axis=0
    )
    out[...] = mm(place, tokens).astype(BF16)

    for c in sent:
        c.wait_send()
    both_ways(me, lambda i: [c[i].wait_send() for c in fb_out] and None)


def on_device_fused(
    filterbank, conv_weight, mlp_gain, up_weight, down_weight, post_gain, audio_weight,
    patches, vision_gain, vision_weight, retention, kept_count,
):
    vm = pl.BlockSpec(memory_space=pltpu.VMEM)
    far = pl.BlockSpec(memory_space=pl.ANY)
    n_out = vision_weight.shape[1]
    scratch = [
        pltpu.VMEM(conv_weight.shape, BF16),
        pltpu.VMEM((n_out, 1280), BF16),
        pltpu.VMEM((64, 1280), BF16),
        pltpu.VMEM((n_out, HALF), BF16),
        pltpu.VMEM((1056, 128), BF16),
        pltpu.VMEM((TM, 8, 128), F32),
        pltpu.VMEM((TM, 400, 128), BF16),
        pltpu.VMEM((TM, 400, 128), BF16),
        pltpu.VMEM((TM, 16, HALF), BF16),
        pltpu.VMEM((TM, MOD, 16, HALF), BF16),
        pltpu.VMEM((TM, 32, n_out), BF16),
        pltpu.VMEM((TM, 32, n_out), BF16),
        pltpu.VMEM((128, 1280), F32),
        pltpu.VMEM((1280, 256), BF16),
        pltpu.VMEM((1024, 1280), BF16),
        pltpu.VMEM((1024, 1280), BF16),
        pltpu.VMEM((MOD, 128, 256), BF16),
        pltpu.VMEM((2, 256, HALF), F32),
        pltpu.VMEM((2, 256, HALF), BF16),
        pltpu.VMEM((2, 256, HALF), BF16),
        pltpu.VMEM((2, 128, HALF), BF16),
        pltpu.VMEM((2, 128, HALF), BF16),
        pltpu.VMEM((2, TM, 16, HALF), BF16),
        pltpu.VMEM((2, TM, 16, HALF), BF16),
        pltpu.VMEM((MOD, 16, 1280), BF16),
        pltpu.SemaphoreType.DMA((4,)),
        pltpu.SemaphoreType.DMA((N_SEM,)),
        pltpu.SemaphoreType.DMA((N_SEM,)),
    ]
    sequence = pl.pallas_call(
        fused_kernel,
        out_shape=jax.ShapeDtypeStruct((SEQ_DEV, vision_weight.shape[1]), BF16),
        in_specs=[vm, far, vm, vm, vm, vm, far, far, vm, far, vm, pl.BlockSpec(memory_space=pltpu.SMEM)],
        out_specs=vm,
        scratch_shapes=scratch,
        compiler_params=pltpu.CompilerParams(
            collective_id=0, has_side_effects=True, vmem_limit_bytes=56 * 1024 * 1024
        ),
    )(
        filterbank, conv_weight, mlp_gain, up_weight, down_weight.T, post_gain,
        audio_weight.T, patches, vision_gain, vision_weight.T, retention, kept_count,
    )
    return sequence[None]


def solution(mesh):
    fused = mesh.shape["tm"] == TM and mesh.shape["mod"] == MOD
    return jax.shard_map(
        on_device_fused if fused else on_device,
        mesh=mesh,
        in_specs=(
            P("tm", None),
            P(),
            P(),
            P("tm", "mod"),
            P("mod", "tm"),
            P(),
            P(None, "mod"),
            P("tm", None),
            P(),
            P("tm", "mod"),
            P("tm", None),
            P("tm"),
        ),
        out_specs=P("tm", None, "mod"),
        check_vma=False,
    )
```

```python
import jax
import jax.numpy as jnp
from jax import lax
from jax.experimental import pallas as pl
from jax.experimental.pallas import tpu as pltpu
from jax.sharding import PartitionSpec as P

MRG_FRAME = 64
AUD_TOK = 64
SEQ_DEV = 96


def carried_in(value, axis, join, neutral):
    count, mine = (lax.axis_size(axis), lax.axis_index(axis))
    pieces = lax.all_gather(value, axis)
    running = jnp.full_like(value, 0) + jnp.asarray(neutral, value.dtype)

    def hop(position, running):
        longer = join(running, pieces[position])
        return jnp.where(position < mine, longer, running)

    return lax.fori_loop(0, count - 1, hop, running)


def padded(shard, sides, width):
    for axis, dim in sides:
        peers, length = (lax.axis_size(axis), shard.shape[dim])
        up = [(i, (i + 1) % peers) for i in range(peers - 1)]
        down = [(j, i) for i, j in up]
        last = lax.slice_in_dim(shard, length - width, length, axis=dim)
        first = lax.slice_in_dim(shard, 0, width, axis=dim)
        before = lax.ppermute(last, axis, up)
        after = lax.ppermute(first, axis, down)
        shard = jnp.concatenate([before, shard, after], axis=dim)
    return shard


def layer_norm(values, scale_gain):
    average = jnp.mean(values, axis=-1, keepdims=True)
    centred = values - average
    variance = jnp.mean(centred * centred, axis=-1, keepdims=True)
    return centred * lax.rsqrt(variance + 1e-05) * scale_gain


def rms_norm(values, scale_gain):
    square_mean = jnp.mean(values * values, axis=-1, keepdims=True)
    return values * lax.rsqrt(square_mean + 1e-06) * scale_gain


def pool_pairs(values):
    return values.reshape(-1, 2, values.shape[-1]).mean(axis=1)


def add_counts(earlier, later):
    return earlier + later


def on_device(
    filterbank,
    conv_weight,
    mlp_gain,
    up_weight,
    down_weight,
    post_gain,
    audio_weight,
    patches,
    vision_gain,
    vision_weight,
    retention,
    kept_count,
):
    placed = kept_count + AUD_TOK
    starts = carried_in(placed, "tm", add_counts, jnp.zeros((1,), jnp.int32))
    framed = padded(filterbank, (("tm", 0),), 1)
    unfolded = jnp.concatenate([framed[:-2], framed[1:-1], framed[2:]], axis=1)
    stem = jax.nn.gelu(
        jnp.dot(unfolded, conv_weight, preferred_element_type=jnp.float32), approximate=False
    ).astype(jnp.bfloat16)
    residual = stem.astype(jnp.float32)
    hidden = layer_norm(residual, mlp_gain).astype(jnp.bfloat16)
    up_share = lax.all_gather(up_weight, "tm", axis=0, tiled=True)
    pre_act = jnp.dot(hidden, up_share, preferred_element_type=jnp.float32)
    activated = jax.nn.gelu(pre_act, approximate=False).astype(jnp.bfloat16)
    down_share = lax.all_gather(down_weight, "tm", axis=1, tiled=True)
    partial_value = jnp.dot(activated, down_share, preferred_element_type=jnp.float32)
    pooled_share = lax.psum_scatter(
        pool_pairs(partial_value).astype(jnp.bfloat16), "mod", scatter_dimension=0, tiled=True
    ).astype(jnp.float32)
    share_rows = pooled_share.shape[0]
    own_rows = lax.dynamic_slice_in_dim(
        pool_pairs(residual), lax.axis_index("mod") * share_rows, share_rows, 0
    )
    share_normed = layer_norm(own_rows + pooled_share, post_gain).astype(jnp.bfloat16)
    normed = lax.all_gather(share_normed, "mod", axis=0, tiled=True)
    audio_tokens = jnp.dot(normed, audio_weight, preferred_element_type=jnp.float32).astype(
        jnp.bfloat16
    )
    patch_normed = rms_norm(patches.astype(jnp.float32), vision_gain).astype(jnp.bfloat16)
    merged = patch_normed.reshape(-1, 4 * patch_normed.shape[1])
    vision_share = lax.all_gather(vision_weight, "tm", axis=0, tiled=True)
    visual_tokens = jnp.dot(merged, vision_share, preferred_element_type=jnp.float32).astype(
        jnp.bfloat16
    )
    peer_count = lax.axis_size("tm")
    per_peer = (AUD_TOK + MRG_FRAME + peer_count - 1) // peer_count
    kept_here = kept_count[0]
    first_slot = starts[0]
    all_tokens = jnp.concatenate([visual_tokens, audio_tokens], axis=0)
    peer_ids = jnp.arange(peer_count, dtype=jnp.int32)[:, None]
    round_ids = jnp.arange(per_peer, dtype=jnp.int32)[None, :]
    local_index = round_ids * peer_count + (peer_ids - first_slot) % peer_count
    valid_rows = local_index < kept_here + AUD_TOK
    kept_index = jnp.take(retention[0], jnp.minimum(local_index, MRG_FRAME - 1), axis=0)
    source_index = jnp.where(
        local_index < kept_here, kept_index, MRG_FRAME + local_index - kept_here
    )
    source_index = jnp.where(valid_rows, source_index, 0).astype(jnp.int32)
    send_rows = jnp.take(all_tokens, source_index.reshape(-1), axis=0).reshape(
        peer_count, per_peer, all_tokens.shape[1]
    )
    send_slots = jnp.where(valid_rows, (first_slot + local_index) // peer_count, SEQ_DEV).astype(
        jnp.int32
    )
    recv_rows, recv_slots = (
        lax.all_to_all(send_rows, "tm", split_axis=0, concat_axis=0, tiled=True),
        lax.all_to_all(send_slots, "tm", split_axis=0, concat_axis=0, tiled=True),
    )
    sequence = jnp.zeros((SEQ_DEV, all_tokens.shape[1]), jnp.bfloat16)
    sequence = sequence.at[recv_slots.reshape(-1)].set(
        recv_rows.reshape(-1, all_tokens.shape[1]), mode="drop"
    )
    return sequence[None]


F32, BF16, I32 = jnp.float32, jnp.bfloat16, jnp.int32
MESH = pl.DeviceIdType.MESH
TM, MOD = 8, 4


def iota(shape, dim):
    return lax.broadcasted_iota(I32, shape, dim)


def onehot(mask, value=1.0):
    return jnp.where(mask, value, 0.0).astype(BF16)


def mm(a, b):
    return lax.dot_general(a, b, (((1,), (0,)), ((), ())), preferred_element_type=F32)


def mm_nt(a, b):
    return lax.dot_general(a, b, (((1,), (1,)), ((), ())), preferred_element_type=F32)


def mm_tn(a, b):
    return lax.dot_general(a, b, (((0,), (0,)), ((), ())), preferred_element_type=F32)


def gelu(x):
    return 0.5 * x * (1.0 + lax.erf(x * 0.7071067811865476))


FB, META, UPW, DNW, MRG, VIS, TOT, FWD, NRM, HID, COR, XAX = 0, 7, 14, 21, 28, 35, 42, 77, 80, 83, 87, 92
N_SEM = 97
CHUNKS, WIDE = 5, 256
HALF = 640
SHIFTS = (4, 3, 5, 2, 6, 1, 7)


def flipped(index, bits):
    for bit in (1, 2, 4):
        if bits % (2 * bit) >= bit:
            index = index + bit - 2 * bit * ((index // bit) % 2)
    return index


def fused_kernel(
    fb, conv_h, gain1, up, dn, gain2, aud_h, pat_h, gain_v, vis_h, ret, kept, out,
    conv, aud_w, pat, vis_w, fbp, meta, w_s, w_r, m_s, x_r, v_s, v_r, pre, w_all, stem, hid, pa, own,
    a_s, a_r, b_s, b_r, c_s, c_r, nrm, load_sem, send_sem, recv_sem,
):
    me = lax.axis_index("tm")
    mo = lax.axis_index("mod")
    xx, cc = mo // 2, mo % 2
    tm_peers = [lax.rem(me + d, TM) for d in SHIFTS]
    tm_sources = [lax.rem(me + TM - d, TM) for d in SHIFTS]
    mod_peers = [flipped(mo, bits) for bits in (2, 3, 1)]
    x_peer, core_peer = mod_peers[0], mod_peers[2]

    barrier = pltpu.get_barrier_semaphore()
    for peer in tm_peers:
        pl.semaphore_signal(barrier, inc=1, device_id={"tm": peer}, device_id_type=MESH)
    for peer in mod_peers:
        pl.semaphore_signal(barrier, inc=1, device_id={"mod": peer}, device_id_type=MESH)

    quarter = pl.ds(pl.multiple_of(mo * 64, 64), 64)
    loads = [
        pltpu.make_async_copy(src, dst, load_sem.at[i])
        for i, (src, dst) in enumerate(
            [(pat_h.at[quarter], pat), (conv_h, conv), (vis_h, vis_w), (aud_h, aud_w)]
        )
    ]
    for c in loads:
        c.start()

    sent = []

    def describe(src, dst, slot, to):
        return pltpu.make_async_remote_copy(
            src_ref=src, dst_ref=dst, send_sem=send_sem.at[slot], recv_sem=recv_sem.at[slot],
            device_id=to, device_id_type=MESH,
        )

    def copy(src, dst, slot, to):
        c = describe(src, dst, slot, to)
        c.start()
        sent.append(c)
        return c

    def to_tm(src_of, dst, base):
        return [copy(src_of(p), dst, base + d, {"tm": p}) for d, p in enumerate(tm_peers)]

    def arrive(copies):
        for c in copies:
            c.wait_recv()

    fbp[0:16] = jnp.zeros((16, 128), BF16)
    fbp[1040:1056] = jnp.zeros((16, 128), BF16)
    my_rows = pl.ds(pl.multiple_of(16 + me * 128, 16), 128)
    fbp[my_rows, :] = fb[...]
    hit = onehot(ret[...] == iota((128, 64), 0) % 64)
    inv = mm_nt(iota((8, 64), 1).astype(F32).astype(BF16), hit)
    kept_f = jnp.full((8, 128), kept[0], I32).astype(F32)
    inv = jnp.where(inv < kept_f, inv, -4096.0)
    meta[me] = jnp.where(iota((8, 128), 0) == 0, inv, kept_f)

    row, col = iota((512, 128), 0), iota((512, 128), 1)
    for t in range(TM):
        w_s[t, 0:160] = up[:, 128 * t : 128 * t + 128]
        w_s[t, 240:400] = dn[:, 128 * t : 128 * t + 128]
    picks = [onehot((row // 128 == col // 32) & (row % 128 == 32 * a + col % 32)) for a in range(4)]
    for g in range(2):
        lanes = slice(1024 + 128 * g, 1152 + 128 * g)
        rest = jnp.concatenate(
            [up[0:80, lanes], up[80:160, lanes], dn[0:80, lanes], dn[80:160, lanes]], axis=1
        )
        for a in range(4):
            w_s[4 * g + a, 160:240] = mm(rest, picks[a]).astype(BF16)
    w_r[me] = w_s[me]

    def frames(d, p, source):
        first = 112 * (source % 2)
        edge = pl.ds(pl.multiple_of(first, 16), 16)
        there = pl.ds(pl.multiple_of(16 + source * 128 + first, 16), 16)
        whole = pl.ds(pl.multiple_of(16 + source * 128, 16), 128)
        return [
            pltpu.make_async_remote_copy(
                src_ref=src, dst_ref=dst, send_sem=send_sem.at[FB + d], recv_sem=recv_sem.at[FB + d],
                device_id={"tm": p}, device_id_type=MESH,
            )
            for src, dst in ((fb, fbp.at[whole]), (fb.at[edge], fbp.at[there]))
        ]

    def both_ways(source, act):
        here = (source // 2) % 2 == cc
        pl.when(here)(lambda: act(0))
        pl.when(jnp.logical_not(here))(lambda: act(1))

    fb_out = [frames(d, p, me) for d, p in enumerate(tm_peers)]
    fb_in = [frames(d, p, p) for d, p in enumerate(tm_sources)]
    pl.semaphore_wait(barrier, TM + MOD - 2)
    both_ways(me, lambda i: [c[i].start() for c in fb_out] and None)
    up_rows, dn_rows = pl.ds(0, 240), pl.ds(240, 160)
    u_copies = to_tm(lambda p: w_s.at[p, up_rows], w_r.at[me, up_rows], UPW)
    meta_copies = to_tm(lambda p: meta.at[me], meta.at[me], META)

    loads[0].wait()
    pv = pat[...].astype(F32)
    ms = jnp.sum(pv * pv, axis=1, keepdims=True) * (1.0 / 1280.0)
    pn = (pv * lax.rsqrt(ms + 1e-06) * gain_v[...][None, :]).astype(BF16)
    r64, c64 = iota((64, 64), 0), iota((64, 64), 1)
    pn = mm(onehot(c64 == 4 * (r64 % 16) + r64 // 16), pn).astype(BF16)
    for t in range(TM):
        q, h = t // 2, t % 2
        m_s[t] = pn[16 * q : 16 * q + 16, HALF * h : HALF * h + HALF]
    m_copies = to_tm(lambda p: m_s.at[p], x_r.at[me, mo], MRG)
    x_r[me, mo] = m_s[me]
    d_copies = to_tm(lambda p: w_s.at[p, dn_rows], w_r.at[me, dn_rows], DNW)

    loads[1].wait()
    for d, p in enumerate(tm_sources):
        both_ways(p, lambda i: fb_in[d][i].wait_recv())

    def span_of(k):
        x_at = (1 - xx) + (k // 2) * (2 * xx - 1)
        return 2 * (2 * x_at + cc) + k % 2

    def hidden_rows(k):
        rows = pl.ds(pl.multiple_of(span_of(k) * 128, 128), 128)
        return describe(hid.at[rows], hid.at[rows], HID + k, {"mod": core_peer})

    x_copies = [
        describe(x_r.at[:, mo], x_r.at[:, mo], FWD + d, {"mod": p})
        for d, p in enumerate((x_peer, core_peer))
    ]

    def stem_step(k, carry):
        base = pl.multiple_of(span_of(k) * 128, 128)
        rows = fbp[pl.ds(base, 160), :].astype(F32)
        taps = jnp.concatenate([rows[15:143], rows[16:144], rows[17:145]], axis=1).astype(BF16)
        pre[...] = mm(taps, conv[...])

        def piece(i, carry):
            at = pl.multiple_of(i * 32, 32)
            st = gelu(pre[pl.ds(at, 32), :]).astype(BF16)
            there = pl.ds(pl.multiple_of(base + at, 32), 32)
            stem[there, :] = st
            v = st.astype(F32)
            v = v - jnp.sum(v, axis=1, keepdims=True) * (1.0 / 1280.0)
            var = jnp.sum(v * v, axis=1, keepdims=True) * (1.0 / 1280.0)
            hid[there, :] = (v * lax.rsqrt(var + 1e-05) * gain1[...][None, :]).astype(BF16)
            return carry

        lax.fori_loop(0, 4, piece, 0)
        hidden_rows(k).start()

        @pl.when(k == 1)
        def _():
            arrive(m_copies)
            for c in x_copies:
                c.start()

        return carry

    lax.fori_loop(0, 4, stem_step, 0)
    h_copies = [hidden_rows(k) for k in range(4)]
    sent.extend(h_copies + x_copies)
    x_copies[0].wait_recv()
    x_copies.append(copy(x_r.at[:, x_peer], x_r.at[:, x_peer], FWD + 2, {"mod": core_peer}))

    arrive(meta_copies)
    ends, before, running = [], [], jnp.zeros((1, 128), F32)
    for s in range(TM):
        before.append(running)
        running = running + meta[s, 1:2, :]
        ends.append(running.astype(I32))

    def ends_of(pair):
        picked = []
        for h in range(2):
            e = ends[h]
            for p in range(1, MOD):
                e = jnp.where(pair == p, ends[2 * p + h], e)
            picked.append(e)
        return picked

    def pool_rows(holder, r_s2, r_q, frames, span_ends):
        blocks = []
        for h in range(2):
            j = 8 * r_q + ((holder - span_ends[h]) & 7)
            blocks.append(onehot((r_s2 == h) & (frames // 2 == j), 0.5))
        return jnp.concatenate(blocks, axis=1)

    arrive(u_copies)
    rem = jnp.concatenate([w_r[t, 160:240] for t in range(TM)], axis=0)
    ri, ci = iota((128, 512), 0), iota((128, 512), 1)
    rem = mm(rem, onehot((ci % 128 < 32) & (ri == 32 * (ci // 128) + ci % 128))).astype(BF16)

    def assemble(first, lane):
        main = jnp.concatenate([w_r[t, first : first + 160] for t in range(TM)], axis=0)
        parts = []
        for t in range(TM):
            parts.append(rem[80 * t : 80 * t + 80, lane : lane + 128])
            parts.append(rem[80 * t : 80 * t + 80, lane + 128 : lane + 256])
        return jnp.concatenate([main, jnp.concatenate(parts, axis=0)], axis=1)

    w_all[...] = assemble(0, 0)
    r128, c128 = iota((128, 128), 0), iota((128, 128), 1)

    def feed(step, carry):
        k = lax.rem(2 + 2 * step + step // 2, 4)
        core = (1 - cc) + (k // 2) * (2 * cc - 1)
        x_at = (1 - xx) + (k % 2) * (2 * xx - 1)
        pl.when(step == 1)(lambda: arrive(h_copies[0:2]))
        pl.when(step == 3)(lambda: arrive(h_copies[2:4]))
        pair = 2 * x_at + core
        rows = pl.ds(pl.multiple_of(pair * 256, 256), 256)
        act = gelu(mm(hid[rows, :], w_all[...])).astype(BF16)
        pool = pool_rows(r128 // 16, (r128 // 8) % 2, r128 % 8, c128, ends_of(pair))
        pa[k] = mm(pool, act).astype(BF16)
        return carry

    lax.fori_loop(0, 4, feed, 0)

    arrive(x_copies[1:])
    lane = iota((1, 128), 1)
    pos = jnp.concatenate(
        [
            jnp.where(lane < 64, meta[t, 0:1, :] + before[t], meta[t + 1, 0:1, :] + before[t + 1])
            for t in range(0, TM, 2)
        ],
        axis=1,
    ).astype(I32)
    r256 = iota((256, 512), 0)
    pick = onehot(pos == 8 * (r256 % 32) + r256 // 32)
    chosen = mm(pick, x_r[...].reshape(512, HALF)).astype(BF16)
    loads[2].wait()
    v_s[...] = mm_nt(chosen, vis_w[...]).astype(BF16).reshape(TM, 32, 448)
    v_copies = to_tm(lambda p: v_s.at[p], v_r.at[me], VIS)
    v_r[me] = v_s[me]

    arrive(d_copies)
    w_all[...] = assemble(240, 256)

    def core_sum(h):
        return describe(a_s.at[h], a_r.at[h], COR + h, {"mod": core_peer})

    def x_sum(h):
        return describe(b_s.at[h], b_r.at[h], XAX + h, {"mod": x_peer})

    def product_half(h, carry):
        cols = pl.ds(pl.multiple_of(h * WIDE, WIDE), WIDE)
        product = mm_nt(pa[...].reshape(512, 256), w_all[cols, :])
        a_s[h] = product[0:256].astype(BF16)
        core_sum(h).start()
        own[h] = product[256:512]
        return carry

    lax.fori_loop(0, CHUNKS, product_half, 0)

    def x_half(h, carry):
        core_sum(h).wait_recv()
        b_s[h] = (own[h, 0:128] + a_r[h, 0:128].astype(F32)).astype(BF16)
        x_sum(h).start()
        return carry

    lax.fori_loop(0, CHUNKS, x_half, 0)
    b_copies = [x_sum(h) for h in range(CHUNKS)]
    sent.extend([core_sum(h) for h in range(CHUNKS)] + b_copies)
    c_copies = []

    r16, c16 = iota((16, 128), 0), iota((16, 128), 1)
    pool = pool_rows(me, r16 // 8, r16 % 8, c16, ends_of(mo))
    pooled = mm(pool, stem[pl.ds(pl.multiple_of(mo * 256, 256), 256), :])
    g = 8 * lane + me
    v_slot = lane
    a_slot = jnp.zeros((1, 128), I32)
    for s in range(TM):
        v_slot = v_slot + jnp.where(ends[s] <= g, 8, 0)
        j = 8 * (lane % 8) + ((me - ends[s]) & 7)
        a_slot = jnp.where((lane - 32) // 8 == s, ((ends[s] + j) >> 3) + 8 * s, a_slot)
    slot = jnp.where(lane < 32, v_slot, jnp.where(lane < 96, a_slot, -1))
    place = onehot(slot == iota((96, 128), 0))

    for h in range(CHUNKS):
        total = own[h, 128:256] + a_r[h, 128:256].astype(F32)
        b_copies[h].wait_recv()
        total = total + b_r[h].astype(F32)
        c_s[h] = total.astype(BF16).reshape(TM, 16, WIDE)
        c_copies.append(to_tm(lambda p: c_s.at[h, p], c_r.at[h, me], TOT + 7 * h))
        c_r[h, me] = c_s[h, me]

    arrive(v_copies)
    visual = v_r[0].astype(F32)
    for t in range(1, TM):
        visual = visual + v_r[t].astype(F32)

    halves = []
    for h in range(CHUNKS):
        arrive(c_copies[h])
        part = pooled[:, WIDE * h : WIDE * h + WIDE]
        for t in range(TM):
            part = part + c_r[h, t].astype(F32)
        halves.append(part)
    pooled = jnp.concatenate(halves, axis=1)
    v = pooled - jnp.sum(pooled, axis=1, keepdims=True) * (1.0 / 1280.0)
    var = jnp.sum(v * v, axis=1, keepdims=True) * (1.0 / 1280.0)
    nrm[mo] = (v * lax.rsqrt(var + 1e-05) * gain2[...][None, :]).astype(BF16)
    n_copies = [copy(nrm.at[mo], nrm.at[mo], NRM + d, {"mod": p}) for d, p in enumerate(mod_peers)]
    loads[3].wait()
    arrive(n_copies)
    audio = mm_nt(nrm[...].reshape(64, 1280), aud_w[...])
    tokens = jnp.concatenate(
        [visual.astype(BF16), audio.astype(BF16), jnp.zeros((32, 448), BF16)], axis=0
    )
    out[...] = mm(place, tokens).astype(BF16)

    for c in sent:
        c.wait_send()
    both_ways(me, lambda i: [c[i].wait_send() for c in fb_out] and None)


def on_device_fused(
    filterbank, conv_weight, mlp_gain, up_weight, down_weight, post_gain, audio_weight,
    patches, vision_gain, vision_weight, retention, kept_count,
):
    vm = pl.BlockSpec(memory_space=pltpu.VMEM)
    far = pl.BlockSpec(memory_space=pl.ANY)
    n_out = vision_weight.shape[1]
    scratch = [
        pltpu.VMEM(conv_weight.shape, BF16),
        pltpu.VMEM((n_out, 1280), BF16),
        pltpu.VMEM((64, 1280), BF16),
        pltpu.VMEM((n_out, HALF), BF16),
        pltpu.VMEM((1056, 128), BF16),
        pltpu.VMEM((TM, 8, 128), F32),
        pltpu.VMEM((TM, 400, 128), BF16),
        pltpu.VMEM((TM, 400, 128), BF16),
        pltpu.VMEM((TM, 16, HALF), BF16),
        pltpu.VMEM((TM, MOD, 16, HALF), BF16),
        pltpu.VMEM((TM, 32, n_out), BF16),
        pltpu.VMEM((TM, 32, n_out), BF16),
        pltpu.VMEM((128, 1280), F32),
        pltpu.VMEM((1280, 256), BF16),
        pltpu.VMEM((1024, 1280), BF16),
        pltpu.VMEM((1024, 1280), BF16),
        pltpu.VMEM((MOD, 128, 256), BF16),
        pltpu.VMEM((CHUNKS, 256, WIDE), F32),
        pltpu.VMEM((CHUNKS, 256, WIDE), BF16),
        pltpu.VMEM((CHUNKS, 256, WIDE), BF16),
        pltpu.VMEM((CHUNKS, 128, WIDE), BF16),
        pltpu.VMEM((CHUNKS, 128, WIDE), BF16),
        pltpu.VMEM((CHUNKS, TM, 16, WIDE), BF16),
        pltpu.VMEM((CHUNKS, TM, 16, WIDE), BF16),
        pltpu.VMEM((MOD, 16, 1280), BF16),
        pltpu.SemaphoreType.DMA((4,)),
        pltpu.SemaphoreType.DMA((N_SEM,)),
        pltpu.SemaphoreType.DMA((N_SEM,)),
    ]
    sequence = pl.pallas_call(
        fused_kernel,
        out_shape=jax.ShapeDtypeStruct((SEQ_DEV, vision_weight.shape[1]), BF16),
        in_specs=[vm, far, vm, vm, vm, vm, far, far, vm, far, vm, pl.BlockSpec(memory_space=pltpu.SMEM)],
        out_specs=vm,
        scratch_shapes=scratch,
        compiler_params=pltpu.CompilerParams(
            collective_id=0, has_side_effects=True, vmem_limit_bytes=56 * 1024 * 1024
        ),
    )(
        filterbank, conv_weight, mlp_gain, up_weight, down_weight.T, post_gain,
        audio_weight.T, patches, vision_gain, vision_weight.T, retention, kept_count,
    )
    return sequence[None]


def solution(mesh):
    fused = mesh.shape["tm"] == TM and mesh.shape["mod"] == MOD
    return jax.shard_map(
        on_device_fused if fused else on_device,
        mesh=mesh,
        in_specs=(
            P("tm", None),
            P(),
            P(),
            P("tm", "mod"),
            P("mod", "tm"),
            P(),
            P(None, "mod"),
            P("tm", None),
            P(),
            P("tm", "mod"),
            P("tm", None),
            P("tm"),
        ),
        out_specs=P("tm", None, "mod"),
        check_vma=False,
    )
```

```python
import jax
import jax.numpy as jnp
from jax import lax
from jax.experimental import pallas as pl
from jax.experimental.pallas import tpu as pltpu
from jax.sharding import PartitionSpec as P

MRG_FRAME = 64
AUD_TOK = 64
SEQ_DEV = 96


def carried_in(value, axis, join, neutral):
    count, mine = (lax.axis_size(axis), lax.axis_index(axis))
    pieces = lax.all_gather(value, axis)
    running = jnp.full_like(value, 0) + jnp.asarray(neutral, value.dtype)

    def hop(position, running):
        longer = join(running, pieces[position])
        return jnp.where(position < mine, longer, running)

    return lax.fori_loop(0, count - 1, hop, running)


def padded(shard, sides, width):
    for axis, dim in sides:
        peers, length = (lax.axis_size(axis), shard.shape[dim])
        up = [(i, (i + 1) % peers) for i in range(peers - 1)]
        down = [(j, i) for i, j in up]
        last = lax.slice_in_dim(shard, length - width, length, axis=dim)
        first = lax.slice_in_dim(shard, 0, width, axis=dim)
        before = lax.ppermute(last, axis, up)
        after = lax.ppermute(first, axis, down)
        shard = jnp.concatenate([before, shard, after], axis=dim)
    return shard


def layer_norm(values, scale_gain):
    average = jnp.mean(values, axis=-1, keepdims=True)
    centred = values - average
    variance = jnp.mean(centred * centred, axis=-1, keepdims=True)
    return centred * lax.rsqrt(variance + 1e-05) * scale_gain


def rms_norm(values, scale_gain):
    square_mean = jnp.mean(values * values, axis=-1, keepdims=True)
    return values * lax.rsqrt(square_mean + 1e-06) * scale_gain


def pool_pairs(values):
    return values.reshape(-1, 2, values.shape[-1]).mean(axis=1)


def add_counts(earlier, later):
    return earlier + later


def on_device(
    filterbank,
    conv_weight,
    mlp_gain,
    up_weight,
    down_weight,
    post_gain,
    audio_weight,
    patches,
    vision_gain,
    vision_weight,
    retention,
    kept_count,
):
    placed = kept_count + AUD_TOK
    starts = carried_in(placed, "tm", add_counts, jnp.zeros((1,), jnp.int32))
    framed = padded(filterbank, (("tm", 0),), 1)
    unfolded = jnp.concatenate([framed[:-2], framed[1:-1], framed[2:]], axis=1)
    stem = jax.nn.gelu(
        jnp.dot(unfolded, conv_weight, preferred_element_type=jnp.float32), approximate=False
    ).astype(jnp.bfloat16)
    residual = stem.astype(jnp.float32)
    hidden = layer_norm(residual, mlp_gain).astype(jnp.bfloat16)
    up_share = lax.all_gather(up_weight, "tm", axis=0, tiled=True)
    pre_act = jnp.dot(hidden, up_share, preferred_element_type=jnp.float32)
    activated = jax.nn.gelu(pre_act, approximate=False).astype(jnp.bfloat16)
    down_share = lax.all_gather(down_weight, "tm", axis=1, tiled=True)
    partial_value = jnp.dot(activated, down_share, preferred_element_type=jnp.float32)
    pooled_share = lax.psum_scatter(
        pool_pairs(partial_value).astype(jnp.bfloat16), "mod", scatter_dimension=0, tiled=True
    ).astype(jnp.float32)
    share_rows = pooled_share.shape[0]
    own_rows = lax.dynamic_slice_in_dim(
        pool_pairs(residual), lax.axis_index("mod") * share_rows, share_rows, 0
    )
    share_normed = layer_norm(own_rows + pooled_share, post_gain).astype(jnp.bfloat16)
    normed = lax.all_gather(share_normed, "mod", axis=0, tiled=True)
    audio_tokens = jnp.dot(normed, audio_weight, preferred_element_type=jnp.float32).astype(
        jnp.bfloat16
    )
    patch_normed = rms_norm(patches.astype(jnp.float32), vision_gain).astype(jnp.bfloat16)
    merged = patch_normed.reshape(-1, 4 * patch_normed.shape[1])
    vision_share = lax.all_gather(vision_weight, "tm", axis=0, tiled=True)
    visual_tokens = jnp.dot(merged, vision_share, preferred_element_type=jnp.float32).astype(
        jnp.bfloat16
    )
    peer_count = lax.axis_size("tm")
    per_peer = (AUD_TOK + MRG_FRAME + peer_count - 1) // peer_count
    kept_here = kept_count[0]
    first_slot = starts[0]
    all_tokens = jnp.concatenate([visual_tokens, audio_tokens], axis=0)
    peer_ids = jnp.arange(peer_count, dtype=jnp.int32)[:, None]
    round_ids = jnp.arange(per_peer, dtype=jnp.int32)[None, :]
    local_index = round_ids * peer_count + (peer_ids - first_slot) % peer_count
    valid_rows = local_index < kept_here + AUD_TOK
    kept_index = jnp.take(retention[0], jnp.minimum(local_index, MRG_FRAME - 1), axis=0)
    source_index = jnp.where(
        local_index < kept_here, kept_index, MRG_FRAME + local_index - kept_here
    )
    source_index = jnp.where(valid_rows, source_index, 0).astype(jnp.int32)
    send_rows = jnp.take(all_tokens, source_index.reshape(-1), axis=0).reshape(
        peer_count, per_peer, all_tokens.shape[1]
    )
    send_slots = jnp.where(valid_rows, (first_slot + local_index) // peer_count, SEQ_DEV).astype(
        jnp.int32
    )
    recv_rows, recv_slots = (
        lax.all_to_all(send_rows, "tm", split_axis=0, concat_axis=0, tiled=True),
        lax.all_to_all(send_slots, "tm", split_axis=0, concat_axis=0, tiled=True),
    )
    sequence = jnp.zeros((SEQ_DEV, all_tokens.shape[1]), jnp.bfloat16)
    sequence = sequence.at[recv_slots.reshape(-1)].set(
        recv_rows.reshape(-1, all_tokens.shape[1]), mode="drop"
    )
    return sequence[None]


F32, BF16, I32 = jnp.float32, jnp.bfloat16, jnp.int32
MESH = pl.DeviceIdType.MESH
TM, MOD = 8, 4


def iota(shape, dim):
    return lax.broadcasted_iota(I32, shape, dim)


def onehot(mask, value=1.0):
    return jnp.where(mask, value, 0.0).astype(BF16)


def mm(a, b):
    return lax.dot_general(a, b, (((1,), (0,)), ((), ())), preferred_element_type=F32)


def mm_nt(a, b):
    return lax.dot_general(a, b, (((1,), (1,)), ((), ())), preferred_element_type=F32)


def mm_tn(a, b):
    return lax.dot_general(a, b, (((0,), (0,)), ((), ())), preferred_element_type=F32)


def gelu(x):
    return 0.5 * x * (1.0 + lax.erf(x * 0.7071067811865476))


FB, META, UPW, DNW, MRG, VIS, TOT, FWD, NRM, HID, COR, XAX = 0, 7, 14, 21, 28, 35, 42, 77, 80, 83, 87, 92
N_SEM = 97
CHUNKS, WIDE = 5, 256
HALF = 640
SHIFTS = (4, 3, 5, 2, 6, 1, 7)


def flipped(index, bits):
    for bit in (1, 2, 4):
        if bits % (2 * bit) >= bit:
            index = index + bit - 2 * bit * ((index // bit) % 2)
    return index


def fused_kernel(
    fb, conv_h, gain1, up, dn, gain2, aud_h, pat_h, gain_v, vis_h, ret, kept, out,
    conv, aud_w, pat, vis_w, fbp, meta, w_s, w_r, m_s, x_r, v_s, v_r, pre, w_all, stem, hid, pa, own,
    a_s, a_r, b_s, b_r, c_s, c_r, nrm, load_sem, send_sem, recv_sem,
):
    me = lax.axis_index("tm")
    mo = lax.axis_index("mod")
    xx, cc = mo // 2, mo % 2
    tm_peers = [lax.rem(me + d, TM) for d in SHIFTS]
    tm_sources = [lax.rem(me + TM - d, TM) for d in SHIFTS]
    mod_peers = [flipped(mo, bits) for bits in (2, 3, 1)]
    x_peer, core_peer = mod_peers[0], mod_peers[2]

    barrier = pltpu.get_barrier_semaphore()
    for peer in tm_peers:
        pl.semaphore_signal(barrier, inc=1, device_id={"tm": peer}, device_id_type=MESH)
    for peer in mod_peers:
        pl.semaphore_signal(barrier, inc=1, device_id={"mod": peer}, device_id_type=MESH)

    quarter = pl.ds(pl.multiple_of(mo * 64, 64), 64)
    loads = [
        pltpu.make_async_copy(src, dst, load_sem.at[i])
        for i, (src, dst) in enumerate(
            [(pat_h.at[quarter], pat), (conv_h, conv), (vis_h, vis_w), (aud_h, aud_w)]
        )
    ]
    for c in loads:
        c.start()

    sent = []

    def describe(src, dst, slot, to):
        return pltpu.make_async_remote_copy(
            src_ref=src, dst_ref=dst, send_sem=send_sem.at[slot], recv_sem=recv_sem.at[slot],
            device_id=to, device_id_type=MESH,
        )

    def copy(src, dst, slot, to):
        c = describe(src, dst, slot, to)
        c.start()
        sent.append(c)
        return c

    def to_tm(src_of, dst, base):
        return [copy(src_of(p), dst, base + d, {"tm": p}) for d, p in enumerate(tm_peers)]

    def arrive(copies):
        for c in copies:
            c.wait_recv()

    fbp[0:16] = jnp.zeros((16, 128), BF16)
    fbp[1040:1056] = jnp.zeros((16, 128), BF16)
    my_rows = pl.ds(pl.multiple_of(16 + me * 128, 16), 128)
    fbp[my_rows, :] = fb[...]
    hit = onehot(ret[...] == iota((128, 64), 0) % 64)
    inv = mm_nt(iota((8, 64), 1).astype(F32).astype(BF16), hit)
    kept_f = jnp.full((8, 128), kept[0], I32).astype(F32)
    inv = jnp.where(inv < kept_f, inv, -4096.0)
    meta[me] = jnp.where(iota((8, 128), 0) == 0, inv, kept_f)

    row, col = iota((512, 128), 0), iota((512, 128), 1)
    for t in range(TM):
        w_s[t, 0:160] = up[:, 128 * t : 128 * t + 128]
        w_s[t, 240:400] = dn[:, 128 * t : 128 * t + 128]
    picks = [onehot((row // 128 == col // 32) & (row % 128 == 32 * a + col % 32)) for a in range(4)]
    for g in range(2):
        lanes = slice(1024 + 128 * g, 1152 + 128 * g)
        rest = jnp.concatenate(
            [up[0:80, lanes], up[80:160, lanes], dn[0:80, lanes], dn[80:160, lanes]], axis=1
        )
        for a in range(4):
            w_s[4 * g + a, 160:240] = mm(rest, picks[a]).astype(BF16)
    w_r[me] = w_s[me]

    def frames(d, p, source):
        first = 112 * (source % 2)
        edge = pl.ds(pl.multiple_of(first, 16), 16)
        there = pl.ds(pl.multiple_of(16 + source * 128 + first, 16), 16)
        whole = pl.ds(pl.multiple_of(16 + source * 128, 16), 128)
        return [
            pltpu.make_async_remote_copy(
                src_ref=src, dst_ref=dst, send_sem=send_sem.at[FB + d], recv_sem=recv_sem.at[FB + d],
                device_id={"tm": p}, device_id_type=MESH,
            )
            for src, dst in ((fb, fbp.at[whole]), (fb.at[edge], fbp.at[there]))
        ]

    def both_ways(source, act):
        here = (source // 2) % 2 == cc
        pl.when(here)(lambda: act(0))
        pl.when(jnp.logical_not(here))(lambda: act(1))

    fb_out = [frames(d, p, me) for d, p in enumerate(tm_peers)]
    fb_in = [frames(d, p, p) for d, p in enumerate(tm_sources)]
    pl.semaphore_wait(barrier, TM + MOD - 2)
    both_ways(me, lambda i: [c[i].start() for c in fb_out] and None)
    up_rows, dn_rows = pl.ds(0, 240), pl.ds(240, 160)
    u_copies = to_tm(lambda p: w_s.at[p, up_rows], w_r.at[me, up_rows], UPW)
    meta_copies = to_tm(lambda p: meta.at[me], meta.at[me], META)

    loads[0].wait()
    pv = pat[...].astype(F32)
    ms = jnp.sum(pv * pv, axis=1, keepdims=True) * (1.0 / 1280.0)
    pn = (pv * lax.rsqrt(ms + 1e-06) * gain_v[...][None, :]).astype(BF16)
    r64, c64 = iota((64, 64), 0), iota((64, 64), 1)
    pn = mm(onehot(c64 == 4 * (r64 % 16) + r64 // 16), pn).astype(BF16)
    for t in range(TM):
        q, h = t // 2, t % 2
        m_s[t] = pn[16 * q : 16 * q + 16, HALF * h : HALF * h + HALF]
    m_copies = to_tm(lambda p: m_s.at[p], x_r.at[me, mo], MRG)
    x_r[me, mo] = m_s[me]
    d_copies = to_tm(lambda p: w_s.at[p, dn_rows], w_r.at[me, dn_rows], DNW)

    loads[1].wait()
    for d, p in enumerate(tm_sources):
        both_ways(p, lambda i: fb_in[d][i].wait_recv())

    def span_of(k):
        x_at = (1 - xx) + (k // 2) * (2 * xx - 1)
        return 2 * (2 * x_at + cc) + k % 2

    def hidden_rows(k):
        rows = pl.ds(pl.multiple_of(span_of(k) * 128, 128), 128)
        return describe(hid.at[rows], hid.at[rows], HID + k, {"mod": core_peer})

    x_copies = [
        describe(x_r.at[:, mo], x_r.at[:, mo], FWD + d, {"mod": p})
        for d, p in enumerate((x_peer, core_peer))
    ]

    def stem_step(k, carry):
        base = pl.multiple_of(span_of(k) * 128, 128)
        rows = fbp[pl.ds(base, 160), :].astype(F32)
        taps = jnp.concatenate([rows[15:143], rows[16:144], rows[17:145]], axis=1).astype(BF16)
        pre[...] = mm(taps, conv[...])

        def piece(i, carry):
            at = pl.multiple_of(i * 32, 32)
            st = gelu(pre[pl.ds(at, 32), :]).astype(BF16)
            there = pl.ds(pl.multiple_of(base + at, 32), 32)
            stem[there, :] = st
            v = st.astype(F32)
            v = v - jnp.sum(v, axis=1, keepdims=True) * (1.0 / 1280.0)
            var = jnp.sum(v * v, axis=1, keepdims=True) * (1.0 / 1280.0)
            hid[there, :] = (v * lax.rsqrt(var + 1e-05) * gain1[...][None, :]).astype(BF16)
            return carry

        lax.fori_loop(0, 4, piece, 0)
        hidden_rows(k).start()

        @pl.when(k == 1)
        def _():
            arrive(m_copies)
            for c in x_copies:
                c.start()

        return carry

    lax.fori_loop(0, 4, stem_step, 0)
    h_copies = [hidden_rows(k) for k in range(4)]
    sent.extend(h_copies + x_copies)
    x_copies[0].wait_recv()
    x_copies.append(copy(x_r.at[:, x_peer], x_r.at[:, x_peer], FWD + 2, {"mod": core_peer}))

    arrive(meta_copies)
    ends, before, running = [], [], jnp.zeros((1, 128), F32)
    for s in range(TM):
        before.append(running)
        running = running + meta[s, 1:2, :]
        ends.append(running.astype(I32))

    def ends_of(pair):
        picked = []
        for h in range(2):
            e = ends[h]
            for p in range(1, MOD):
                e = jnp.where(pair == p, ends[2 * p + h], e)
            picked.append(e)
        return picked

    def pool_rows(holder, r_s2, r_q, frames, span_ends):
        blocks = []
        for h in range(2):
            j = 8 * r_q + ((holder - span_ends[h]) & 7)
            blocks.append(onehot((r_s2 == h) & (frames // 2 == j), 0.5))
        return jnp.concatenate(blocks, axis=1)

    arrive(u_copies)
    rem = jnp.concatenate([w_r[t, 160:240] for t in range(TM)], axis=0)
    ri, ci = iota((128, 512), 0), iota((128, 512), 1)
    rem = mm(rem, onehot((ci % 128 < 32) & (ri == 32 * (ci // 128) + ci % 128))).astype(BF16)

    def assemble(first, lane):
        main = jnp.concatenate([w_r[t, first : first + 160] for t in range(TM)], axis=0)
        parts = []
        for t in range(TM):
            parts.append(rem[80 * t : 80 * t + 80, lane : lane + 128])
            parts.append(rem[80 * t : 80 * t + 80, lane + 128 : lane + 256])
        return jnp.concatenate([main, jnp.concatenate(parts, axis=0)], axis=1)

    w_all[...] = assemble(0, 0)
    r128, c128 = iota((128, 128), 0), iota((128, 128), 1)

    def feed(step, carry):
        k = lax.rem(2 + 2 * step + step // 2, 4)
        core = (1 - cc) + (k // 2) * (2 * cc - 1)
        x_at = (1 - xx) + (k % 2) * (2 * xx - 1)
        pl.when(step == 1)(lambda: arrive(h_copies[0:2]))
        pl.when(step == 3)(lambda: arrive(h_copies[2:4]))
        pair = 2 * x_at + core
        rows = pl.ds(pl.multiple_of(pair * 256, 256), 256)
        act = gelu(mm(hid[rows, :], w_all[...])).astype(BF16)
        pool = pool_rows(r128 // 16, (r128 // 8) % 2, r128 % 8, c128, ends_of(pair))
        pa[k] = mm(pool, act).astype(BF16)
        return carry

    lax.fori_loop(0, 4, feed, 0)

    arrive(x_copies[1:])
    lane = iota((1, 128), 1)
    pos = jnp.concatenate(
        [
            jnp.where(lane < 64, meta[t, 0:1, :] + before[t], meta[t + 1, 0:1, :] + before[t + 1])
            for t in range(0, TM, 2)
        ],
        axis=1,
    ).astype(I32)
    r256 = iota((256, 512), 0)
    pick = onehot(pos == 8 * (r256 % 32) + r256 // 32)
    chosen = mm(pick, x_r[...].reshape(512, HALF)).astype(BF16)
    loads[2].wait()
    v_s[...] = mm_nt(chosen, vis_w[...]).astype(BF16).reshape(TM, 32, 448)
    v_copies = to_tm(lambda p: v_s.at[p], v_r.at[me], VIS)
    v_r[me] = v_s[me]

    arrive(d_copies)
    w_all[...] = assemble(240, 256)

    def core_sum(h):
        return describe(a_s.at[h], a_r.at[h], COR + h, {"mod": core_peer})

    def x_sum(h):
        return describe(b_s.at[h], b_r.at[h], XAX + h, {"mod": x_peer})

    def product_half(h, carry):
        cols = pl.ds(pl.multiple_of(h * WIDE, WIDE), WIDE)
        product = mm_nt(pa[...].reshape(512, 256), w_all[cols, :])
        a_s[h] = product[0:256].astype(BF16)
        core_sum(h).start()
        own[h] = product[256:512]
        return carry

    def x_half(h, carry):
        core_sum(h).wait_recv()
        b_s[h] = (own[h, 0:128] + a_r[h, 0:128].astype(F32)).astype(BF16)
        x_sum(h).start()
        return carry

    def both(h, carry):
        product_half(h, carry)
        return x_half(h - 1, carry)

    product_half(0, 0)
    lax.fori_loop(1, CHUNKS, both, 0)
    x_half(CHUNKS - 1, 0)
    b_copies = [x_sum(h) for h in range(CHUNKS)]
    sent.extend([core_sum(h) for h in range(CHUNKS)] + b_copies)
    c_copies = []

    r16, c16 = iota((16, 128), 0), iota((16, 128), 1)
    pool = pool_rows(me, r16 // 8, r16 % 8, c16, ends_of(mo))
    pooled = mm(pool, stem[pl.ds(pl.multiple_of(mo * 256, 256), 256), :])
    g = 8 * lane + me
    v_slot = lane
    a_slot = jnp.zeros((1, 128), I32)
    for s in range(TM):
        v_slot = v_slot + jnp.where(ends[s] <= g, 8, 0)
        j = 8 * (lane % 8) + ((me - ends[s]) & 7)
        a_slot = jnp.where((lane - 32) // 8 == s, ((ends[s] + j) >> 3) + 8 * s, a_slot)
    slot = jnp.where(lane < 32, v_slot, jnp.where(lane < 96, a_slot, -1))
    place = onehot(slot == iota((96, 128), 0))

    for h in range(CHUNKS):
        total = own[h, 128:256] + a_r[h, 128:256].astype(F32)
        b_copies[h].wait_recv()
        total = total + b_r[h].astype(F32)
        c_s[h] = total.astype(BF16).reshape(TM, 16, WIDE)
        c_copies.append(to_tm(lambda p: c_s.at[h, p], c_r.at[h, me], TOT + 7 * h))
        c_r[h, me] = c_s[h, me]

    arrive(v_copies)
    visual = v_r[0].astype(F32)
    for t in range(1, TM):
        visual = visual + v_r[t].astype(F32)

    halves = []
    for h in range(CHUNKS):
        arrive(c_copies[h])
        part = pooled[:, WIDE * h : WIDE * h + WIDE]
        for t in range(TM):
            part = part + c_r[h, t].astype(F32)
        halves.append(part)
    pooled = jnp.concatenate(halves, axis=1)
    v = pooled - jnp.sum(pooled, axis=1, keepdims=True) * (1.0 / 1280.0)
    var = jnp.sum(v * v, axis=1, keepdims=True) * (1.0 / 1280.0)
    nrm[mo] = (v * lax.rsqrt(var + 1e-05) * gain2[...][None, :]).astype(BF16)
    n_copies = [copy(nrm.at[mo], nrm.at[mo], NRM + d, {"mod": p}) for d, p in enumerate(mod_peers)]
    loads[3].wait()
    arrive(n_copies)
    audio = mm_nt(nrm[...].reshape(64, 1280), aud_w[...])
    tokens = jnp.concatenate(
        [visual.astype(BF16), audio.astype(BF16), jnp.zeros((32, 448), BF16)], axis=0
    )
    out[...] = mm(place, tokens).astype(BF16)

    for c in sent:
        c.wait_send()
    both_ways(me, lambda i: [c[i].wait_send() for c in fb_out] and None)


def on_device_fused(
    filterbank, conv_weight, mlp_gain, up_weight, down_weight, post_gain, audio_weight,
    patches, vision_gain, vision_weight, retention, kept_count,
):
    vm = pl.BlockSpec(memory_space=pltpu.VMEM)
    far = pl.BlockSpec(memory_space=pl.ANY)
    n_out = vision_weight.shape[1]
    scratch = [
        pltpu.VMEM(conv_weight.shape, BF16),
        pltpu.VMEM((n_out, 1280), BF16),
        pltpu.VMEM((64, 1280), BF16),
        pltpu.VMEM((n_out, HALF), BF16),
        pltpu.VMEM((1056, 128), BF16),
        pltpu.VMEM((TM, 8, 128), F32),
        pltpu.VMEM((TM, 400, 128), BF16),
        pltpu.VMEM((TM, 400, 128), BF16),
        pltpu.VMEM((TM, 16, HALF), BF16),
        pltpu.VMEM((TM, MOD, 16, HALF), BF16),
        pltpu.VMEM((TM, 32, n_out), BF16),
        pltpu.VMEM((TM, 32, n_out), BF16),
        pltpu.VMEM((128, 1280), F32),
        pltpu.VMEM((1280, 256), BF16),
        pltpu.VMEM((1024, 1280), BF16),
        pltpu.VMEM((1024, 1280), BF16),
        pltpu.VMEM((MOD, 128, 256), BF16),
        pltpu.VMEM((CHUNKS, 256, WIDE), F32),
        pltpu.VMEM((CHUNKS, 256, WIDE), BF16),
        pltpu.VMEM((CHUNKS, 256, WIDE), BF16),
        pltpu.VMEM((CHUNKS, 128, WIDE), BF16),
        pltpu.VMEM((CHUNKS, 128, WIDE), BF16),
        pltpu.VMEM((CHUNKS, TM, 16, WIDE), BF16),
        pltpu.VMEM((CHUNKS, TM, 16, WIDE), BF16),
        pltpu.VMEM((MOD, 16, 1280), BF16),
        pltpu.SemaphoreType.DMA((4,)),
        pltpu.SemaphoreType.DMA((N_SEM,)),
        pltpu.SemaphoreType.DMA((N_SEM,)),
    ]
    sequence = pl.pallas_call(
        fused_kernel,
        out_shape=jax.ShapeDtypeStruct((SEQ_DEV, vision_weight.shape[1]), BF16),
        in_specs=[vm, far, vm, vm, vm, vm, far, far, vm, far, vm, pl.BlockSpec(memory_space=pltpu.SMEM)],
        out_specs=vm,
        scratch_shapes=scratch,
        compiler_params=pltpu.CompilerParams(
            collective_id=0, has_side_effects=True, vmem_limit_bytes=56 * 1024 * 1024
        ),
    )(
        filterbank, conv_weight, mlp_gain, up_weight, down_weight.T, post_gain,
        audio_weight.T, patches, vision_gain, vision_weight.T, retention, kept_count,
    )
    return sequence[None]


def solution(mesh):
    fused = mesh.shape["tm"] == TM and mesh.shape["mod"] == MOD
    return jax.shard_map(
        on_device_fused if fused else on_device,
        mesh=mesh,
        in_specs=(
            P("tm", None),
            P(),
            P(),
            P("tm", "mod"),
            P("mod", "tm"),
            P(),
            P(None, "mod"),
            P("tm", None),
            P(),
            P("tm", "mod"),
            P("tm", None),
            P("tm"),
        ),
        out_specs=P("tm", None, "mod"),
        check_vma=False,
    )
```
